32 devices in a mesh: dp: 8 (over y, x, core), tensor: 4 (over z).
Axes of the slice: x: 2, y: 2, z: 4, core: 2. Of those that a mesh axis runs over, the one named last changes fastest.
Arguments:
- block_input: bfloat16 [48, 200, 512], P('dp', 'tensor'), may hold values from -6 to 6
- gains: bfloat16 [512, 2], P('dp'), may hold values from 0.5 to 1.5
- w_qkv: bfloat16 [512, 3, 512], P('dp', None, 'tensor'), may hold values from -0.25 to 0.25
- w_o: bfloat16 [512, 512], P('tensor', 'dp'), may hold values from -1.5 to 1.5
- w_router: bfloat16 [512, 16], P('dp'), may hold values from -0.1875 to 0.1875
- w_in: bfloat16 [512, 16, 2048], P('dp', None, 'tensor'), may hold values from -0.25 to 0.25
- w_out: bfloat16 [2048, 16, 512], P('tensor', None, 'dp'), may hold values from -1 to 1
- pictures_alive_per_shard: int32 [8], P('dp'), may hold values from 5 to 6, as said below
- expert_ids: int32 [48, 200, 2], P('dp'), may hold values from 0 to 15, as said below
- slot_index: int32 [48, 200, 2], P('dp'), may hold values from -1 to 191, as said below
- cotangent: bfloat16 [48, 200, 512], P('dp', 'tensor'), may hold values from -6 to 6
Outputs:
- output: bfloat16 [48, 200, 512], P('dp', 'tensor')
- grad_x: float32 [48, 200, 512], P('dp', 'tensor')
- grad_gains: float32 [512, 2], P('dp')
- grad_qkv: float32 [512, 3, 512], P('dp', None, 'tensor')
- grad_o: float32 [512, 512], P('tensor', 'dp')
- grad_router: float32 [512, 16], P('dp')
- grad_in: float32 [512, 16, 2048], P('dp', None, 'tensor')
- grad_out: float32 [2048, 16, 512], P('tensor', None, 'dp')
The draws below stay inside these ranges and needn't reach their ends.
Inputs may be any that keep to these rules, and one draw needn't show every extreme that they name: `pictures_alive_per_shard`: each index of dp has 5 or 6 live images; both counts occur in every draw. `expert_ids`: the two experts of a token differ. `slot_index`: within one group, slots are given to live tokens' choices in order, all first choices of the group in token order and then all second choices; a choice gets -1 when its token isn't live or its expert already has 192 entries. Distinct choices of a group never share an (expert, slot) pair.
All inputs are finite; a program needn't handle non-finite values.
Results may differ from the reference program's by a relative error of at most 0.014.
Values may be sent and summed in bfloat16 or wider, within the bound.
A program may use at most 192 MiB of HBM per device.

```python
import math
from functools import partial
import jax
import jax.numpy as jnp
from jax import lax

D = 512
HEADS = 8
HEAD_DIM = 64
FF = 2048
SPECIALIST_TOTAL = 16
TOK_IMG = 197
LEN = 200
IMG_DEV = 6
IMAGES = 48
CAP = 192
N_DP = 8
N_TENSOR = 4


def counts_core(key):
    key = jax.random.fold_in(key, 101)
    key_base, key_first, key_second = jax.random.split(key, 3)
    base = jax.random.randint(key_base, (N_DP,), IMG_DEV - 1, IMG_DEV + 1)
    first = jax.random.randint(key_first, (), 0, N_DP)
    second = (first + 1 + jax.random.randint(key_second, (), 0, N_DP - 1)) % N_DP
    return base.at[first].set(IMG_DEV).at[second].set(IMG_DEV - 1).astype(jnp.int32)


def experts_core(key):
    key = jax.random.fold_in(key, 202)
    extra_logit_seed, jitter_logit_seed = jax.random.split(key, 2)
    dispatch_logit_offset = jax.random.randint(extra_logit_seed, (N_DP, 1, SPECIALIST_TOTAL), 0, SPECIALIST_TOTAL) * (32768 // SPECIALIST_TOTAL)
    gating_jitter = jax.random.randint(jitter_logit_seed, (N_DP, IMG_DEV * LEN, SPECIALIST_TOTAL), 0, 65536)
    gating_logits_matrix = (gating_jitter + dispatch_logit_offset) * SPECIALIST_TOTAL + jnp.arange(SPECIALIST_TOTAL, dtype=jnp.int32)[None, None, :]
    return lax.top_k(gating_logits_matrix, 2)[1].astype(jnp.int32)


def draw_pictures_alive_per_shard(key, part):
    return counts_core(key)


def draw_expert_ids(key, part):
    return experts_core(key).reshape(N_DP * IMG_DEV, LEN, 2)


def draw_slot_index(key, part):
    counts = counts_core(key)
    chosen = experts_core(key)
    group_rows = IMG_DEV * LEN
    row_ids = jnp.arange(group_rows, dtype=jnp.int32)
    image_of = row_ids // LEN
    place_of = row_ids % LEN
    live = (image_of[None, :] < counts[:, None]) & (place_of < TOK_IMG)[None, :]
    order = jnp.concatenate([chosen[:, :, 0], chosen[:, :, 1]], 1)
    live_both = jnp.concatenate([live, live], 1)
    hot = ((order[:, :, None] == jnp.arange(SPECIALIST_TOTAL, dtype=jnp.int32)[None, None, :]) & live_both[:, :, None]).astype(jnp.int32)
    before = jnp.cumsum(hot, 1) - hot
    placed = jnp.sum(before * hot, -1)
    slots = jnp.where(live_both & (placed < CAP), placed, -1)
    stacked = jnp.stack([slots[:, :group_rows], slots[:, group_rows:]], -1)
    return stacked.reshape(N_DP * IMG_DEV, LEN, 2).astype(jnp.int32)


def level_of(stream_key, extent, cuts, smallest, high):
    level = 1.0
    for axis_at, blocks in cuts:
        heights = jax.random.uniform(jax.random.fold_in(jax.random.fold_in(stream_key, 6), axis_at), (blocks,), jnp.float32, smallest / len(cuts), high / len(cuts))
        level = level * jnp.repeat(jnp.exp(heights), extent[axis_at] // blocks).reshape((-1,) + (1,) * (len(extent) - 1 - axis_at))
    return level


def gaussian(rng, dims, scale, reach, pieces=(), kind=jnp.bfloat16):
    array = jax.random.normal(rng, dims, jnp.float32) * scale
    if len(pieces) > 0:
        array = level_of(rng, dims, pieces, -0.22, 0.18) * array
    return jnp.clip(array, min=-reach, max=reach).astype(kind)


def setup_inputs(seed: int = 0) -> dict:
    key_list = jax.random.split(jax.random.key(seed), 12)
    block_input = gaussian(key_list[0], (IMAGES, LEN, D), 1.0, 6.0, ((0, 8), (1, 4)))
    gains = jnp.clip(1.0 + 0.1 * jax.random.normal(key_list[1], (D, 2), jnp.float32), 0.5, 1.5).astype(jnp.bfloat16)
    w_qkv = gaussian(key_list[2], (D, 3, D), D ** -0.5, 0.25, ((0, 8), (2, 4)))
    w_o = gaussian(key_list[3], (D, D), (D // 32) ** -0.5, 1.5, ((0, 4), (1, 8)))
    w_router = gaussian(key_list[4], (D, SPECIALIST_TOTAL), (D * 2) ** -0.5, 0.1875, ((0, 8),))
    w_in = gaussian(key_list[5], (D, SPECIALIST_TOTAL, FF), D ** -0.5, 0.25, ((0, 8), (2, 4)))
    w_out = gaussian(key_list[6], (FF, SPECIALIST_TOTAL, D), (FF // 64) ** -0.5, 1.0, ((0, 4), (2, 8)))
    pictures_alive_per_shard = draw_pictures_alive_per_shard(jax.random.fold_in(key_list[11], 71), 0)
    expert_ids = draw_expert_ids(jax.random.fold_in(key_list[11], 71), 0)
    slot_index = draw_slot_index(jax.random.fold_in(key_list[11], 71), 0)
    cotangent = gaussian(key_list[10], (IMAGES, LEN, D), 1.0, 6.0, ((0, 8), (1, 4)))
    return dict(block_input=block_input, gains=gains, w_qkv=w_qkv, w_o=w_o, w_router=w_router, w_in=w_in, w_out=w_out, pictures_alive_per_shard=pictures_alive_per_shard, expert_ids=expert_ids, slot_index=slot_index, cotangent=cotangent)


@jax.custom_vjp
def low(v):
    return lax.optimization_barrier(v.astype(jnp.bfloat16)).astype(jnp.float32)

@jax.custom_vjp
def low_back(v):
    return v

def low_keep(v):
    return (low(v), None)

def low_pass(kept, grad):
    return (grad,)

def back_keep(v):
    return (v, None)

def back_low(kept, grad):
    return (low(grad),)
low.defvjp(low_keep, low_pass)
low_back.defvjp(back_keep, back_low)
exact_prec = lax.Precision.HIGHEST
epsilon = 1e-06
negative_fill = -1e+30

def layer_norm(values, gain):
    centre = values - lax.optimization_barrier(jnp.mean(values, -1, keepdims=True))
    spread = lax.optimization_barrier(jnp.mean(centre * centre, -1, keepdims=True))
    return centre * lax.rsqrt(spread + epsilon) * gain

def group_block(weights, inputs):
    gains, w_qkv, w_o, w_router, w_in, w_out = weights
    x_group, count, ids_group, slots_group = inputs
    image_ids = jnp.arange(IMG_DEV)
    positions = jnp.arange(LEN)
    key_live = positions < TOK_IMG
    live = ((image_ids < count)[:, None] & key_live[None, :]).astype(x_group.dtype)
    normed = low(layer_norm(x_group, gains[:, 0]))
    project = low(low_back(jnp.einsum('ild,djc->iljc', normed, w_qkv, precision=exact_prec)))
    queries = project[:, :, 0].reshape(IMG_DEV, LEN, HEADS, HEAD_DIM)
    keys_all = project[:, :, 1].reshape(IMG_DEV, LEN, HEADS, HEAD_DIM)
    values_all = project[:, :, 2].reshape(IMG_DEV, LEN, HEADS, HEAD_DIM)
    scale_factor = 1.0 / math.sqrt(HEAD_DIM)
    gating_logits_matrix = low_back(jnp.einsum('ilhe,imhe->ihlm', queries, keys_all, precision=exact_prec) * scale_factor)
    masked = jnp.where(key_live[None, None, None, :], gating_logits_matrix, negative_fill)
    att_probs = low(jax.nn.softmax(masked, axis=-1))
    attended = low(low_back(jnp.einsum('ihlm,imhe->ilhe', att_probs, values_all, precision=exact_prec)))
    attended = attended.reshape(IMG_DEV, LEN, D)
    branch = low_back(jnp.einsum('ilc,cd->ild', attended, w_o, precision=exact_prec))
    middle = x_group + live[:, :, None] * branch
    normed_two = low(layer_norm(middle, gains[:, 1]))
    logits = low_back(jnp.einsum('ild,de->ile', normed_two, w_router, precision=exact_prec))
    router_probs = jax.nn.softmax(logits, axis=-1)
    gates = jnp.take_along_axis(router_probs, ids_group, axis=-1)
    total_rows = IMG_DEV * LEN
    flat_in = normed_two.reshape(total_rows, D)
    targets = jnp.where(slots_group >= 0, ids_group * CAP + slots_group, SPECIALIST_TOTAL * CAP).astype(jnp.int32)
    targets = targets.reshape(total_rows, 2)
    dispatched = jnp.zeros((SPECIALIST_TOTAL * CAP + 1, D), flat_in.dtype)
    dispatched = dispatched.at[targets[:, 0]].add(flat_in).at[targets[:, 1]].add(flat_in)
    dispatched = dispatched[:SPECIALIST_TOTAL * CAP].reshape(SPECIALIST_TOTAL, CAP, D)
    part_ff = FF // N_TENSOR
    expert_out = jnp.zeros((SPECIALIST_TOTAL, CAP, D), flat_in.dtype)
    for part_index in range(N_TENSOR):
        lower = part_index * part_ff
        hidden = low_back(jnp.einsum('ecd,def->ecf', low_back(dispatched), w_in[:, :, lower:lower + part_ff], precision=exact_prec))
        active = low(jax.nn.gelu(hidden, approximate=False))
        expert_out = expert_out + low(jnp.einsum('ecf,fed->ecd', active, w_out[lower:lower + part_ff], precision=exact_prec))
    padded = jnp.concatenate([expert_out.reshape(SPECIALIST_TOTAL * CAP, D), jnp.zeros((1, D), flat_in.dtype)], 0)
    first_rows = low_back(padded[targets[:, 0]])
    second_rows = low_back(padded[targets[:, 1]])
    gate_rows = gates.reshape(total_rows, 2)
    mixture = gate_rows[:, 0:1] * first_rows + gate_rows[:, 1:2] * second_rows
    return middle + mixture.reshape(IMG_DEV, LEN, D)

def forward(x_float, weights, pictures_alive_per_shard, expert_ids, slot_index):
    x_groups = x_float.reshape(N_DP, IMG_DEV, LEN, D)
    id_groups = expert_ids.reshape(N_DP, IMG_DEV, LEN, 2)
    slot_groups = slot_index.reshape(N_DP, IMG_DEV, LEN, 2)
    result = lax.map(jax.checkpoint(partial(group_block, weights)), (x_groups, pictures_alive_per_shard, id_groups, slot_groups))
    return result.reshape(IMAGES, LEN, D)

def reference(block_input, gains, w_qkv, w_o, w_router, w_in, w_out, pictures_alive_per_shard, expert_ids, slot_index, cotangent):
    floats = (block_input.astype(jnp.float32), gains.astype(jnp.float32), w_qkv.astype(jnp.float32), w_o.astype(jnp.float32), w_router.astype(jnp.float32), w_in.astype(jnp.float32), w_out.astype(jnp.float32))

    def whole(x_float, gain_f, qkv_f, outproj_f, router_weight_float, expin_f, expout_f):
        return forward(x_float, (gain_f, qkv_f, outproj_f, router_weight_float, expin_f, expout_f), pictures_alive_per_shard, expert_ids, slot_index)
    output, pull_back = jax.vjp(whole, *floats)
    grads = pull_back(cotangent.astype(jnp.float32))
    return (output.astype(jnp.bfloat16), grads[0], grads[1], grads[2], grads[3], grads[4], grads[5], grads[6])
```

```python
import math
from typing import NamedTuple

import jax
import jax.numpy as jnp
from jax import lax
from jax.experimental import pallas as pl
from jax.experimental.pallas import tpu as pltpu
from jax.sharding import PartitionSpec as P

HEAD_DIM = 64
TOK_IMG = 197
CAP = 192


epsilon = 1e-06
negative_fill = -1e30


def as_sent(shard):
    return jax.tree.map(lambda a: a.astype(jnp.bfloat16) if a.dtype == jnp.float32 else a, shard)


def layer_norm(values, gain):
    centre = values - jnp.mean(values, -1, keepdims=True)
    spread = jnp.mean(centre * centre, -1, keepdims=True)
    return centre * lax.rsqrt(spread + epsilon) * gain


def gelu_exact(values):
    return jax.nn.gelu(values, approximate=False)


def gate_values(logits, chosen):
    router_probs = jax.nn.softmax(logits, axis=-1)
    return jnp.einsum("re,rke->rk", router_probs, chosen)


def rows_in(values):
    return lax.all_gather(values, "tensor", axis=1, tiled=True)


def rows_out(values):
    return lax.psum_scatter(values, "tensor", scatter_dimension=1, tiled=True)


def grads_in(values):
    return jax.tree.map(
        lambda part, own: part.astype(own.dtype),
        lax.all_gather(as_sent(values), "tensor", axis=1, tiled=True),
        values,
    )


def grads_out(values):
    return lax.psum_scatter(values, "tensor", scatter_dimension=1, tiled=True)


def attention_scores(queries, keys_all, key_live, scale_factor):
    gating_logits_matrix = (
        jnp.einsum("ilhe,imhe->ihlm", queries, keys_all, preferred_element_type=jnp.float32)
        * scale_factor
    )
    return jnp.where(key_live[None, None, None, :], gating_logits_matrix, negative_fill)


def body(
    block_input,
    gains,
    w_qkv,
    w_o,
    w_router,
    w_in,
    w_out,
    pictures_alive_per_shard,
    expert_ids,
    slot_index,
    cotangent,
):
    tensor_size = lax.axis_size("tensor")
    tensor_pos = lax.axis_index("tensor")
    images, quarter, model_width = block_input.shape
    length = quarter * tensor_size
    all_rows = images * length
    own_rows = images * quarter
    start_row = tensor_pos * quarter
    experts = w_in.shape[1]
    slot_count = experts * CAP
    key_live = jnp.arange(length) < TOK_IMG
    live_all = (
        (jnp.arange(images) < pictures_alive_per_shard[0])[:, None] & key_live[None, :]
    ).astype(jnp.float32)
    live_own = lax.dynamic_slice_in_dim(live_all, start_row, quarter, 1)
    gathered = (
        lax.all_gather(gains, "dp", axis=0, tiled=True),
        lax.all_gather(w_qkv, "dp", axis=0, tiled=True),
        lax.all_gather(w_o, "dp", axis=1, tiled=True),
        lax.all_gather(w_router, "dp", axis=0, tiled=True),
        lax.all_gather(w_in, "dp", axis=0, tiled=True),
        lax.all_gather(w_out, "dp", axis=2, tiled=True),
    )
    gain_all, qkv_all, outproj_all, router_all, expin_all, expout_all = gathered
    head_cols = qkv_all.shape[2]
    local_heads = head_cols // HEAD_DIM
    scale_factor = 1.0 / math.sqrt(HEAD_DIM)
    gain_one = gain_all[:, 0].astype(jnp.float32)
    gain_two = gain_all[:, 1].astype(jnp.float32)
    x_float = block_input.astype(jnp.float32)
    normed = layer_norm(x_float, gain_one).astype(jnp.bfloat16)
    normed_all = rows_in(normed).reshape(all_rows, model_width)
    project = jnp.einsum(
        "rd,djc->rjc", normed_all, qkv_all, preferred_element_type=jnp.float32
    ).astype(jnp.bfloat16)
    queries = project[:, 0].reshape(images, length, local_heads, HEAD_DIM)
    keys_all = project[:, 1].reshape(images, length, local_heads, HEAD_DIM)
    values_all = project[:, 2].reshape(images, length, local_heads, HEAD_DIM)
    masked = attention_scores(queries, keys_all, key_live, scale_factor)
    top_score = jnp.max(masked, -1, keepdims=True)
    expd = jnp.exp(masked - top_score)
    total = jnp.sum(expd, -1, keepdims=True)
    att_probs = expd / total
    log_total = top_score + jnp.log(total)
    attended = jnp.einsum(
        "ihlm,imhe->ilhe",
        att_probs.astype(jnp.bfloat16),
        values_all,
        preferred_element_type=jnp.float32,
    )
    attended = attended.astype(jnp.bfloat16).reshape(all_rows, head_cols)
    branch_part = jnp.dot(attended, outproj_all, preferred_element_type=jnp.float32).reshape(
        images, length, model_width
    )
    middle = x_float + live_own[:, :, None] * rows_out(branch_part)
    normed_two = layer_norm(middle, gain_two).astype(jnp.bfloat16)
    normed_two_all = rows_in(normed_two).reshape(all_rows, model_width)
    own_flat = normed_two.reshape(own_rows, model_width)
    expert_range = jnp.arange(experts)
    own_ids = lax.dynamic_slice_in_dim(expert_ids, start_row, quarter, 1).reshape(own_rows, 2)
    chosen = (own_ids[:, :, None] == expert_range[None, None, :]).astype(jnp.float32)
    targets = jnp.where(slot_index >= 0, expert_ids * CAP + slot_index, -1).reshape(all_rows, 2)
    slot_ids = jnp.arange(slot_count)
    first_hot = (targets[:, 0:1] == slot_ids[None, :]).astype(jnp.bfloat16)
    second_hot = (targets[:, 1:2] == slot_ids[None, :]).astype(jnp.bfloat16)
    dispatched = jnp.einsum(
        "rs,rd->sd", first_hot, normed_two_all, preferred_element_type=jnp.float32
    )
    dispatched = dispatched + jnp.einsum(
        "rs,rd->sd", second_hot, normed_two_all, preferred_element_type=jnp.float32
    )
    dispatched = dispatched.astype(jnp.bfloat16).reshape(experts, CAP, model_width)
    hidden = jnp.einsum("ecd,def->ecf", dispatched, expin_all, preferred_element_type=jnp.float32)
    active = gelu_exact(hidden).astype(jnp.bfloat16)
    expert_part = jnp.einsum("ecf,fed->ecd", active, expout_all, preferred_element_type=jnp.float32)
    expert_part = expert_part.astype(jnp.bfloat16).reshape(slot_count, model_width)
    first_rows = jnp.dot(first_hot, expert_part, preferred_element_type=jnp.float32)
    second_rows = jnp.dot(second_hot, expert_part, preferred_element_type=jnp.float32)
    logits = jnp.dot(own_flat, router_all, preferred_element_type=jnp.float32)
    gates = gate_values(logits, chosen)
    first_own, second_own = rows_out(
        (
            first_rows.reshape(images, length, model_width),
            second_rows.reshape(images, length, model_width),
        )
    )
    gate_grid = gates.reshape(images, quarter, 2)
    output = middle + gate_grid[:, :, 0:1] * first_own + gate_grid[:, :, 1:2] * second_own
    grad_output = cotangent.astype(jnp.float32)
    grad_first = (gate_grid[:, :, 0:1] * grad_output).astype(jnp.bfloat16)
    grad_second = (gate_grid[:, :, 1:2] * grad_output).astype(jnp.bfloat16)
    grad_gates = jnp.stack(
        [jnp.sum(grad_output * first_own, -1), jnp.sum(grad_output * second_own, -1)], -1
    ).reshape(own_rows, 2)
    leading_cotangent, second_back = grads_in((grad_first, grad_second))
    leading_cotangent = leading_cotangent.reshape(all_rows, model_width)
    second_back = second_back.reshape(all_rows, model_width)
    unused_gates, gate_pull = jax.vjp(lambda values: gate_values(values, chosen), logits)
    grad_logits = gate_pull(grad_gates)[0].astype(jnp.bfloat16)
    grad_router = jnp.einsum("rd,re->de", own_flat, grad_logits, preferred_element_type=jnp.float32)
    router_back = jnp.einsum(
        "re,de->rd", grad_logits, router_all, preferred_element_type=jnp.float32
    )
    grad_expert = jnp.einsum(
        "rs,rd->sd", first_hot, leading_cotangent, preferred_element_type=jnp.float32
    )
    grad_expert = grad_expert + jnp.einsum(
        "rs,rd->sd", second_hot, second_back, preferred_element_type=jnp.float32
    )
    grad_expert = grad_expert.astype(jnp.bfloat16).reshape(experts, CAP, model_width)
    grad_active = jnp.einsum(
        "ecd,fed->ecf", grad_expert, expout_all, preferred_element_type=jnp.float32
    )
    grad_expout = jnp.einsum(
        "ecf,ecd->fed", active, grad_expert, preferred_element_type=jnp.float32
    )
    unused_gelu, gelu_pull = jax.vjp(gelu_exact, hidden)
    grad_hidden = gelu_pull(grad_active)[0].astype(jnp.bfloat16)
    grad_expin = jnp.einsum(
        "ecd,ecf->def", dispatched, grad_hidden, preferred_element_type=jnp.float32
    )
    grad_dispatch = jnp.einsum(
        "ecf,def->ecd", grad_hidden, expin_all, preferred_element_type=jnp.float32
    )
    grad_dispatch = grad_dispatch.astype(jnp.bfloat16).reshape(slot_count, model_width)
    back_rows = jnp.dot(first_hot, grad_dispatch, preferred_element_type=jnp.float32)
    back_rows = back_rows + jnp.dot(second_hot, grad_dispatch, preferred_element_type=jnp.float32)
    grad_normed_two = grads_out(
        back_rows.reshape(images, length, model_width)
    ) + router_back.reshape(images, quarter, model_width)
    unused_two, norm_two_pull = jax.vjp(layer_norm, middle, gain_two)
    grad_middle_norm, grad_gain_two = norm_two_pull(grad_normed_two)
    grad_middle = grad_output + grad_middle_norm
    grad_branch = (live_own[:, :, None] * grad_middle).astype(jnp.bfloat16)
    grad_branch_all = grads_in(grad_branch).reshape(all_rows, model_width)
    grad_outproj = jnp.einsum(
        "rc,rd->cd", attended, grad_branch_all, preferred_element_type=jnp.float32
    )
    grad_attended = jnp.einsum(
        "rd,cd->rc", grad_branch_all, outproj_all, preferred_element_type=jnp.float32
    )
    grad_attended = grad_attended.astype(jnp.bfloat16).reshape(
        images, length, local_heads, HEAD_DIM
    )
    masked_again = attention_scores(queries, keys_all, key_live, scale_factor)
    probs_again = jnp.exp(masked_again - log_total)
    grad_values = jnp.einsum(
        "ihlm,ilhe->imhe",
        probs_again.astype(jnp.bfloat16),
        grad_attended,
        preferred_element_type=jnp.float32,
    )
    grad_values = grad_values.astype(jnp.bfloat16)
    grad_probs = jnp.einsum(
        "ilhe,imhe->ihlm", grad_attended, values_all, preferred_element_type=jnp.float32
    )
    grad_scores = probs_again * (grad_probs - jnp.sum(probs_again * grad_probs, -1, keepdims=True))
    grad_scores = grad_scores.astype(jnp.bfloat16)
    grad_queries = (
        jnp.einsum("ihlm,imhe->ilhe", grad_scores, keys_all, preferred_element_type=jnp.float32)
        * scale_factor
    ).astype(jnp.bfloat16)
    grad_keys = (
        jnp.einsum("ihlm,ilhe->imhe", grad_scores, queries, preferred_element_type=jnp.float32)
        * scale_factor
    ).astype(jnp.bfloat16)
    grad_project = jnp.stack([grad_queries, grad_keys, grad_values], 2).reshape(
        all_rows, 3, head_cols
    )
    grad_qkv = jnp.einsum(
        "rd,rjc->djc", normed_all, grad_project, preferred_element_type=jnp.float32
    )
    normed_back = jnp.einsum(
        "rjc,djc->rd", grad_project, qkv_all, preferred_element_type=jnp.float32
    )
    grad_normed = grads_out(normed_back.reshape(images, length, model_width))
    unused_one, norm_one_pull = jax.vjp(layer_norm, x_float, gain_one)
    grad_x_norm, grad_gain_one = norm_one_pull(grad_normed)
    grad_input = grad_middle + grad_x_norm
    router_sum, gain_sum = lax.psum(
        (grad_router, jnp.stack([grad_gain_one, grad_gain_two], 1)), "tensor"
    )
    expert_fractions = (
        lax.psum_scatter(gain_sum, "dp", scatter_dimension=0, tiled=True),
        lax.psum_scatter(grad_qkv, "dp", scatter_dimension=0, tiled=True),
        lax.psum_scatter(grad_outproj, "dp", scatter_dimension=1, tiled=True),
        lax.psum_scatter(router_sum, "dp", scatter_dimension=0, tiled=True),
        lax.psum_scatter(grad_expin, "dp", scatter_dimension=0, tiled=True),
        lax.psum_scatter(grad_expout, "dp", scatter_dimension=2, tiled=True),
    )
    return (
        output.astype(jnp.bfloat16),
        grad_input,
        expert_fractions[0],
        expert_fractions[1],
        expert_fractions[2],
        expert_fractions[3],
        expert_fractions[4],
        expert_fractions[5],
    )


MESH = pl.DeviceIdType.MESH
BF = jnp.bfloat16
F32 = jnp.float32
VMEM_BYTES = 60 << 20


class Sizes(NamedTuple):
    n_dp: int
    n_t: int
    images: int
    quarter: int
    rows: int
    irows: int
    width: int
    shard: int
    heads: int
    experts: int
    ff: int
    lanes: int

    @property
    def half(self):
        return self.experts // 2

    @property
    def slots(self):
        return self.half * CAP


def up(value, step):
    return -(-value // step) * step


def norm_parts(values):
    centre = values - jnp.mean(values, -1, keepdims=True)
    scale = lax.rsqrt(jnp.mean(centre * centre, -1, keepdims=True) + epsilon)
    return centre * scale, scale


def norm_back(values, gain, grad):
    unit, scale = norm_parts(values)
    inner = grad * gain
    mean_a = jnp.mean(inner, -1, keepdims=True)
    mean_b = jnp.mean(inner * unit, -1, keepdims=True)
    return scale * (inner - mean_a - unit * mean_b), unit


def dot(a, b):
    return jnp.dot(a, b, preferred_element_type=F32)


def dot_nt(a, b):
    return lax.dot_general(a, b, (((1,), (1,)), ((), ())), preferred_element_type=F32)


def dot_tn(a, b):
    return lax.dot_general(a, b, (((0,), (0,)), ((), ())), preferred_element_type=F32)


class Place:
    def __init__(self, s):
        self.s = s
        self.dp = lax.axis_index("dp")
        self.t = lax.axis_index("tensor")
        self.c = lax.rem(self.dp, 2)
        self.x = lax.rem(self.dp // 2, 2)
        self.y = self.dp // 4
        self.chip = self.dp // 2
        self.chip_x = self.y * 2 + (1 - self.x)
        self.chip_y = (1 - self.y) * 2 + self.x
        self.sib = (self.chip * 2 + (1 - self.c), self.t)
        self.nx = (self.chip_x * 2 + self.c, self.t)
        self.ny = (self.chip_y * 2 + self.c, self.t)

    def ring_dp(self, k):
        return lax.rem(self.dp + k, self.s.n_dp)

    def ring_t(self, k):
        return lax.rem(self.t + k, self.s.n_t)

    def from_t(self, k):
        return lax.rem(self.t + self.s.n_t - k, self.s.n_t)

    def greet(self):
        barrier = pltpu.get_barrier_semaphore()
        for k in range(1, self.s.n_dp):
            pl.semaphore_signal(barrier, inc=1, device_id=(self.ring_dp(k), self.t), device_id_type=MESH)
        for k in range(1, self.s.n_t):
            pl.semaphore_signal(barrier, inc=1, device_id=(self.dp, self.ring_t(k)), device_id_type=MESH)
        pl.semaphore_wait(barrier, self.s.n_dp + self.s.n_t - 2)


class Copies:
    def __init__(self, send, recv, local):
        self.send, self.recv, self.local = send, recv, local
        self.n = 0
        self.m = 0
        self.sent = []

    def to(self, src, dst, device):
        copy = pltpu.make_async_remote_copy(
            src_ref=src,
            dst_ref=dst,
            send_sem=self.send.at[self.n],
            recv_sem=self.recv.at[self.n],
            device_id=device,
            device_id_type=MESH,
        )
        self.n += 1
        copy.start()
        self.sent.append(copy)
        return copy

    def here(self, src, dst):
        copy = pltpu.make_async_copy(src, dst, self.local.at[self.m])
        self.m += 1
        copy.start()
        return copy

    def finish(self):
        for copy in self.sent:
            copy.wait_send()


def head_masks(s):
    lane = lax.broadcasted_iota(jnp.int32, (s.irows, s.heads), 1)
    return [(lane // HEAD_DIM) == h for h in range(s.heads // HEAD_DIM)]


def stack_heads(values, masks):
    zero = jnp.zeros_like(values)
    return jnp.concatenate([jnp.where(mask, values, zero) for mask in masks], 0)


def pick_heads(stacked, masks, irows):
    out = stacked[:irows]
    for h in range(1, len(masks)):
        out = jnp.where(masks[h], stacked[h * irows : (h + 1) * irows], out)
    return out


def front_kernel(
    s,
    x_ref, dz_ref, wq_ref, wo_ref, sm_ref, win_ref, wout_ref, live_ref, tgt_ref,
    win_all, wout_all, n2_all, dz_all, prob_all, tgt_all,
    y_ref, n2_ref, prob_ref, qkv_ref, p_ref, n1_ref, o_ref, wq_all, wo_all, small_ref,
    x_all, sm_all, wo_z, blk, img, oimg, oblk, o_send, send, recv, local,
):
    here = Place(s)
    dp, t, c = here.dp, here.t, here.c
    here.greet()
    go = Copies(send, recv, local)
    nt = s.n_t

    keep_in = go.here(win_ref.at[c], win_all.at[:, dp])
    keep_out = go.here(wout_ref.at[c], wout_all.at[:, dp])
    give_in = go.to(win_ref.at[1 - c], win_all.at[:, dp], here.sib)
    give_out = go.to(wout_ref.at[1 - c], wout_all.at[:, dp], here.sib)
    keep_sm = go.here(sm_ref, sm_all.at[dp])
    keep_wq = go.here(wq_ref, wq_all.at[dp])
    keep_wo = go.here(wo_ref, wo_z.at[t])
    wo_copies = [go.to(wo_ref, wo_z.at[t], (dp, here.ring_t(k))) for k in range(1, nt)]
    sm_copies = [go.to(sm_ref, sm_all.at[dp], (here.ring_dp(k), t)) for k in range(1, s.n_dp)]
    wq_copies = [go.to(wq_ref, wq_all.at[dp], (here.ring_dp(k), t)) for k in range(1, s.n_dp)]
    x_copies = [go.to(x_ref, x_all.at[t], (dp, here.ring_t(k))) for k in range(1, nt)]
    tgt_copy = go.to(tgt_ref, tgt_all.at[c], here.sib)
    keep_tgt = go.here(tgt_ref, tgt_all.at[c])
    dz_sib = go.to(dz_ref, dz_all.at[c, t], here.sib)
    keep_dz = go.here(dz_ref, dz_all.at[c, t])

    mine = pl.ds(2 * here.chip, 2)
    keep_in.wait()
    give_in.wait_recv()
    in_x = go.to(win_all.at[:, mine], win_all.at[:, mine], here.nx)
    in_y = go.to(win_all.at[:, mine], win_all.at[:, mine], here.ny)

    keep_sm.wait()
    for copy in sm_copies:
        copy.wait_recv()
    small = jnp.sum(sm_all[...].astype(F32), 0)
    small_ref[...] = small
    gain_one = small[s.experts : s.experts + 1]
    gain_two = small[s.experts + 1 : s.experts + 2]
    keep_wq.wait()
    for copy in wq_copies:
        copy.wait_recv()

    keep_out.wait()
    give_out.wait_recv()
    out_x = go.to(wout_all.at[:, mine], wout_all.at[:, mine], here.nx)
    out_y = go.to(wout_all.at[:, mine], wout_all.at[:, mine], here.ny)

    keep_wo.wait()
    for copy in wo_copies:
        copy.wait_recv()
    keep_wo_all = go.here(wo_z, wo_all.at[dp])
    wo_out = [go.to(wo_z, wo_all.at[dp], (here.ring_dp(k), t)) for k in range(1, s.n_dp)]

    def project(slot, values):
        unit, _ = norm_parts(values.astype(F32))
        normed = (unit * gain_one).astype(BF)
        n1_ref[slot] = normed
        weights = wq_all[...].reshape(s.width, 3 * s.heads)
        blk[slot] = dot(normed, weights)

    project(t, x_ref[...])
    for k, copy in enumerate(x_copies, 1):
        copy.wait_recv()
        project(here.from_t(k), x_all[here.from_t(k)])

    dz_copies = [go.to(dz_ref, dz_all.at[c, t], (dp, here.ring_t(k))) for k in range(1, nt)]

    from_x = pl.ds(2 * here.chip_x, 2)
    from_y = pl.ds(2 * here.chip_y, 2)
    low_half, high_half = pl.ds(0, s.half // 2), pl.ds(s.half // 2, s.half // 2)
    in_x.wait_recv()
    in_on_y = go.to(win_all.at[low_half, from_x], win_all.at[low_half, from_x], here.ny)
    in_y.wait_recv()
    in_on_x = go.to(win_all.at[high_half, from_y], win_all.at[high_half, from_y], here.nx)

    length = s.quarter * nt
    img[:, pl.ds(length, s.irows - length), :] = jnp.zeros((s.images, s.irows - length, 3 * s.heads), F32)
    for i in range(s.images):
        for q in range(nt):
            img[i, pl.ds(q * s.quarter, s.quarter), :] = blk[q, pl.ds(i * s.quarter, s.quarter), :]

    masks = head_masks(s)

    def attend(i, carry):
        block = img[i].astype(BF)
        qkv_ref[i] = block
        queries = stack_heads(block[:, : s.heads], masks)
        scores = dot_nt(queries, block[:, s.heads : 2 * s.heads]) * (1.0 / math.sqrt(HEAD_DIM))
        key = lax.broadcasted_iota(jnp.int32, scores.shape, 1)
        scores = jnp.where(key < TOK_IMG, scores, negative_fill)
        expd = jnp.exp(scores - jnp.max(scores, -1, keepdims=True))
        probs = (expd / jnp.sum(expd, -1, keepdims=True)).astype(BF)
        p_ref[i] = probs
        oimg[i] = pick_heads(dot(probs, block[:, 2 * s.heads :]), masks, s.irows)
        return carry

    lax.fori_loop(0, s.images, attend, 0)
    used = s.images * s.quarter
    for q in range(nt):
        oblk[q, pl.ds(used, s.rows - used), :] = jnp.zeros((s.rows - used, s.heads), F32)
        for i in range(s.images):
            oblk[q, pl.ds(i * s.quarter, s.quarter), :] = oimg[i, pl.ds(q * s.quarter, s.quarter), :]
        o_send[q] = oblk[q].astype(BF)
    o_copies = [go.to(o_send.at[here.ring_t(k)], o_ref.at[t], (dp, here.ring_t(k))) for k in range(1, nt)]
    o_ref[t] = o_send[t]

    keep_wo_all.wait()
    for copy in wo_out:
        copy.wait_recv()
    for copy in o_copies:
        copy.wait_recv()
    branch = jnp.zeros((s.rows, s.width), F32)
    for q in range(nt):
        branch = branch + dot_nt(o_ref[q], wo_all[:, q].reshape(s.width, s.heads))
    middle = x_ref[...].astype(F32) + live_ref[...] * branch
    y_ref[...] = middle
    unit, _ = norm_parts(middle)
    normed_two = (unit * gain_two).astype(BF)
    n2_ref[...] = normed_two
    n2_sib = go.to(n2_ref, n2_all.at[c, t], here.sib)
    n2_copies = [go.to(n2_ref, n2_all.at[c, t], (dp, here.ring_t(k))) for k in range(1, nt)]
    keep_n2 = go.here(n2_ref, n2_all.at[c, t])
    logits = dot_nt(small[: s.experts].astype(BF), normed_two)
    expd = jnp.exp(logits - jnp.max(logits, 0, keepdims=True))
    prob_ref[...] = jnp.zeros((s.experts, s.lanes), F32)
    prob_ref[:, : s.rows] = expd / jnp.sum(expd, 0, keepdims=True)
    pr_sib = go.to(prob_ref, prob_all.at[c, t], here.sib)
    pr_copies = [go.to(prob_ref, prob_all.at[c, t], (dp, here.ring_t(k))) for k in range(1, nt)]
    keep_pr = go.here(prob_ref, prob_all.at[c, t])

    out_x.wait_recv()
    out_on_y = go.to(wout_all.at[low_half, from_x], wout_all.at[low_half, from_x], here.ny)
    out_y.wait_recv()
    out_on_x = go.to(wout_all.at[high_half, from_y], wout_all.at[high_half, from_y], here.nx)

    on = []
    for k in range(1, nt):
        slot = here.from_t(k)
        for array, copies in ((dz_all, dz_copies), (n2_all, n2_copies), (prob_all, pr_copies)):
            copies[k - 1].wait_recv()
            on.append(go.to(array.at[c, slot], array.at[c, slot], here.sib))

    for copy in (keep_tgt, keep_dz, keep_n2, keep_pr):
        copy.wait()
    for copy in [tgt_copy, dz_sib, n2_sib, pr_sib, in_on_y, in_on_x, out_on_y, out_on_x] + on:
        copy.wait_recv()
    go.finish()


def expert_kernel(
    s,
    n2_ref, dz_ref, tgt_ref, prob_ref, win_ref, wout_ref,
    dx_ref, ge_ref, gi_ref, go_ref, dpr_ref,
    pr, dpr,
):
    e = pl.program_id(0)
    core = lax.rem(lax.axis_index("dp"), 2)
    expert = core * s.half + e

    @pl.when(e == 0)
    def _():
        for q in range(2):
            pr[q] = jnp.concatenate([prob_ref[q, k][:, : s.rows] for k in range(s.n_t)], 1)

    ids = expert * CAP + lax.broadcasted_iota(jnp.int32, (CAP, s.n_t * s.rows), 0)
    hits, xs, zs, gates = [], [], [], []
    for q in range(2):
        hit = (tgt_ref[q, 0:1, :] == ids) | (tgt_ref[q, 1:2, :] == ids)
        hot = jnp.where(hit, 1.0, 0.0).astype(BF)
        hits.append(hit)
        xs.append(dot(hot, n2_ref[q]).astype(BF))
        zs.append(dot(hot, dz_ref[q]))
        row = pr[q, pl.ds(expert, 1), :]
        gates.append(jnp.sum(jnp.where(hit, row, 0.0), 1, keepdims=True))
    x_in = jnp.concatenate(xs, 0)
    z_in = jnp.concatenate(zs, 0)
    gate = jnp.concatenate(gates, 0)
    w_in, w_out = win_ref[0], wout_ref[0]
    hidden = dot(x_in, w_in)
    size = jnp.abs(hidden)
    bell = jnp.exp(-0.5 * hidden * hidden)
    u = 1.0 / (1.0 + (0.3275911 / math.sqrt(2.0)) * size)
    poly = u * (0.254829592 + u * (-0.284496736 + u * (1.421413741 + u * (-1.453152027 + u * 1.061405429))))
    tail = 0.5 * poly * bell
    phi = jnp.where(hidden >= 0, 1.0 - tail, tail)
    active = (hidden * phi).astype(BF)
    slope = phi + hidden * bell * (1.0 / math.sqrt(2.0 * math.pi))
    out = dot_nt(active, w_out).astype(BF).astype(F32)
    dgate = jnp.sum(z_in * out, 1, keepdims=True)
    grad = (gate * z_in).astype(BF)
    go_ref[...] = dot_tn(grad, active).astype(BF).reshape(go_ref.shape)
    dhidden = (dot(grad, w_out) * slope).astype(BF)
    gi_ref[...] = dot_tn(x_in, dhidden).astype(BF).reshape(gi_ref.shape)
    dx_ref[...] = dot_nt(dhidden, w_in).astype(BF).reshape(dx_ref.shape)
    ge_ref[...] = (gate * out).astype(BF).reshape(ge_ref.shape)
    for q in range(2):
        row = jnp.sum(jnp.where(hits[q], dgate[q * CAP : (q + 1) * CAP], 0.0), 0, keepdims=True)
        dpr[q, pl.ds(e, 1), :] = row

    @pl.when(e == s.half - 1)
    def _():
        dpr_ref[...] = jnp.zeros(dpr_ref.shape, F32)
        for q in range(2):
            for k in range(s.n_t):
                dpr_ref[q, k, :, : s.rows] = dpr[q][:, k * s.rows : (k + 1) * s.rows]


def back_kernel(
    s,
    x_ref, dz_ref, y_ref, n2_ref, prob_ref, live_ref, tcol_ref, qkv_ref, p_ref, n1_ref, o_ref,
    wq_ref, wo_ref, small_ref, dpr_ref, dx_ref, ge_ref, gi_ref, go_ref,
    out_ref, gx_ref, gw_ref, gqo_ref, gsm_ref,
    dxv, gev, dprf, dprz, comb, rs_send, rs_recv, m_send, m_recv, n_send, n_recv,
    da_s, do_send, do_recv, doblk, doimg, dimg, dblk, dqkv, go_send, go_recv, gq_send, gq_recv,
    sm_send, sm_z, sm_dp, own, ra, rb, sa, sb, fa, fb, fin, fin_recv, send, recv, local,
):
    here = Place(s)
    dp, t, c = here.dp, here.t, here.c
    x, y = here.x, here.y
    here.greet()
    go = Copies(send, recv, local)
    nt = s.n_t
    per = s.half // 2

    ra_copies, rb_copies = [], []
    for j in range(2):
        piece = pl.ds(j * per, per)
        ra_copies.append(go.to(gi_ref.at[:, 1 - x, piece], ra.at[j], here.nx))
        rb_copies.append(go.to(go_ref.at[1 - y, :, piece], rb.at[j], here.ny))
    dx_sib = go.to(dx_ref.at[1 - c], dxv.at[c], here.sib)
    dpr_sib = go.to(dpr_ref.at[1 - c], dprf.at[:, c], here.sib)
    ge_sib = go.to(ge_ref.at[1 - c], gev.at[c], here.sib)
    keep_dx = go.here(dx_ref.at[c], dxv.at[c])
    keep_dpr = go.here(dpr_ref.at[c], dprf.at[:, c])
    keep_ge = go.here(ge_ref.at[c], gev.at[c])
    own_a = go.here(gi_ref.at[:, x], own.at[0])
    own_b = go.here(go_ref.at[y], own.at[1])

    chunk = s.slots // 2

    def combine(values, half, q, total):
        first = tcol_ref[q, :, 0:1]
        second = tcol_ref[q, :, 1:2]
        for j in range(2):
            ids = half * s.slots + j * chunk + lax.broadcasted_iota(jnp.int32, (s.rows, chunk), 1)
            hot = jnp.where((first == ids) | (second == ids), 1.0, 0.0).astype(BF)
            total = total + dot(hot, values[half, pl.ds(j * chunk, chunk), :])
        return total

    zero_rows = jnp.zeros((s.rows, s.width), F32)
    keep_dx.wait()
    for k in range(nt):
        comb[k] = combine(dxv, c, here.ring_t(k), zero_rows)
    dx_sib.wait_recv()
    rs_copies = []
    for k in range(1, nt):
        q = here.ring_t(k)
        rs_send[k - 1] = combine(dxv, 1 - c, q, comb[k]).astype(BF)
        rs_copies.append(go.to(rs_send.at[k - 1], rs_recv.at[k - 1], (dp, q)))
    keep_dpr.wait()
    dpr_sib.wait_recv()
    dpr_copies = [go.to(dprf.at[here.ring_t(k)], dprz.at[k - 1], (dp, here.ring_t(k))) for k in range(1, nt)]
    comb[0] = combine(dxv, 1 - c, t, comb[0])

    keep_ge.wait()
    ge_sib.wait_recv()
    for k in range(1, nt):
        q = here.ring_t(k)
        m_send[k - 1] = combine(gev, 1 - c, q, combine(gev, c, q, zero_rows)).astype(BF)
    out_own = combine(gev, 1 - c, t, combine(gev, c, t, zero_rows))
    gx_ref[...] = out_own

    dprobs = dprf[t]
    for k, copy in enumerate(dpr_copies):
        copy.wait_recv()
        dprobs = dprobs + dprz[k]
    dprobs = dprobs.reshape(s.experts, s.lanes)
    probs = prob_ref[...]
    dlogits = (probs * (dprobs - jnp.sum(probs * dprobs, 0, keepdims=True))).astype(BF)[:, : s.rows]
    small = small_ref[...]
    gain_one = small[s.experts : s.experts + 1]
    gain_two = small[s.experts + 1 : s.experts + 2]
    grad_router = dot_tn(n2_ref[...], dlogits.T).T
    dn2 = comb[0] + dot_tn(dlogits, small[: s.experts].astype(BF))
    for k, copy in enumerate(rs_copies):
        copy.wait_recv()
        dn2 = dn2 + rs_recv[k].astype(F32)
    middle = y_ref[...]
    dy_ln, unit = norm_back(middle, gain_two, dn2)
    dgain_two = jnp.sum(dn2 * unit, 0, keepdims=True)
    dy = dz_ref[...].astype(F32) + dy_ln
    comb[0] = dy
    da = (live_ref[...] * dy).astype(BF)
    da_s[...] = da
    for q in range(nt):
        do_send[q] = dot(da, wo_ref[:, q].reshape(s.width, s.heads)).astype(BF)
    do_copies = [go.to(do_send.at[here.ring_t(k)], do_recv.at[t], (dp, here.ring_t(k))) for k in range(1, nt)]
    do_recv[t] = do_send[t]
    for q in range(nt):
        go_send[q] = dot_tn(da, o_ref[q]).astype(BF)

    own_a.wait()
    own_b.wait()

    def add_up(a, b, out):
        def step(i, carry):
            out[i] = (a[i].astype(F32) + b[i].astype(F32)).astype(out.dtype)
            return carry

        lax.fori_loop(0, out.shape[0], step, 0)

    fa_copies, fb_copies = [], []

    def pump(j):
        piece = pl.ds(j * per, per)
        ra_copies[j].wait_recv()
        add_up(own.at[0, 1 - y, piece], ra.at[j, 1 - y], sa.at[j])
        fa_copies.append(go.to(sa.at[j], fa.at[j], here.ny))
        rb_copies[j].wait_recv()
        add_up(own.at[1, 1 - x, piece], rb.at[j, 1 - x], sb.at[j])
        fb_copies.append(go.to(sb.at[j], fb.at[j], here.nx))

    pump(0)

    for copy in do_copies:
        copy.wait_recv()
    go_copies = [go.to(go_send.at[here.ring_t(k)], go_recv.at[k - 1], (dp, here.ring_t(k))) for k in range(1, nt)]
    m_copies = [go.to(m_send.at[k - 1], m_recv.at[k - 1], (dp, here.ring_t(k))) for k in range(1, nt)]
    length = s.quarter * nt
    doblk[...] = do_recv[...].astype(F32)
    doimg[:, pl.ds(length, s.irows - length), :] = jnp.zeros((s.images, s.irows - length, s.heads), F32)
    for i in range(s.images):
        for q in range(nt):
            doimg[i, pl.ds(q * s.quarter, s.quarter), :] = doblk[q, pl.ds(i * s.quarter, s.quarter), :]
    masks = head_masks(s)
    scale_factor = 1.0 / math.sqrt(HEAD_DIM)

    def attend_back(i, carry):
        block = qkv_ref[i]
        queries = stack_heads(block[:, : s.heads], masks)
        grads = stack_heads(doimg[i].astype(BF), masks)
        probs = p_ref[i]
        dvalues = dot_tn(probs, grads)
        dprob = dot_nt(grads, block[:, 2 * s.heads :])
        wide = probs.astype(F32)
        both = wide * dprob
        dscore = (both - wide * jnp.sum(both, -1, keepdims=True)).astype(BF)
        dqueries = pick_heads(dot(dscore, block[:, s.heads : 2 * s.heads]), masks, s.irows)
        dkeys = dot_tn(dscore, queries)
        dimg[i, :, : s.heads] = dqueries * scale_factor
        dimg[i, :, s.heads : 2 * s.heads] = dkeys * scale_factor
        dimg[i, :, 2 * s.heads :] = dvalues
        return carry

    lax.fori_loop(0, s.images, attend_back, 0)
    used = s.images * s.quarter
    for q in range(nt):
        dblk[q, pl.ds(used, s.rows - used), :] = jnp.zeros((s.rows - used, 3 * s.heads), F32)
        for i in range(s.images):
            dblk[q, pl.ds(i * s.quarter, s.quarter), :] = dimg[i, pl.ds(q * s.quarter, s.quarter), :]
    dqkv[...] = dblk[...].astype(BF)
    w_qkv = wq_ref[...].reshape(s.width, 3 * s.heads)
    n_copies = []
    dgain_one = jnp.zeros((1, s.width), F32)
    for k in list(range(1, nt)) + [0]:
        q = here.ring_t(k)
        part = dot_nt(dqkv[q], w_qkv)
        dgain_one = dgain_one + jnp.sum(part * n1_ref[q].astype(F32), 0, keepdims=True)
        if k:
            n_send[k - 1] = part.astype(BF)
            n_copies.append(go.to(n_send.at[k - 1], n_recv.at[k - 1], (dp, q)))
        else:
            comb[1] = part
    dgain_one = dgain_one / gain_one

    sm_send[0] = jnp.concatenate(
        [grad_router, dgain_one, dgain_two, jnp.zeros((sm_send.shape[1] - s.experts - 2, s.width), F32)], 0
    )
    sm_copies = [go.to(sm_send.at[0], sm_z.at[k - 1], (dp, here.ring_t(k))) for k in range(1, nt)]

    grad_qkv = jnp.zeros((s.width, 3 * s.heads), F32)
    for q in range(nt):
        grad_qkv = grad_qkv + dot_tn(n1_ref[q], dqkv[q])
    gq_send[:, :, : 3 * s.heads] = grad_qkv.astype(BF).reshape(s.n_dp, s.shard, 3 * s.heads)
    total = go_send[t].astype(F32)
    for k, copy in enumerate(go_copies):
        copy.wait_recv()
        total = total + go_recv[k].astype(F32)
    gq_send[:, :, 3 * s.heads :] = total.astype(BF).reshape(s.n_dp, s.shard, s.heads)
    gq_copies = [go.to(gq_send.at[here.ring_dp(k)], gq_recv.at[k - 1], (here.ring_dp(k), t)) for k in range(1, s.n_dp)]
    pump(1)
    total = sm_send[0]
    for k, copy in enumerate(sm_copies):
        copy.wait_recv()
        total = total + sm_z[k]
    sm_send[1] = total
    smd_copies = [go.to(sm_send.at[1], sm_dp.at[k - 1], (here.ring_dp(k), t)) for k in range(1, s.n_dp)]

    dn1 = comb[1]
    for k, copy in enumerate(n_copies):
        copy.wait_recv()
        dn1 = dn1 + n_recv[k].astype(F32)
    result = gx_ref[...] + middle
    for k, copy in enumerate(m_copies):
        copy.wait_recv()
        result = result + m_recv[k].astype(F32)
    out_ref[...] = result.astype(BF)
    dx_ln, _ = norm_back(x_ref[...].astype(F32), gain_one, dn1)
    gx_ref[...] = comb[0] + dx_ln

    grad = gq_send[dp].astype(F32)
    for k, copy in enumerate(gq_copies):
        copy.wait_recv()
        grad = grad + gq_recv[k].astype(F32)
    gqo_ref[...] = grad

    mine = pl.ds(pl.multiple_of(c * s.shard, s.shard), s.shard)
    other = pl.ds(pl.multiple_of((1 - c) * s.shard, s.shard), s.shard)
    fin_copies = []
    for w, (first, mine_first, second, copies) in enumerate(((ra, y, fa, fa_copies), (rb, x, fb, fb_copies))):
        for j in range(2):
            copies[j].wait_recv()

            def last(i, carry, w=w, first=first, mine_first=mine_first, second=second, j=j):
                def total(rows):
                    return (
                        own[w, mine_first, j * per + i, rows, :].astype(F32)
                        + first[j, mine_first, i, rows, :].astype(F32)
                        + second[j, i, rows, :].astype(F32)
                    )

                fin[w, j, i] = total(other).astype(BF)
                gw_ref[w, c, j * per + i] = total(mine)
                return carry

            lax.fori_loop(0, per, last, 0)
            fin_copies.append(go.to(fin.at[w, j], fin_recv.at[w, j], here.sib))
    total = sm_send[1]
    for k, copy in enumerate(smd_copies):
        copy.wait_recv()
        total = total + sm_dp[k]
    gsm_ref[...] = total
    for w in range(2):
        for j in range(2):
            fin_copies[2 * w + j].wait_recv()

            def widen(i, carry, w=w, j=j):
                gw_ref[w, 1 - c, j * per + i] = fin_recv[w, j, i].astype(F32)
                return carry

            lax.fori_loop(0, per, widen, 0)
    go.finish()


VSPEC = pl.BlockSpec(memory_space=pltpu.VMEM)
ASPEC = pl.BlockSpec(memory_space=pl.ANY)


def shape(dims, kind):
    return jax.ShapeDtypeStruct(dims, kind)


def linked_body(
    block_input,
    gains,
    w_qkv,
    w_o,
    w_router,
    w_in,
    w_out,
    pictures_alive_per_shard,
    expert_ids,
    slot_index,
    cotangent,
):
    images, quarter, width = block_input.shape
    n_dp, n_t = lax.axis_size("dp"), lax.axis_size("tensor")
    shard, experts, ff = w_in.shape
    heads = w_qkv.shape[2]
    length = quarter * n_t
    used = images * quarter
    rows = up(used, 16)
    s = Sizes(n_dp, n_t, images, quarter, rows, up(length, 16), width, shard, heads, experts, ff, up(rows, 128))
    dp, t = lax.axis_index("dp"), lax.axis_index("tensor")

    def by_rows(values):
        return jnp.pad(values.reshape(used, width), ((0, rows - used), (0, 0)))

    x_own, dz_own = by_rows(block_input), by_rows(cotangent)
    wq = w_qkv.reshape(shard, 3 * heads)
    wo = w_o.T
    sm_rows = up(experts + 2, 16)
    small = jnp.zeros((sm_rows, width), BF)
    piece = jnp.concatenate([w_router.T, gains.T], 0)
    small = lax.dynamic_update_slice(small, piece, (0, dp * shard))
    win_t = w_in.transpose(1, 0, 2).reshape(2, s.half, shard, ff)
    wout_t = w_out.transpose(1, 2, 0).reshape(2, s.half, shard, ff)
    place = t * quarter + jnp.arange(quarter)
    live = (jnp.arange(images) < pictures_alive_per_shard[0])[:, None] & (place < TOK_IMG)[None, :]
    live = jnp.pad(live.astype(F32).reshape(used, 1), ((0, rows - used), (0, 0)))
    targets = jnp.where(slot_index >= 0, expert_ids * CAP + slot_index, -1)
    targets = targets.reshape(images, n_t, quarter, 2).transpose(1, 0, 2, 3).reshape(n_t, used, 2)
    targets = jnp.pad(targets, ((0, 0), (0, rows - used), (0, 0)), constant_values=-1)
    tgt_rows = jnp.pad(targets.reshape(n_t * rows, 2).T, ((0, 6), (0, 0)), constant_values=-1)

    params = dict(has_side_effects=True, vmem_limit_bytes=VMEM_BYTES)
    front_links = 2 + (n_t - 1) * 6 + (n_dp - 1) * 3 + 8 + 4 + (n_t - 1) * 3
    front = pl.pallas_call(
        lambda *refs: front_kernel(s, *refs),
        out_shape=(
            shape((s.half, n_dp, shard, ff), BF),
            shape((s.half, n_dp, shard, ff), BF),
            shape((2, n_t, rows, width), BF),
            shape((2, n_t, rows, width), BF),
            shape((2, n_t, experts, s.lanes), F32),
            shape((2, 8, n_t * rows), jnp.int32),
            shape((rows, width), F32),
            shape((rows, width), BF),
            shape((experts, s.lanes), F32),
            shape((images, s.irows, 3 * heads), BF),
            shape((images, heads // HEAD_DIM * s.irows, s.irows), BF),
            shape((n_t, rows, width), BF),
            shape((n_t, rows, heads), BF),
            shape((n_dp, shard, 3 * heads), BF),
            shape((n_dp, n_t, shard, heads), BF),
            shape((sm_rows, width), F32),
        ),
        in_specs=[VSPEC] * 5 + [ASPEC] * 2 + [VSPEC] * 2,
        out_specs=[ASPEC] * 6 + [VSPEC] * 10,
        scratch_shapes=[
            pltpu.VMEM((n_t, rows, width), BF),
            pltpu.VMEM((n_dp, sm_rows, width), BF),
            pltpu.VMEM((n_t, shard, heads), BF),
            pltpu.VMEM((n_t, rows, 3 * heads), F32),
            pltpu.VMEM((images, s.irows, 3 * heads), F32),
            pltpu.VMEM((images, s.irows, heads), F32),
            pltpu.VMEM((n_t, rows, heads), F32),
            pltpu.VMEM((n_t, rows, heads), BF),
            pltpu.SemaphoreType.DMA((front_links,)),
            pltpu.SemaphoreType.DMA((front_links,)),
            pltpu.SemaphoreType.DMA((10,)),
        ],
        compiler_params=pltpu.CompilerParams(collective_id=1, **params),
        name="front",
    )
    (
        win_all, wout_all, n2_all, dz_all, prob_all, tgt_all,
        y, n2, prob, qkv, p, n1, o, wq_all, wo_all, small_sum,
    ) = front(x_own, dz_own, wq, wo, small, win_t, wout_t, live, tgt_rows)

    tokens = n_t * rows
    two_y, two_x = n_dp // 4, 2
    whole = lambda *dims: pl.BlockSpec(dims, lambda e: (0,) * len(dims))
    experts_call = pl.pallas_call(
        lambda *refs: expert_kernel(s, *refs),
        grid=(s.half,),
        out_shape=(
            shape((2, s.slots, width), BF),
            shape((2, s.slots, width), BF),
            shape((two_y, two_x, s.half, 2 * shard, ff), BF),
            shape((two_y, two_x, s.half, 2 * shard, ff), BF),
            shape((2, n_t, s.half, s.lanes), F32),
        ),
        in_specs=[
            whole(2, tokens, width),
            whole(2, tokens, width),
            whole(2, 8, tokens),
            whole(2, n_t, experts, s.lanes),
            pl.BlockSpec((1, width, ff), lambda e: (e, 0, 0)),
            pl.BlockSpec((1, width, ff), lambda e: (e, 0, 0)),
        ],
        out_specs=[
            pl.BlockSpec((2, CAP, width), lambda e: (0, e, 0)),
            pl.BlockSpec((2, CAP, width), lambda e: (0, e, 0)),
            pl.BlockSpec((two_y, two_x, 1, 2 * shard, ff), lambda e: (0, 0, e, 0, 0)),
            pl.BlockSpec((two_y, two_x, 1, 2 * shard, ff), lambda e: (0, 0, e, 0, 0)),
            whole(2, n_t, s.half, s.lanes),
        ],
        scratch_shapes=[
            pltpu.VMEM((2, experts, tokens), F32),
            pltpu.VMEM((2, s.half, tokens), F32),
        ],
        compiler_params=pltpu.CompilerParams(vmem_limit_bytes=VMEM_BYTES),
        name="experts",
    )
    dx, ge, gi, go, dpr = experts_call(
        n2_all.reshape(2, tokens, width),
        dz_all.reshape(2, tokens, width),
        tgt_all,
        prob_all,
        win_all.reshape(s.half, width, ff),
        wout_all.reshape(s.half, width, ff),
    )

    per = s.half // 2
    gsm_rows = up(experts + 2, 8)
    back_links = 4 + 3 + (n_t - 1) * 7 + 4 + 4 + 2 * (n_dp - 1)
    out, gx, gw, gqo, gsm = pl.pallas_call(
        lambda *refs: back_kernel(s, *refs),
        out_shape=(
            shape((rows, width), BF),
            shape((rows, width), F32),
            shape((2, 2, s.half, shard, ff), F32),
            shape((shard, 4 * heads), F32),
            shape((gsm_rows, width), F32),
        ),
        in_specs=[VSPEC] * 14 + [ASPEC] * 5,
        out_specs=[VSPEC] * 5,
        scratch_shapes=[
            pltpu.VMEM((2, s.slots, width), BF),
            pltpu.VMEM((2, s.slots, width), BF),
            pltpu.VMEM((n_t, 2, s.half, s.lanes), F32),
            pltpu.VMEM((n_t - 1, 2, s.half, s.lanes), F32),
            pltpu.VMEM((n_t, rows, width), F32),
            pltpu.VMEM((n_t - 1, rows, width), BF),
            pltpu.VMEM((n_t - 1, rows, width), BF),
            pltpu.VMEM((n_t - 1, rows, width), BF),
            pltpu.VMEM((n_t - 1, rows, width), BF),
            pltpu.VMEM((n_t - 1, rows, width), BF),
            pltpu.VMEM((n_t - 1, rows, width), BF),
            pltpu.VMEM((rows, width), BF),
            pltpu.VMEM((n_t, rows, heads), BF),
            pltpu.VMEM((n_t, rows, heads), BF),
            pltpu.VMEM((n_t, rows, heads), F32),
            pltpu.VMEM((images, s.irows, heads), F32),
            pltpu.VMEM((images, s.irows, 3 * heads), F32),
            pltpu.VMEM((n_t, rows, 3 * heads), F32),
            pltpu.VMEM((n_t, rows, 3 * heads), BF),
            pltpu.VMEM((n_t, width, heads), BF),
            pltpu.VMEM((n_t - 1, width, heads), BF),
            pltpu.VMEM((n_dp, shard, 4 * heads), BF),
            pltpu.VMEM((n_dp - 1, shard, 4 * heads), BF),
            pltpu.VMEM((2, gsm_rows, width), F32),
            pltpu.VMEM((n_t - 1, gsm_rows, width), F32),
            pltpu.VMEM((n_dp - 1, gsm_rows, width), F32),
            pltpu.VMEM((2, 2, s.half, 2 * shard, ff), BF),
            pltpu.VMEM((2, 2, per, 2 * shard, ff), BF),
            pltpu.VMEM((2, 2, per, 2 * shard, ff), BF),
            pltpu.VMEM((2, per, 2 * shard, ff), BF),
            pltpu.VMEM((2, per, 2 * shard, ff), BF),
            pltpu.VMEM((2, per, 2 * shard, ff), BF),
            pltpu.VMEM((2, per, 2 * shard, ff), BF),
            pltpu.VMEM((2, 2, per, shard, ff), BF),
            pltpu.VMEM((2, 2, per, shard, ff), BF),
            pltpu.SemaphoreType.DMA((back_links,)),
            pltpu.SemaphoreType.DMA((back_links,)),
            pltpu.SemaphoreType.DMA((5,)),
        ],
        compiler_params=pltpu.CompilerParams(collective_id=2, **params),
        name="back",
    )(
        x_own, dz_own, y, n2, prob, live, targets, qkv, p, n1, o,
        wq_all, wo_all, small_sum, dpr, dx, ge, gi, go,
    )

    def by_image(values):
        return values[:used].reshape(images, quarter, width)

    gw = gw.reshape(2, experts, shard, ff)
    own_small = lax.dynamic_slice(gsm, (0, dp * shard), (gsm_rows, shard))
    return (
        by_image(out),
        by_image(gx),
        own_small[experts : experts + 2].T,
        gqo[:, : 3 * heads].reshape(shard, 3, heads),
        gqo[:, 3 * heads :].T,
        own_small[:experts].T,
        gw[0].transpose(1, 0, 2),
        gw[1].transpose(2, 0, 1),
    )


def solution(mesh):
    placed = (
        P("dp", "tensor", None),
        P("dp", None),
        P("dp", None, "tensor"),
        P("tensor", "dp"),
        P("dp", None),
        P("dp", None, "tensor"),
        P("tensor", None, "dp"),
        P("dp"),
        P("dp", None, None),
        P("dp", None, None),
        P("dp", "tensor", None),
    )
    linked = mesh.shape["dp"] == 8 and mesh.shape["tensor"] > 1
    return jax.shard_map(
        linked_body if linked else body,
        mesh=mesh,
        in_specs=placed,
        out_specs=(
            P("dp", "tensor", None),
            P("dp", "tensor", None),
            P("dp", None),
            P("dp", None, "tensor"),
            P("tensor", "dp"),
            P("dp", None),
            P("dp", None, "tensor"),
            P("tensor", None, "dp"),
        ),
        check_vma=False,
    )
```

```python
import math
from typing import NamedTuple

import jax
import jax.numpy as jnp
from jax import lax
from jax.experimental import pallas as pl
from jax.experimental.pallas import tpu as pltpu
from jax.sharding import PartitionSpec as P

HEAD_DIM = 64
TOK_IMG = 197
CAP = 192


epsilon = 1e-06
negative_fill = -1e30


def as_sent(shard):
    return jax.tree.map(lambda a: a.astype(jnp.bfloat16) if a.dtype == jnp.float32 else a, shard)


def layer_norm(values, gain):
    centre = values - jnp.mean(values, -1, keepdims=True)
    spread = jnp.mean(centre * centre, -1, keepdims=True)
    return centre * lax.rsqrt(spread + epsilon) * gain


def gelu_exact(values):
    return jax.nn.gelu(values, approximate=False)


def gate_values(logits, chosen):
    router_probs = jax.nn.softmax(logits, axis=-1)
    return jnp.einsum("re,rke->rk", router_probs, chosen)


def rows_in(values):
    return lax.all_gather(values, "tensor", axis=1, tiled=True)


def rows_out(values):
    return lax.psum_scatter(values, "tensor", scatter_dimension=1, tiled=True)


def grads_in(values):
    return jax.tree.map(
        lambda part, own: part.astype(own.dtype),
        lax.all_gather(as_sent(values), "tensor", axis=1, tiled=True),
        values,
    )


def grads_out(values):
    return lax.psum_scatter(values, "tensor", scatter_dimension=1, tiled=True)


def attention_scores(queries, keys_all, key_live, scale_factor):
    gating_logits_matrix = (
        jnp.einsum("ilhe,imhe->ihlm", queries, keys_all, preferred_element_type=jnp.float32)
        * scale_factor
    )
    return jnp.where(key_live[None, None, None, :], gating_logits_matrix, negative_fill)


def body(
    block_input,
    gains,
    w_qkv,
    w_o,
    w_router,
    w_in,
    w_out,
    pictures_alive_per_shard,
    expert_ids,
    slot_index,
    cotangent,
):
    tensor_size = lax.axis_size("tensor")
    tensor_pos = lax.axis_index("tensor")
    images, quarter, model_width = block_input.shape
    length = quarter * tensor_size
    all_rows = images * length
    own_rows = images * quarter
    start_row = tensor_pos * quarter
    experts = w_in.shape[1]
    slot_count = experts * CAP
    key_live = jnp.arange(length) < TOK_IMG
    live_all = (
        (jnp.arange(images) < pictures_alive_per_shard[0])[:, None] & key_live[None, :]
    ).astype(jnp.float32)
    live_own = lax.dynamic_slice_in_dim(live_all, start_row, quarter, 1)
    gathered = (
        lax.all_gather(gains, "dp", axis=0, tiled=True),
        lax.all_gather(w_qkv, "dp", axis=0, tiled=True),
        lax.all_gather(w_o, "dp", axis=1, tiled=True),
        lax.all_gather(w_router, "dp", axis=0, tiled=True),
        lax.all_gather(w_in, "dp", axis=0, tiled=True),
        lax.all_gather(w_out, "dp", axis=2, tiled=True),
    )
    gain_all, qkv_all, outproj_all, router_all, expin_all, expout_all = gathered
    head_cols = qkv_all.shape[2]
    local_heads = head_cols // HEAD_DIM
    scale_factor = 1.0 / math.sqrt(HEAD_DIM)
    gain_one = gain_all[:, 0].astype(jnp.float32)
    gain_two = gain_all[:, 1].astype(jnp.float32)
    x_float = block_input.astype(jnp.float32)
    normed = layer_norm(x_float, gain_one).astype(jnp.bfloat16)
    normed_all = rows_in(normed).reshape(all_rows, model_width)
    project = jnp.einsum(
        "rd,djc->rjc", normed_all, qkv_all, preferred_element_type=jnp.float32
    ).astype(jnp.bfloat16)
    queries = project[:, 0].reshape(images, length, local_heads, HEAD_DIM)
    keys_all = project[:, 1].reshape(images, length, local_heads, HEAD_DIM)
    values_all = project[:, 2].reshape(images, length, local_heads, HEAD_DIM)
    masked = attention_scores(queries, keys_all, key_live, scale_factor)
    top_score = jnp.max(masked, -1, keepdims=True)
    expd = jnp.exp(masked - top_score)
    total = jnp.sum(expd, -1, keepdims=True)
    att_probs = expd / total
    log_total = top_score + jnp.log(total)
    attended = jnp.einsum(
        "ihlm,imhe->ilhe",
        att_probs.astype(jnp.bfloat16),
        values_all,
        preferred_element_type=jnp.float32,
    )
    attended = attended.astype(jnp.bfloat16).reshape(all_rows, head_cols)
    branch_part = jnp.dot(attended, outproj_all, preferred_element_type=jnp.float32).reshape(
        images, length, model_width
    )
    middle = x_float + live_own[:, :, None] * rows_out(branch_part)
    normed_two = layer_norm(middle, gain_two).astype(jnp.bfloat16)
    normed_two_all = rows_in(normed_two).reshape(all_rows, model_width)
    own_flat = normed_two.reshape(own_rows, model_width)
    expert_range = jnp.arange(experts)
    own_ids = lax.dynamic_slice_in_dim(expert_ids, start_row, quarter, 1).reshape(own_rows, 2)
    chosen = (own_ids[:, :, None] == expert_range[None, None, :]).astype(jnp.float32)
    targets = jnp.where(slot_index >= 0, expert_ids * CAP + slot_index, -1).reshape(all_rows, 2)
    slot_ids = jnp.arange(slot_count)
    first_hot = (targets[:, 0:1] == slot_ids[None, :]).astype(jnp.bfloat16)
    second_hot = (targets[:, 1:2] == slot_ids[None, :]).astype(jnp.bfloat16)
    dispatched = jnp.einsum(
        "rs,rd->sd", first_hot, normed_two_all, preferred_element_type=jnp.float32
    )
    dispatched = dispatched + jnp.einsum(
        "rs,rd->sd", second_hot, normed_two_all, preferred_element_type=jnp.float32
    )
    dispatched = dispatched.astype(jnp.bfloat16).reshape(experts, CAP, model_width)
    hidden = jnp.einsum("ecd,def->ecf", dispatched, expin_all, preferred_element_type=jnp.float32)
    active = gelu_exact(hidden).astype(jnp.bfloat16)
    expert_part = jnp.einsum("ecf,fed->ecd", active, expout_all, preferred_element_type=jnp.float32)
    expert_part = expert_part.astype(jnp.bfloat16).reshape(slot_count, model_width)
    first_rows = jnp.dot(first_hot, expert_part, preferred_element_type=jnp.float32)
    second_rows = jnp.dot(second_hot, expert_part, preferred_element_type=jnp.float32)
    logits = jnp.dot(own_flat, router_all, preferred_element_type=jnp.float32)
    gates = gate_values(logits, chosen)
    first_own, second_own = rows_out(
        (
            first_rows.reshape(images, length, model_width),
            second_rows.reshape(images, length, model_width),
        )
    )
    gate_grid = gates.reshape(images, quarter, 2)
    output = middle + gate_grid[:, :, 0:1] * first_own + gate_grid[:, :, 1:2] * second_own
    grad_output = cotangent.astype(jnp.float32)
    grad_first = (gate_grid[:, :, 0:1] * grad_output).astype(jnp.bfloat16)
    grad_second = (gate_grid[:, :, 1:2] * grad_output).astype(jnp.bfloat16)
    grad_gates = jnp.stack(
        [jnp.sum(grad_output * first_own, -1), jnp.sum(grad_output * second_own, -1)], -1
    ).reshape(own_rows, 2)
    leading_cotangent, second_back = grads_in((grad_first, grad_second))
    leading_cotangent = leading_cotangent.reshape(all_rows, model_width)
    second_back = second_back.reshape(all_rows, model_width)
    unused_gates, gate_pull = jax.vjp(lambda values: gate_values(values, chosen), logits)
    grad_logits = gate_pull(grad_gates)[0].astype(jnp.bfloat16)
    grad_router = jnp.einsum("rd,re->de", own_flat, grad_logits, preferred_element_type=jnp.float32)
    router_back = jnp.einsum(
        "re,de->rd", grad_logits, router_all, preferred_element_type=jnp.float32
    )
    grad_expert = jnp.einsum(
        "rs,rd->sd", first_hot, leading_cotangent, preferred_element_type=jnp.float32
    )
    grad_expert = grad_expert + jnp.einsum(
        "rs,rd->sd", second_hot, second_back, preferred_element_type=jnp.float32
    )
    grad_expert = grad_expert.astype(jnp.bfloat16).reshape(experts, CAP, model_width)
    grad_active = jnp.einsum(
        "ecd,fed->ecf", grad_expert, expout_all, preferred_element_type=jnp.float32
    )
    grad_expout = jnp.einsum(
        "ecf,ecd->fed", active, grad_expert, preferred_element_type=jnp.float32
    )
    unused_gelu, gelu_pull = jax.vjp(gelu_exact, hidden)
    grad_hidden = gelu_pull(grad_active)[0].astype(jnp.bfloat16)
    grad_expin = jnp.einsum(
        "ecd,ecf->def", dispatched, grad_hidden, preferred_element_type=jnp.float32
    )
    grad_dispatch = jnp.einsum(
        "ecf,def->ecd", grad_hidden, expin_all, preferred_element_type=jnp.float32
    )
    grad_dispatch = grad_dispatch.astype(jnp.bfloat16).reshape(slot_count, model_width)
    back_rows = jnp.dot(first_hot, grad_dispatch, preferred_element_type=jnp.float32)
    back_rows = back_rows + jnp.dot(second_hot, grad_dispatch, preferred_element_type=jnp.float32)
    grad_normed_two = grads_out(
        back_rows.reshape(images, length, model_width)
    ) + router_back.reshape(images, quarter, model_width)
    unused_two, norm_two_pull = jax.vjp(layer_norm, middle, gain_two)
    grad_middle_norm, grad_gain_two = norm_two_pull(grad_normed_two)
    grad_middle = grad_output + grad_middle_norm
    grad_branch = (live_own[:, :, None] * grad_middle).astype(jnp.bfloat16)
    grad_branch_all = grads_in(grad_branch).reshape(all_rows, model_width)
    grad_outproj = jnp.einsum(
        "rc,rd->cd", attended, grad_branch_all, preferred_element_type=jnp.float32
    )
    grad_attended = jnp.einsum(
        "rd,cd->rc", grad_branch_all, outproj_all, preferred_element_type=jnp.float32
    )
    grad_attended = grad_attended.astype(jnp.bfloat16).reshape(
        images, length, local_heads, HEAD_DIM
    )
    masked_again = attention_scores(queries, keys_all, key_live, scale_factor)
    probs_again = jnp.exp(masked_again - log_total)
    grad_values = jnp.einsum(
        "ihlm,ilhe->imhe",
        probs_again.astype(jnp.bfloat16),
        grad_attended,
        preferred_element_type=jnp.float32,
    )
    grad_values = grad_values.astype(jnp.bfloat16)
    grad_probs = jnp.einsum(
        "ilhe,imhe->ihlm", grad_attended, values_all, preferred_element_type=jnp.float32
    )
    grad_scores = probs_again * (grad_probs - jnp.sum(probs_again * grad_probs, -1, keepdims=True))
    grad_scores = grad_scores.astype(jnp.bfloat16)
    grad_queries = (
        jnp.einsum("ihlm,imhe->ilhe", grad_scores, keys_all, preferred_element_type=jnp.float32)
        * scale_factor
    ).astype(jnp.bfloat16)
    grad_keys = (
        jnp.einsum("ihlm,ilhe->imhe", grad_scores, queries, preferred_element_type=jnp.float32)
        * scale_factor
    ).astype(jnp.bfloat16)
    grad_project = jnp.stack([grad_queries, grad_keys, grad_values], 2).reshape(
        all_rows, 3, head_cols
    )
    grad_qkv = jnp.einsum(
        "rd,rjc->djc", normed_all, grad_project, preferred_element_type=jnp.float32
    )
    normed_back = jnp.einsum(
        "rjc,djc->rd", grad_project, qkv_all, preferred_element_type=jnp.float32
    )
    grad_normed = grads_out(normed_back.reshape(images, length, model_width))
    unused_one, norm_one_pull = jax.vjp(layer_norm, x_float, gain_one)
    grad_x_norm, grad_gain_one = norm_one_pull(grad_normed)
    grad_input = grad_middle + grad_x_norm
    router_sum, gain_sum = lax.psum(
        (grad_router, jnp.stack([grad_gain_one, grad_gain_two], 1)), "tensor"
    )
    expert_fractions = (
        lax.psum_scatter(gain_sum, "dp", scatter_dimension=0, tiled=True),
        lax.psum_scatter(grad_qkv, "dp", scatter_dimension=0, tiled=True),
        lax.psum_scatter(grad_outproj, "dp", scatter_dimension=1, tiled=True),
        lax.psum_scatter(router_sum, "dp", scatter_dimension=0, tiled=True),
        lax.psum_scatter(grad_expin, "dp", scatter_dimension=0, tiled=True),
        lax.psum_scatter(grad_expout, "dp", scatter_dimension=2, tiled=True),
    )
    return (
        output.astype(jnp.bfloat16),
        grad_input,
        expert_fractions[0],
        expert_fractions[1],
        expert_fractions[2],
        expert_fractions[3],
        expert_fractions[4],
        expert_fractions[5],
    )


MESH = pl.DeviceIdType.MESH
BF = jnp.bfloat16
F32 = jnp.float32
VMEM_BYTES = 60 << 20


class Sizes(NamedTuple):
    n_dp: int
    n_t: int
    images: int
    quarter: int
    rows: int
    irows: int
    width: int
    shard: int
    heads: int
    experts: int
    ff: int
    lanes: int

    @property
    def half(self):
        return self.experts // 2

    @property
    def slots(self):
        return self.half * CAP


def up(value, step):
    return -(-value // step) * step


def norm_parts(values):
    centre = values - jnp.mean(values, -1, keepdims=True)
    scale = lax.rsqrt(jnp.mean(centre * centre, -1, keepdims=True) + epsilon)
    return centre * scale, scale


def norm_back(values, gain, grad):
    unit, scale = norm_parts(values)
    inner = grad * gain
    mean_a = jnp.mean(inner, -1, keepdims=True)
    mean_b = jnp.mean(inner * unit, -1, keepdims=True)
    return scale * (inner - mean_a - unit * mean_b), unit


def dot(a, b):
    return jnp.dot(a, b, preferred_element_type=F32)


def dot_nt(a, b):
    return lax.dot_general(a, b, (((1,), (1,)), ((), ())), preferred_element_type=F32)


def dot_tn(a, b):
    return lax.dot_general(a, b, (((0,), (0,)), ((), ())), preferred_element_type=F32)


class Place:
    def __init__(self, s):
        self.s = s
        self.dp = lax.axis_index("dp")
        self.t = lax.axis_index("tensor")
        self.c = lax.rem(self.dp, 2)
        self.x = lax.rem(self.dp // 2, 2)
        self.y = self.dp // 4
        self.chip = self.dp // 2
        self.chip_x = self.y * 2 + (1 - self.x)
        self.chip_y = (1 - self.y) * 2 + self.x
        self.sib = (self.chip * 2 + (1 - self.c), self.t)
        self.nx_other = (self.chip_x * 2 + (1 - self.c), self.t)
        self.ny_other = (self.chip_y * 2 + (1 - self.c), self.t)
        self.pair = lax.rem(self.t, 2) * (-2) + self.t + 1
        self.far = lax.rem(self.t + 2, 4)
        self.cross = lax.rem(self.pair + 2, 4)
        self.nx = (self.chip_x * 2 + self.c, self.t)
        self.ny = (self.chip_y * 2 + self.c, self.t)

    def ring_dp(self, k):
        return lax.rem(self.dp + k, self.s.n_dp)

    def ring_t(self, k):
        return lax.rem(self.t + k, self.s.n_t)

    def from_t(self, k):
        return lax.rem(self.t + self.s.n_t - k, self.s.n_t)

    def greet(self):
        barrier = pltpu.get_barrier_semaphore()
        for k in range(1, self.s.n_dp):
            pl.semaphore_signal(barrier, inc=1, device_id=(self.ring_dp(k), self.t), device_id_type=MESH)
        for k in range(1, self.s.n_t):
            pl.semaphore_signal(barrier, inc=1, device_id=(self.dp, self.ring_t(k)), device_id_type=MESH)
        pl.semaphore_wait(barrier, self.s.n_dp + self.s.n_t - 2)


class Copies:
    def __init__(self, send, recv, local):
        self.send, self.recv, self.local = send, recv, local
        self.n = 0
        self.m = 0
        self.sent = []

    def to(self, src, dst, device):
        copy = pltpu.make_async_remote_copy(
            src_ref=src,
            dst_ref=dst,
            send_sem=self.send.at[self.n],
            recv_sem=self.recv.at[self.n],
            device_id=device,
            device_id_type=MESH,
        )
        self.n += 1
        copy.start()
        self.sent.append(copy)
        return copy

    def here(self, src, dst):
        copy = pltpu.make_async_copy(src, dst, self.local.at[self.m])
        self.m += 1
        copy.start()
        return copy

    def finish(self):
        for copy in self.sent:
            copy.wait_send()


def pieces_of(rows):
    first = up(rows // 2, 16)
    return [pl.ds(0, first), pl.ds(first, rows - first)]


class Gather:
    def __init__(self, go, here, own, full):
        self.go, self.here, self.full = go, here, full
        self.pieces = pieces_of(here.s.rows)
        mine = full(here.t)
        self.to_far = [go.to(own.at[p], mine.at[p], (here.dp, here.far)) for p in self.pieces]
        self.to_pair = [go.to(own.at[p], mine.at[p], (here.dp, here.pair)) for p in self.pieces]

    def relay(self):
        block = self.full(self.here.far)
        self.passed = []
        for p, copy in zip(self.pieces, self.to_far):
            copy.wait_recv()
            self.passed.append(self.go.to(block.at[p], block.at[p], (self.here.dp, self.here.pair)))

    def wait_pair(self):
        for copy in self.to_pair:
            copy.wait_recv()

    def wait_cross(self):
        for copy in self.passed:
            copy.wait_recv()

    def share(self, block):
        return self.go.to(self.full(block), self.full(block), self.here.sib)


class Reduce:
    def __init__(self, go, here, send, recv):
        self.go, self.here, self.send, self.recv = go, here, send, recv
        self.pieces = pieces_of(here.s.rows)
        self.copies = [[], [], []]

    def put(self, k, p, device):
        self.copies[k].append(self.go.to(self.send.at[k, p], self.recv.at[k, p], (self.here.dp, device)))

    def pair(self, k, value):
        self.send[k] = value.astype(BF)
        for p in self.pieces:
            self.put(k, p, self.here.pair)

    def across(self, part):
        for i, p in enumerate(self.pieces):
            self.copies[0][i].wait_recv()
            self.send[2, p] = (part[p] + self.recv[0, p].astype(F32)).astype(BF)
            self.put(2, p, self.here.far)

    def total(self, part):
        for copy in self.copies[1] + self.copies[2]:
            copy.wait_recv()
        return part + self.recv[1].astype(F32) + self.recv[2].astype(F32)


def head_masks(s):
    lane = lax.broadcasted_iota(jnp.int32, (s.irows, s.heads), 1)
    return [(lane // HEAD_DIM) == h for h in range(s.heads // HEAD_DIM)]


def stack_heads(values, masks):
    zero = jnp.zeros_like(values)
    return jnp.concatenate([jnp.where(mask, values, zero) for mask in masks], 0)


def pick_heads(stacked, masks, irows):
    out = stacked[:irows]
    for h in range(1, len(masks)):
        out = jnp.where(masks[h], stacked[h * irows : (h + 1) * irows], out)
    return out


def front_kernel(
    s,
    x_ref, dz_ref, wq_ref, wo_ref, sm_ref, win_ref, wout_ref, live_ref, tgt_ref,
    win_all, wout_all, n2_all, dz_all, prob_all, tgt_all,
    y_ref, n2_ref, prob_ref, qkv_ref, p_ref, n1_ref, o_ref, wq_all, wo_all, small_ref,
    x_all, sm_all, wo_z, blk, img, oimg, oblk, o_send, send, recv, local,
):
    here = Place(s)
    dp, t, c = here.dp, here.t, here.c
    here.greet()
    go = Copies(send, recv, local)
    nt = s.n_t

    wo_copies = [go.to(wo_ref, wo_z.at[t], (dp, here.ring_t(k))) for k in range(1, nt)]
    x_all_blocks = Gather(go, here, x_ref, lambda block: x_all.at[block])
    sm_copies = [go.to(sm_ref, sm_all.at[dp], (here.ring_dp(k), t)) for k in range(1, s.n_dp)]
    wq_copies = [go.to(wq_ref, wq_all.at[dp], (here.ring_dp(k), t)) for k in range(1, s.n_dp)]

    def spread(shard, full):
        to = full.at[:, dp]
        half, rest = shard.at[c], shard.at[1 - c]
        from_x = [go.to(half, to, here.nx), go.to(rest, to, here.nx_other)]
        from_y = [go.to(half, to, here.ny), go.to(rest, to, here.ny_other)]
        return from_x, from_y, go.to(rest, to, here.sib), go.here(half, to)

    in_x, in_y, in_sib, keep_in = spread(win_ref, win_all)
    keep_sm = go.here(sm_ref, sm_all.at[dp])
    keep_wq = go.here(wq_ref, wq_all.at[dp])
    keep_wo = go.here(wo_ref, wo_z.at[t])
    tgt_copy = go.to(tgt_ref, tgt_all.at[c], here.sib)
    keep_tgt = go.here(tgt_ref, tgt_all.at[c])
    dz_sib = go.to(dz_ref, dz_all.at[c, t], here.sib)
    keep_dz = go.here(dz_ref, dz_all.at[c, t])

    keep_sm.wait()
    for copy in sm_copies:
        copy.wait_recv()
    small = jnp.sum(sm_all[...].astype(F32), 0)
    small_ref[...] = small
    gain_one = small[s.experts : s.experts + 1]
    gain_two = small[s.experts + 1 : s.experts + 2]
    keep_wq.wait()
    for copy in wq_copies:
        copy.wait_recv()

    keep_wo.wait()
    for copy in wo_copies:
        copy.wait_recv()
    keep_wo_all = go.here(wo_z, wo_all.at[dp])
    wo_out = [go.to(wo_z, wo_all.at[dp], (here.ring_dp(k), t)) for k in range(1, s.n_dp)]

    def project(slot, values):
        unit, _ = norm_parts(values.astype(F32))
        normed = (unit * gain_one).astype(BF)
        n1_ref[slot] = normed
        weights = wq_all[...].reshape(s.width, 3 * s.heads)
        blk[slot] = dot(normed, weights)

    project(t, x_ref[...])
    x_all_blocks.relay()
    out_x, out_y, out_sib, keep_out = spread(wout_ref, wout_all)
    project(here.far, x_all[here.far])
    x_all_blocks.wait_pair()
    project(here.pair, x_all[here.pair])
    x_all_blocks.wait_cross()
    project(here.cross, x_all[here.cross])
    dz_blocks = Gather(go, here, dz_ref, lambda block: dz_all.at[c, block])

    from_x = pl.ds(2 * here.chip_x, 2)
    from_y = pl.ds(2 * here.chip_y, 2)
    low_half, high_half = pl.ds(0, s.half // 2), pl.ds(s.half // 2, s.half // 2)

    def pass_on(full, by_x, by_y):
        for copy in by_x:
            copy.wait_recv()
        on_y = go.to(full.at[low_half, from_x], full.at[low_half, from_x], here.ny)
        for copy in by_y:
            copy.wait_recv()
        return on_y, go.to(full.at[high_half, from_y], full.at[high_half, from_y], here.nx)

    in_on_y, in_on_x = pass_on(win_all, in_x, in_y)
    length = s.quarter * nt
    img[:, pl.ds(length, s.irows - length), :] = jnp.zeros((s.images, s.irows - length, 3 * s.heads), F32)
    for i in range(s.images):
        for q in range(nt):
            img[i, pl.ds(q * s.quarter, s.quarter), :] = blk[q, pl.ds(i * s.quarter, s.quarter), :]

    masks = head_masks(s)

    def attend(i, carry):
        block = img[i].astype(BF)
        qkv_ref[i] = block
        queries = stack_heads(block[:, : s.heads], masks)
        scores = dot_nt(queries, block[:, s.heads : 2 * s.heads]) * (1.0 / math.sqrt(HEAD_DIM))
        key = lax.broadcasted_iota(jnp.int32, scores.shape, 1)
        scores = jnp.where(key < TOK_IMG, scores, negative_fill)
        expd = jnp.exp(scores - jnp.max(scores, -1, keepdims=True))
        probs = (expd / jnp.sum(expd, -1, keepdims=True)).astype(BF)
        p_ref[i] = probs
        oimg[i] = pick_heads(dot(probs, block[:, 2 * s.heads :]), masks, s.irows)
        return carry

    lax.fori_loop(0, s.images, attend, 0)
    used = s.images * s.quarter
    for q in range(nt):
        oblk[q, pl.ds(used, s.rows - used), :] = jnp.zeros((s.rows - used, s.heads), F32)
        for i in range(s.images):
            oblk[q, pl.ds(i * s.quarter, s.quarter), :] = oimg[i, pl.ds(q * s.quarter, s.quarter), :]
        o_send[q] = oblk[q].astype(BF)
    o_copies = [go.to(o_send.at[here.ring_t(k)], o_ref.at[t], (dp, here.ring_t(k))) for k in range(1, nt)]
    o_ref[t] = o_send[t]

    dz_blocks.relay()
    keep_wo_all.wait()
    for copy in wo_out:
        copy.wait_recv()
    for copy in o_copies:
        copy.wait_recv()
    branch = jnp.zeros((s.rows, s.width), F32)
    for q in range(nt):
        branch = branch + dot_nt(o_ref[q], wo_all[:, q].reshape(s.width, s.heads))
    middle = x_ref[...].astype(F32) + live_ref[...] * branch
    y_ref[...] = middle
    unit, _ = norm_parts(middle)
    normed_two = (unit * gain_two).astype(BF)
    n2_ref[...] = normed_two
    n2_sib = go.to(n2_ref, n2_all.at[c, t], here.sib)
    n2_blocks = Gather(go, here, n2_ref, lambda block: n2_all.at[c, block])
    keep_n2 = go.here(n2_ref, n2_all.at[c, t])
    logits = dot_nt(small[: s.experts].astype(BF), normed_two)
    expd = jnp.exp(logits - jnp.max(logits, 0, keepdims=True))
    prob_ref[...] = jnp.zeros((s.experts, s.lanes), F32)
    prob_ref[:, : s.rows] = expd / jnp.sum(expd, 0, keepdims=True)
    pr_sib = go.to(prob_ref, prob_all.at[c, t], here.sib)
    pr_copies = [go.to(prob_ref, prob_all.at[c, t], (dp, here.ring_t(k))) for k in range(1, nt)]
    keep_pr = go.here(prob_ref, prob_all.at[c, t])

    n2_blocks.relay()
    on = [n2_blocks.share(here.far), dz_blocks.share(here.far)]
    dz_blocks.wait_pair()
    on.append(dz_blocks.share(here.pair))
    dz_blocks.wait_cross()
    on.append(dz_blocks.share(here.cross))
    out_on_y, out_on_x = pass_on(wout_all, out_x, out_y)
    n2_blocks.wait_pair()
    on.append(n2_blocks.share(here.pair))
    for k, copy in enumerate(pr_copies, 1):
        copy.wait_recv()
        on.append(go.to(prob_all.at[c, here.from_t(k)], prob_all.at[c, here.from_t(k)], here.sib))
    n2_blocks.wait_cross()
    on.append(n2_blocks.share(here.cross))
    for copy in (keep_tgt, keep_dz, keep_n2, keep_pr, keep_in, keep_out):
        copy.wait()
    for copy in [tgt_copy, dz_sib, n2_sib, pr_sib, in_sib, out_sib, in_on_y, in_on_x, out_on_y, out_on_x] + on:
        copy.wait_recv()
    go.finish()


def expert_kernel(
    s,
    n2_ref, dz_ref, tgt_ref, prob_ref, win_ref, wout_ref,
    dx_ref, ge_ref, gi_ref, go_ref, dpr_ref,
    pr, dpr,
):
    e = pl.program_id(0)
    core = lax.rem(lax.axis_index("dp"), 2)
    expert = core * s.half + e

    @pl.when(e == 0)
    def _():
        for q in range(2):
            pr[q] = jnp.concatenate([prob_ref[q, k][:, : s.rows] for k in range(s.n_t)], 1)

    ids = expert * CAP + lax.broadcasted_iota(jnp.int32, (CAP, s.n_t * s.rows), 0)
    hits, xs, zs, gates = [], [], [], []
    for q in range(2):
        hit = (tgt_ref[q, 0:1, :] == ids) | (tgt_ref[q, 1:2, :] == ids)
        hot = jnp.where(hit, 1.0, 0.0).astype(BF)
        hits.append(hit)
        xs.append(dot(hot, n2_ref[q]).astype(BF))
        zs.append(dot(hot, dz_ref[q]))
        row = pr[q, pl.ds(expert, 1), :]
        gates.append(jnp.sum(jnp.where(hit, row, 0.0), 1, keepdims=True))
    x_in = jnp.concatenate(xs, 0)
    z_in = jnp.concatenate(zs, 0)
    gate = jnp.concatenate(gates, 0)
    w_in, w_out = win_ref[0], wout_ref[0]
    hidden = dot(x_in, w_in)
    size = jnp.abs(hidden)
    bell = jnp.exp(-0.5 * hidden * hidden)
    u = 1.0 / (1.0 + (0.3275911 / math.sqrt(2.0)) * size)
    poly = u * (0.254829592 + u * (-0.284496736 + u * (1.421413741 + u * (-1.453152027 + u * 1.061405429))))
    tail = 0.5 * poly * bell
    phi = jnp.where(hidden >= 0, 1.0 - tail, tail)
    active = (hidden * phi).astype(BF)
    slope = phi + hidden * bell * (1.0 / math.sqrt(2.0 * math.pi))
    out = dot_nt(active, w_out).astype(BF).astype(F32)
    dgate = jnp.sum(z_in * out, 1, keepdims=True)
    grad = (gate * z_in).astype(BF)
    go_ref[...] = dot_tn(grad, active).astype(BF).reshape(go_ref.shape)
    dhidden = (dot(grad, w_out) * slope).astype(BF)
    gi_ref[...] = dot_tn(x_in, dhidden).astype(BF).reshape(gi_ref.shape)
    dx_ref[...] = dot_nt(dhidden, w_in).astype(BF).reshape(dx_ref.shape)
    ge_ref[...] = (gate * out).astype(BF).reshape(ge_ref.shape)
    for q in range(2):
        row = jnp.sum(jnp.where(hits[q], dgate[q * CAP : (q + 1) * CAP], 0.0), 0, keepdims=True)
        dpr[q, pl.ds(e, 1), :] = row

    @pl.when(e == s.half - 1)
    def _():
        dpr_ref[...] = jnp.zeros(dpr_ref.shape, F32)
        for q in range(2):
            for k in range(s.n_t):
                dpr_ref[q, k, :, : s.rows] = dpr[q][:, k * s.rows : (k + 1) * s.rows]


def back_kernel(
    s,
    x_ref, dz_ref, y_ref, n2_ref, prob_ref, live_ref, tcol_ref, qkv_ref, p_ref, n1_ref, o_ref,
    wq_ref, wo_ref, small_ref, dpr_ref, dx_ref, ge_ref, gi_ref, go_ref,
    out_ref, gx_ref, gw_ref, gqo_ref, gsm_ref,
    dxv, gev, dprf, dprz, comb, rs_send, rs_recv, m_send, m_recv, m_far, n_send, n_recv,
    da_s, do_send, do_recv, doblk, doimg, dimg, dblk, dqkv, grads, gs_send, gs_recv, gx_send, gx_recv,
    gy_send, gy_recv, gz_send, gz_recv, sm_send, sm_recv, own, ra, rb, sa, sb, fa, fb, fin, fin_recv,
    send, recv, local,
):
    here = Place(s)
    dp, t, c = here.dp, here.t, here.c
    x, y = here.x, here.y
    here.greet()
    go = Copies(send, recv, local)
    nt = s.n_t
    per = s.half // 2

    ra_copies, rb_copies = [], []
    for j in range(2):
        piece = pl.ds(j * per, per)
        ra_copies.append(go.to(gi_ref.at[:, 1 - x, piece], ra.at[j], here.nx))
        rb_copies.append(go.to(go_ref.at[1 - y, :, piece], rb.at[j], here.ny))
    dx_sib = go.to(dx_ref.at[1 - c], dxv.at[c], here.sib)
    dpr_sib = go.to(dpr_ref.at[1 - c], dprf.at[:, c], here.sib)
    ge_sib = go.to(ge_ref.at[1 - c], gev.at[c], here.sib)
    keep_dx = go.here(dx_ref.at[c], dxv.at[c])
    keep_dpr = go.here(dpr_ref.at[c], dprf.at[:, c])
    keep_ge = go.here(ge_ref.at[c], gev.at[c])
    own_a = go.here(gi_ref.at[:, x], own.at[0])
    own_b = go.here(go_ref.at[y], own.at[1])

    chunk = s.slots // 2

    def combine(values, half, q, total):
        first = tcol_ref[q, :, 0:1]
        second = tcol_ref[q, :, 1:2]
        for j in range(2):
            ids = half * s.slots + j * chunk + lax.broadcasted_iota(jnp.int32, (s.rows, chunk), 1)
            hot = jnp.where((first == ids) | (second == ids), 1.0, 0.0).astype(BF)
            total = total + dot(hot, values[half, pl.ds(j * chunk, chunk), :])
        return total

    zero_rows = jnp.zeros((s.rows, s.width), F32)
    keep_dx.wait()
    order = (here.cross, here.pair, here.far, t)
    for k, q in enumerate(order):
        comb[k] = combine(dxv, c, q, zero_rows)
    dx_sib.wait_recv()
    dn2_sum = Reduce(go, here, rs_send, rs_recv)
    for k in range(2):
        dn2_sum.pair(k, combine(dxv, 1 - c, order[k], comb[k]))
    keep_dpr.wait()
    dpr_sib.wait_recv()
    dpr_copies = [go.to(dprf.at[here.ring_t(k)], dprz.at[k - 1], (dp, here.ring_t(k))) for k in range(1, nt)]
    dn2_sum.across(combine(dxv, 1 - c, here.far, comb[2]))
    comb[0] = combine(dxv, 1 - c, t, comb[3])

    keep_ge.wait()
    ge_sib.wait_recv()

    def forward_sum(q):
        return combine(gev, 1 - c, q, combine(gev, c, q, zero_rows))

    m_send[0] = forward_sum(here.cross).astype(BF)
    m_send[1] = forward_sum(here.pair).astype(BF)
    m_far[...] = forward_sum(here.far)
    gx_ref[...] = forward_sum(t)
    dprobs = dprf[t]
    for k, copy in enumerate(dpr_copies):
        copy.wait_recv()
        dprobs = dprobs + dprz[k]
    dprobs = dprobs.reshape(s.experts, s.lanes)
    probs = prob_ref[...]
    dlogits = (probs * (dprobs - jnp.sum(probs * dprobs, 0, keepdims=True))).astype(BF)[:, : s.rows]
    small = small_ref[...]
    gain_one = small[s.experts : s.experts + 1]
    gain_two = small[s.experts + 1 : s.experts + 2]
    grad_router = dot_tn(n2_ref[...], dlogits.T).T
    dn2 = comb[0] + dot_tn(dlogits, small[: s.experts].astype(BF))
    dn2 = dn2_sum.total(dn2)
    middle = y_ref[...]
    dy_ln, unit = norm_back(middle, gain_two, dn2)
    dgain_two = jnp.sum(dn2 * unit, 0, keepdims=True)
    dy = dz_ref[...].astype(F32) + dy_ln
    comb[0] = dy
    da = (live_ref[...] * dy).astype(BF)
    da_s[...] = da
    for q in range(nt):
        do_send[q] = dot(da, wo_ref[:, q].reshape(s.width, s.heads)).astype(BF)
    do_copies = [go.to(do_send.at[here.ring_t(k)], do_recv.at[t], (dp, here.ring_t(k))) for k in range(1, nt)]
    do_recv[t] = do_send[t]
    for q in range(nt):
        part = dot_tn(da, o_ref[q]).reshape(*grads.shape[:3], s.shard, s.heads)
        grads[:, :, :, :, (3 + q) * s.heads : (4 + q) * s.heads] = part
    own_a.wait()
    own_b.wait()

    def add_up(a, b, out):
        def step(i, carry):
            out[i] = (a[i].astype(F32) + b[i].astype(F32)).astype(out.dtype)
            return carry

        lax.fori_loop(0, out.shape[0], step, 0)

    fa_copies, fb_copies = [], []

    def pump(j):
        piece = pl.ds(j * per, per)
        ra_copies[j].wait_recv()
        add_up(own.at[0, 1 - y, piece], ra.at[j, 1 - y], sa.at[j])
        fa_copies.append(go.to(sa.at[j], fa.at[j], here.ny))
        rb_copies[j].wait_recv()
        add_up(own.at[1, 1 - x, piece], rb.at[j, 1 - x], sb.at[j])
        fb_copies.append(go.to(sb.at[j], fb.at[j], here.nx))

    for copy in do_copies:
        copy.wait_recv()
    m_sum = Reduce(go, here, m_send, m_recv)
    for k in range(2):
        for p in m_sum.pieces:
            m_sum.put(k, p, here.pair)
    length = s.quarter * nt
    doblk[...] = do_recv[...].astype(F32)
    doimg[:, pl.ds(length, s.irows - length), :] = jnp.zeros((s.images, s.irows - length, s.heads), F32)
    for i in range(s.images):
        for q in range(nt):
            doimg[i, pl.ds(q * s.quarter, s.quarter), :] = doblk[q, pl.ds(i * s.quarter, s.quarter), :]
    masks = head_masks(s)
    scale_factor = 1.0 / math.sqrt(HEAD_DIM)

    def attend_back(i, carry):
        block = qkv_ref[i]
        queries = stack_heads(block[:, : s.heads], masks)
        grads = stack_heads(doimg[i].astype(BF), masks)
        probs = p_ref[i]
        dvalues = dot_tn(probs, grads)
        dprob = dot_nt(grads, block[:, 2 * s.heads :])
        wide = probs.astype(F32)
        both = wide * dprob
        dscore = (both - wide * jnp.sum(both, -1, keepdims=True)).astype(BF)
        dqueries = pick_heads(dot(dscore, block[:, s.heads : 2 * s.heads]), masks, s.irows)
        dkeys = dot_tn(dscore, queries)
        dimg[i, :, : s.heads] = dqueries * scale_factor
        dimg[i, :, s.heads : 2 * s.heads] = dkeys * scale_factor
        dimg[i, :, 2 * s.heads :] = dvalues
        return carry

    lax.fori_loop(0, s.images, attend_back, 0)
    pump(0)
    used = s.images * s.quarter
    for q in range(nt):
        dblk[q, pl.ds(used, s.rows - used), :] = jnp.zeros((s.rows - used, 3 * s.heads), F32)
        for i in range(s.images):
            dblk[q, pl.ds(i * s.quarter, s.quarter), :] = dimg[i, pl.ds(q * s.quarter, s.quarter), :]
    dqkv[...] = dblk[...].astype(BF)
    w_qkv = wq_ref[...].reshape(s.width, 3 * s.heads)
    dn1_sum = Reduce(go, here, n_send, n_recv)
    dgain_one = jnp.zeros((1, s.width), F32)
    for k, q in enumerate(order):
        part = dot_nt(dqkv[q], w_qkv)
        dgain_one = dgain_one + jnp.sum(part * n1_ref[q].astype(F32), 0, keepdims=True)
        if k < 2:
            dn1_sum.pair(k, part)
        else:
            comb[2 * k - 3] = part
    dgain_one = dgain_one / gain_one

    pump(1)

    grad_qkv = jnp.zeros((s.width, 3 * s.heads), F32)
    for q in range(nt):
        grad_qkv = grad_qkv + dot_tn(n1_ref[q], dqkv[q])
    grads[:, :, :, :, : 3 * s.heads] = grad_qkv.reshape(*grads.shape[:3], s.shard, 3 * s.heads)
    gs_send[...] = grads[:, :, 1 - c].astype(BF)
    sm_send[0] = jnp.concatenate(
        [grad_router, dgain_one, dgain_two, jnp.zeros((sm_send.shape[1] - s.experts - 2, s.width), F32)], 0
    )
    step = [go.to(gs_send, gs_recv, here.sib), go.to(sm_send.at[0], sm_recv.at[0], here.sib)]
    dn1_sum.across(comb[1])
    m_sum.across(m_far[...])

    def add_small(k):
        sm_send[k + 1] = sm_send[k] + sm_recv[k]

    for copy in step:
        copy.wait_recv()
    grads[:, :, c] = grads[:, :, c] + gs_recv[...].astype(F32)
    add_small(0)
    gx_send[...] = grads[:, 1 - x, c].astype(BF)
    step = [go.to(gx_send, gx_recv, here.nx), go.to(sm_send.at[1], sm_recv.at[1], here.nx)]
    for copy in step:
        copy.wait_recv()
    grads[:, x, c] = grads[:, x, c] + gx_recv[...].astype(F32)
    add_small(1)
    gy_send[...] = grads[1 - y, x, c].astype(BF)
    step = [go.to(gy_send, gy_recv, here.ny), go.to(sm_send.at[2], sm_recv.at[2], here.ny)]
    for copy in step:
        copy.wait_recv()
    add_small(2)
    grads[y, x, c] = grads[y, x, c] + gy_recv[...].astype(F32)
    gqo_ref[:, : 3 * s.heads] = grads[y, x, c, :, : 3 * s.heads]
    for q in range(nt):
        gz_send[q] = grads[y, x, c, :, (3 + q) * s.heads : (4 + q) * s.heads].astype(BF)
    gz_copies = [go.to(gz_send.at[here.ring_t(k)], gz_recv.at[k - 1], (dp, here.ring_t(k))) for k in range(1, nt)]
    sm_copies = [go.to(sm_send.at[3], sm_recv.at[2 + k], (dp, here.ring_t(k))) for k in range(1, nt)]

    dn1 = dn1_sum.total(comb[3])
    dx_ln, _ = norm_back(x_ref[...].astype(F32), gain_one, dn1)
    result = gx_ref[...] + middle
    gx_ref[...] = comb[0] + dx_ln
    out_ref[...] = m_sum.total(result).astype(BF)
    total = gz_send[t].astype(F32)
    for k, copy in enumerate(gz_copies):
        copy.wait_recv()
        total = total + gz_recv[k].astype(F32)
    gqo_ref[:, 3 * s.heads :] = total
    total = sm_send[3]
    for k, copy in enumerate(sm_copies):
        copy.wait_recv()
        total = total + sm_recv[3 + k]
    gsm_ref[...] = total

    mine = pl.ds(pl.multiple_of(c * s.shard, s.shard), s.shard)
    other = pl.ds(pl.multiple_of((1 - c) * s.shard, s.shard), s.shard)
    fin_copies = []
    for w, (first, mine_first, second, copies) in enumerate(((ra, y, fa, fa_copies), (rb, x, fb, fb_copies))):
        for j in range(2):
            copies[j].wait_recv()

            def last(i, carry, w=w, first=first, mine_first=mine_first, second=second, j=j):
                def total(rows):
                    return (
                        own[w, mine_first, j * per + i, rows, :].astype(F32)
                        + first[j, mine_first, i, rows, :].astype(F32)
                        + second[j, i, rows, :].astype(F32)
                    )

                fin[w, j, i] = total(other).astype(BF)
                gw_ref[w, c, j * per + i] = total(mine)
                return carry

            lax.fori_loop(0, per, last, 0)
            fin_copies.append(go.to(fin.at[w, j], fin_recv.at[w, j], here.sib))
    for w in range(2):
        for j in range(2):
            fin_copies[2 * w + j].wait_recv()

            def widen(i, carry, w=w, j=j):
                gw_ref[w, 1 - c, j * per + i] = fin_recv[w, j, i].astype(F32)
                return carry

            lax.fori_loop(0, per, widen, 0)
    go.finish()


VSPEC = pl.BlockSpec(memory_space=pltpu.VMEM)
ASPEC = pl.BlockSpec(memory_space=pl.ANY)


def shape(dims, kind):
    return jax.ShapeDtypeStruct(dims, kind)


def linked_body(
    block_input,
    gains,
    w_qkv,
    w_o,
    w_router,
    w_in,
    w_out,
    pictures_alive_per_shard,
    expert_ids,
    slot_index,
    cotangent,
):
    images, quarter, width = block_input.shape
    n_dp, n_t = lax.axis_size("dp"), lax.axis_size("tensor")
    shard, experts, ff = w_in.shape
    heads = w_qkv.shape[2]
    length = quarter * n_t
    used = images * quarter
    rows = up(used, 16)
    s = Sizes(n_dp, n_t, images, quarter, rows, up(length, 16), width, shard, heads, experts, ff, up(rows, 128))
    dp, t = lax.axis_index("dp"), lax.axis_index("tensor")

    def by_rows(values):
        return jnp.pad(values.reshape(used, width), ((0, rows - used), (0, 0)))

    x_own, dz_own = by_rows(block_input), by_rows(cotangent)
    wq = w_qkv.reshape(shard, 3 * heads)
    wo = w_o.T
    sm_rows = up(experts + 2, 16)
    small = jnp.zeros((sm_rows, width), BF)
    piece = jnp.concatenate([w_router.T, gains.T], 0)
    small = lax.dynamic_update_slice(small, piece, (0, dp * shard))
    win_t = w_in.transpose(1, 0, 2).reshape(2, s.half, shard, ff)
    wout_t = w_out.transpose(1, 2, 0).reshape(2, s.half, shard, ff)
    place = t * quarter + jnp.arange(quarter)
    live = (jnp.arange(images) < pictures_alive_per_shard[0])[:, None] & (place < TOK_IMG)[None, :]
    live = jnp.pad(live.astype(F32).reshape(used, 1), ((0, rows - used), (0, 0)))
    targets = jnp.where(slot_index >= 0, expert_ids * CAP + slot_index, -1)
    targets = targets.reshape(images, n_t, quarter, 2).transpose(1, 0, 2, 3).reshape(n_t, used, 2)
    targets = jnp.pad(targets, ((0, 0), (0, rows - used), (0, 0)), constant_values=-1)
    tgt_rows = jnp.pad(targets.reshape(n_t * rows, 2).T, ((0, 6), (0, 0)), constant_values=-1)

    params = dict(has_side_effects=True, vmem_limit_bytes=VMEM_BYTES)
    front_links = 80
    front = pl.pallas_call(
        lambda *refs: front_kernel(s, *refs),
        out_shape=(
            shape((s.half, n_dp, shard, ff), BF),
            shape((s.half, n_dp, shard, ff), BF),
            shape((2, n_t, rows, width), BF),
            shape((2, n_t, rows, width), BF),
            shape((2, n_t, experts, s.lanes), F32),
            shape((2, 8, n_t * rows), jnp.int32),
            shape((rows, width), F32),
            shape((rows, width), BF),
            shape((experts, s.lanes), F32),
            shape((images, s.irows, 3 * heads), BF),
            shape((images, heads // HEAD_DIM * s.irows, s.irows), BF),
            shape((n_t, rows, width), BF),
            shape((n_t, rows, heads), BF),
            shape((n_dp, shard, 3 * heads), BF),
            shape((n_dp, n_t, shard, heads), BF),
            shape((sm_rows, width), F32),
        ),
        in_specs=[VSPEC] * 9,
        out_specs=[ASPEC] * 6 + [VSPEC] * 10,
        scratch_shapes=[
            pltpu.VMEM((n_t, rows, width), BF),
            pltpu.VMEM((n_dp, sm_rows, width), BF),
            pltpu.VMEM((n_t, shard, heads), BF),
            pltpu.VMEM((n_t, rows, 3 * heads), F32),
            pltpu.VMEM((images, s.irows, 3 * heads), F32),
            pltpu.VMEM((images, s.irows, heads), F32),
            pltpu.VMEM((n_t, rows, heads), F32),
            pltpu.VMEM((n_t, rows, heads), BF),
            pltpu.SemaphoreType.DMA((front_links,)),
            pltpu.SemaphoreType.DMA((front_links,)),
            pltpu.SemaphoreType.DMA((10,)),
        ],
        compiler_params=pltpu.CompilerParams(collective_id=1, **params),
        name="front",
    )
    (
        win_all, wout_all, n2_all, dz_all, prob_all, tgt_all,
        y, n2, prob, qkv, p, n1, o, wq_all, wo_all, small_sum,
    ) = front(x_own, dz_own, wq, wo, small, win_t, wout_t, live, tgt_rows)

    tokens = n_t * rows
    two_y, two_x = n_dp // 4, 2
    whole = lambda *dims: pl.BlockSpec(dims, lambda e: (0,) * len(dims))
    experts_call = pl.pallas_call(
        lambda *refs: expert_kernel(s, *refs),
        grid=(s.half,),
        out_shape=(
            shape((2, s.slots, width), BF),
            shape((2, s.slots, width), BF),
            shape((two_y, two_x, s.half, 2 * shard, ff), BF),
            shape((two_y, two_x, s.half, 2 * shard, ff), BF),
            shape((2, n_t, s.half, s.lanes), F32),
        ),
        in_specs=[
            whole(2, tokens, width),
            whole(2, tokens, width),
            whole(2, 8, tokens),
            whole(2, n_t, experts, s.lanes),
            pl.BlockSpec((1, width, ff), lambda e: (e, 0, 0)),
            pl.BlockSpec((1, width, ff), lambda e: (e, 0, 0)),
        ],
        out_specs=[
            pl.BlockSpec((2, CAP, width), lambda e: (0, e, 0)),
            pl.BlockSpec((2, CAP, width), lambda e: (0, e, 0)),
            pl.BlockSpec((two_y, two_x, 1, 2 * shard, ff), lambda e: (0, 0, e, 0, 0)),
            pl.BlockSpec((two_y, two_x, 1, 2 * shard, ff), lambda e: (0, 0, e, 0, 0)),
            whole(2, n_t, s.half, s.lanes),
        ],
        scratch_shapes=[
            pltpu.VMEM((2, experts, tokens), F32),
            pltpu.VMEM((2, s.half, tokens), F32),
        ],
        compiler_params=pltpu.CompilerParams(vmem_limit_bytes=VMEM_BYTES),
        name="experts",
    )
    dx, ge, gi, go, dpr = experts_call(
        n2_all.reshape(2, tokens, width),
        dz_all.reshape(2, tokens, width),
        tgt_all,
        prob_all,
        win_all.reshape(s.half, width, ff),
        wout_all.reshape(s.half, width, ff),
    )

    per = s.half // 2
    gsm_rows = up(experts + 2, 8)
    back_links = 64
    out, gx, gw, gqo, gsm = pl.pallas_call(
        lambda *refs: back_kernel(s, *refs),
        out_shape=(
            shape((rows, width), BF),
            shape((rows, width), F32),
            shape((2, 2, s.half, shard, ff), F32),
            shape((shard, 4 * heads), F32),
            shape((gsm_rows, width), F32),
        ),
        in_specs=[VSPEC] * 14 + [ASPEC] * 5,
        out_specs=[VSPEC] * 5,
        scratch_shapes=[
            pltpu.VMEM((2, s.slots, width), BF),
            pltpu.VMEM((2, s.slots, width), BF),
            pltpu.VMEM((n_t, 2, s.half, s.lanes), F32),
            pltpu.VMEM((n_t - 1, 2, s.half, s.lanes), F32),
            pltpu.VMEM((n_t, rows, width), F32),
            pltpu.VMEM((n_t - 1, rows, width), BF),
            pltpu.VMEM((n_t - 1, rows, width), BF),
            pltpu.VMEM((n_t - 1, rows, width), BF),
            pltpu.VMEM((n_t - 1, rows, width), BF),
            pltpu.VMEM((rows, width), F32),
            pltpu.VMEM((n_t - 1, rows, width), BF),
            pltpu.VMEM((n_t - 1, rows, width), BF),
            pltpu.VMEM((rows, width), BF),
            pltpu.VMEM((n_t, rows, heads), BF),
            pltpu.VMEM((n_t, rows, heads), BF),
            pltpu.VMEM((n_t, rows, heads), F32),
            pltpu.VMEM((images, s.irows, heads), F32),
            pltpu.VMEM((images, s.irows, 3 * heads), F32),
            pltpu.VMEM((n_t, rows, 3 * heads), F32),
            pltpu.VMEM((n_t, rows, 3 * heads), BF),
            pltpu.VMEM((two_y, two_x, 2, shard, 7 * heads), F32),
            pltpu.VMEM((two_y, two_x, shard, 7 * heads), BF),
            pltpu.VMEM((two_y, two_x, shard, 7 * heads), BF),
            pltpu.VMEM((two_y, shard, 7 * heads), BF),
            pltpu.VMEM((two_y, shard, 7 * heads), BF),
            pltpu.VMEM((shard, 7 * heads), BF),
            pltpu.VMEM((shard, 7 * heads), BF),
            pltpu.VMEM((n_t, shard, heads), BF),
            pltpu.VMEM((n_t - 1, shard, heads), BF),
            pltpu.VMEM((4, gsm_rows, width), F32),
            pltpu.VMEM((n_t + 2, gsm_rows, width), F32),
            pltpu.VMEM((2, 2, s.half, 2 * shard, ff), BF),
            pltpu.VMEM((2, 2, per, 2 * shard, ff), BF),
            pltpu.VMEM((2, 2, per, 2 * shard, ff), BF),
            pltpu.VMEM((2, per, 2 * shard, ff), BF),
            pltpu.VMEM((2, per, 2 * shard, ff), BF),
            pltpu.VMEM((2, per, 2 * shard, ff), BF),
            pltpu.VMEM((2, per, 2 * shard, ff), BF),
            pltpu.VMEM((2, 2, per, shard, ff), BF),
            pltpu.VMEM((2, 2, per, shard, ff), BF),
            pltpu.SemaphoreType.DMA((back_links,)),
            pltpu.SemaphoreType.DMA((back_links,)),
            pltpu.SemaphoreType.DMA((5,)),
        ],
        compiler_params=pltpu.CompilerParams(collective_id=2, **params),
        name="back",
    )(
        x_own, dz_own, y, n2, prob, live, targets, qkv, p, n1, o,
        wq_all, wo_all, small_sum, dpr, dx, ge, gi, go,
    )

    def by_image(values):
        return values[:used].reshape(images, quarter, width)

    gw = gw.reshape(2, experts, shard, ff)
    own_small = lax.dynamic_slice(gsm, (0, dp * shard), (gsm_rows, shard))
    return (
        by_image(out),
        by_image(gx),
        own_small[experts : experts + 2].T,
        gqo[:, : 3 * heads].reshape(shard, 3, heads),
        gqo[:, 3 * heads :].T,
        own_small[:experts].T,
        gw[0].transpose(1, 0, 2),
        gw[1].transpose(2, 0, 1),
    )


def solution(mesh):
    placed = (
        P("dp", "tensor", None),
        P("dp", None),
        P("dp", None, "tensor"),
        P("tensor", "dp"),
        P("dp", None),
        P("dp", None, "tensor"),
        P("tensor", None, "dp"),
        P("dp"),
        P("dp", None, None),
        P("dp", None, None),
        P("dp", "tensor", None),
    )
    linked = mesh.shape["dp"] == 8 and mesh.shape["tensor"] == 4
    return jax.shard_map(
        linked_body if linked else body,
        mesh=mesh,
        in_specs=placed,
        out_specs=(
            P("dp", "tensor", None),
            P("dp", "tensor", None),
            P("dp", None),
            P("dp", None, "tensor"),
            P("tensor", "dp"),
            P("dp", None),
            P("dp", None, "tensor"),
            P("tensor", None, "dp"),
        ),
        check_vma=False,
    )
```

```python
import math
from types import SimpleNamespace
from typing import NamedTuple

import jax
import jax.numpy as jnp
from jax import lax
from jax.experimental import pallas as pl
from jax.experimental.pallas import tpu as pltpu
from jax.sharding import PartitionSpec as P

HEAD_DIM = 64
TOK_IMG = 197
CAP = 192


epsilon = 1e-06
negative_fill = -1e30


def as_sent(shard):
    return jax.tree.map(lambda a: a.astype(jnp.bfloat16) if a.dtype == jnp.float32 else a, shard)


def layer_norm(values, gain):
    centre = values - jnp.mean(values, -1, keepdims=True)
    spread = jnp.mean(centre * centre, -1, keepdims=True)
    return centre * lax.rsqrt(spread + epsilon) * gain


def gelu_exact(values):
    return jax.nn.gelu(values, approximate=False)


def gate_values(logits, chosen):
    router_probs = jax.nn.softmax(logits, axis=-1)
    return jnp.einsum("re,rke->rk", router_probs, chosen)


def rows_in(values):
    return lax.all_gather(values, "tensor", axis=1, tiled=True)


def rows_out(values):
    return lax.psum_scatter(values, "tensor", scatter_dimension=1, tiled=True)


def grads_in(values):
    return jax.tree.map(
        lambda part, own: part.astype(own.dtype),
        lax.all_gather(as_sent(values), "tensor", axis=1, tiled=True),
        values,
    )


def grads_out(values):
    return lax.psum_scatter(values, "tensor", scatter_dimension=1, tiled=True)


def attention_scores(queries, keys_all, key_live, scale_factor):
    gating_logits_matrix = (
        jnp.einsum("ilhe,imhe->ihlm", queries, keys_all, preferred_element_type=jnp.float32)
        * scale_factor
    )
    return jnp.where(key_live[None, None, None, :], gating_logits_matrix, negative_fill)


def body(
    block_input,
    gains,
    w_qkv,
    w_o,
    w_router,
    w_in,
    w_out,
    pictures_alive_per_shard,
    expert_ids,
    slot_index,
    cotangent,
):
    tensor_size = lax.axis_size("tensor")
    tensor_pos = lax.axis_index("tensor")
    images, quarter, model_width = block_input.shape
    length = quarter * tensor_size
    all_rows = images * length
    own_rows = images * quarter
    start_row = tensor_pos * quarter
    experts = w_in.shape[1]
    slot_count = experts * CAP
    key_live = jnp.arange(length) < TOK_IMG
    live_all = (
        (jnp.arange(images) < pictures_alive_per_shard[0])[:, None] & key_live[None, :]
    ).astype(jnp.float32)
    live_own = lax.dynamic_slice_in_dim(live_all, start_row, quarter, 1)
    gathered = (
        lax.all_gather(gains, "dp", axis=0, tiled=True),
        lax.all_gather(w_qkv, "dp", axis=0, tiled=True),
        lax.all_gather(w_o, "dp", axis=1, tiled=True),
        lax.all_gather(w_router, "dp", axis=0, tiled=True),
        lax.all_gather(w_in, "dp", axis=0, tiled=True),
        lax.all_gather(w_out, "dp", axis=2, tiled=True),
    )
    gain_all, qkv_all, outproj_all, router_all, expin_all, expout_all = gathered
    head_cols = qkv_all.shape[2]
    local_heads = head_cols // HEAD_DIM
    scale_factor = 1.0 / math.sqrt(HEAD_DIM)
    gain_one = gain_all[:, 0].astype(jnp.float32)
    gain_two = gain_all[:, 1].astype(jnp.float32)
    x_float = block_input.astype(jnp.float32)
    normed = layer_norm(x_float, gain_one).astype(jnp.bfloat16)
    normed_all = rows_in(normed).reshape(all_rows, model_width)
    project = jnp.einsum(
        "rd,djc->rjc", normed_all, qkv_all, preferred_element_type=jnp.float32
    ).astype(jnp.bfloat16)
    queries = project[:, 0].reshape(images, length, local_heads, HEAD_DIM)
    keys_all = project[:, 1].reshape(images, length, local_heads, HEAD_DIM)
    values_all = project[:, 2].reshape(images, length, local_heads, HEAD_DIM)
    masked = attention_scores(queries, keys_all, key_live, scale_factor)
    top_score = jnp.max(masked, -1, keepdims=True)
    expd = jnp.exp(masked - top_score)
    total = jnp.sum(expd, -1, keepdims=True)
    att_probs = expd / total
    log_total = top_score + jnp.log(total)
    attended = jnp.einsum(
        "ihlm,imhe->ilhe",
        att_probs.astype(jnp.bfloat16),
        values_all,
        preferred_element_type=jnp.float32,
    )
    attended = attended.astype(jnp.bfloat16).reshape(all_rows, head_cols)
    branch_part = jnp.dot(attended, outproj_all, preferred_element_type=jnp.float32).reshape(
        images, length, model_width
    )
    middle = x_float + live_own[:, :, None] * rows_out(branch_part)
    normed_two = layer_norm(middle, gain_two).astype(jnp.bfloat16)
    normed_two_all = rows_in(normed_two).reshape(all_rows, model_width)
    own_flat = normed_two.reshape(own_rows, model_width)
    expert_range = jnp.arange(experts)
    own_ids = lax.dynamic_slice_in_dim(expert_ids, start_row, quarter, 1).reshape(own_rows, 2)
    chosen = (own_ids[:, :, None] == expert_range[None, None, :]).astype(jnp.float32)
    targets = jnp.where(slot_index >= 0, expert_ids * CAP + slot_index, -1).reshape(all_rows, 2)
    slot_ids = jnp.arange(slot_count)
    first_hot = (targets[:, 0:1] == slot_ids[None, :]).astype(jnp.bfloat16)
    second_hot = (targets[:, 1:2] == slot_ids[None, :]).astype(jnp.bfloat16)
    dispatched = jnp.einsum(
        "rs,rd->sd", first_hot, normed_two_all, preferred_element_type=jnp.float32
    )
    dispatched = dispatched + jnp.einsum(
        "rs,rd->sd", second_hot, normed_two_all, preferred_element_type=jnp.float32
    )
    dispatched = dispatched.astype(jnp.bfloat16).reshape(experts, CAP, model_width)
    hidden = jnp.einsum("ecd,def->ecf", dispatched, expin_all, preferred_element_type=jnp.float32)
    active = gelu_exact(hidden).astype(jnp.bfloat16)
    expert_part = jnp.einsum("ecf,fed->ecd", active, expout_all, preferred_element_type=jnp.float32)
    expert_part = expert_part.astype(jnp.bfloat16).reshape(slot_count, model_width)
    first_rows = jnp.dot(first_hot, expert_part, preferred_element_type=jnp.float32)
    second_rows = jnp.dot(second_hot, expert_part, preferred_element_type=jnp.float32)
    logits = jnp.dot(own_flat, router_all, preferred_element_type=jnp.float32)
    gates = gate_values(logits, chosen)
    first_own, second_own = rows_out(
        (
            first_rows.reshape(images, length, model_width),
            second_rows.reshape(images, length, model_width),
        )
    )
    gate_grid = gates.reshape(images, quarter, 2)
    output = middle + gate_grid[:, :, 0:1] * first_own + gate_grid[:, :, 1:2] * second_own
    grad_output = cotangent.astype(jnp.float32)
    grad_first = (gate_grid[:, :, 0:1] * grad_output).astype(jnp.bfloat16)
    grad_second = (gate_grid[:, :, 1:2] * grad_output).astype(jnp.bfloat16)
    grad_gates = jnp.stack(
        [jnp.sum(grad_output * first_own, -1), jnp.sum(grad_output * second_own, -1)], -1
    ).reshape(own_rows, 2)
    leading_cotangent, second_back = grads_in((grad_first, grad_second))
    leading_cotangent = leading_cotangent.reshape(all_rows, model_width)
    second_back = second_back.reshape(all_rows, model_width)
    unused_gates, gate_pull = jax.vjp(lambda values: gate_values(values, chosen), logits)
    grad_logits = gate_pull(grad_gates)[0].astype(jnp.bfloat16)
    grad_router = jnp.einsum("rd,re->de", own_flat, grad_logits, preferred_element_type=jnp.float32)
    router_back = jnp.einsum(
        "re,de->rd", grad_logits, router_all, preferred_element_type=jnp.float32
    )
    grad_expert = jnp.einsum(
        "rs,rd->sd", first_hot, leading_cotangent, preferred_element_type=jnp.float32
    )
    grad_expert = grad_expert + jnp.einsum(
        "rs,rd->sd", second_hot, second_back, preferred_element_type=jnp.float32
    )
    grad_expert = grad_expert.astype(jnp.bfloat16).reshape(experts, CAP, model_width)
    grad_active = jnp.einsum(
        "ecd,fed->ecf", grad_expert, expout_all, preferred_element_type=jnp.float32
    )
    grad_expout = jnp.einsum(
        "ecf,ecd->fed", active, grad_expert, preferred_element_type=jnp.float32
    )
    unused_gelu, gelu_pull = jax.vjp(gelu_exact, hidden)
    grad_hidden = gelu_pull(grad_active)[0].astype(jnp.bfloat16)
    grad_expin = jnp.einsum(
        "ecd,ecf->def", dispatched, grad_hidden, preferred_element_type=jnp.float32
    )
    grad_dispatch = jnp.einsum(
        "ecf,def->ecd", grad_hidden, expin_all, preferred_element_type=jnp.float32
    )
    grad_dispatch = grad_dispatch.astype(jnp.bfloat16).reshape(slot_count, model_width)
    back_rows = jnp.dot(first_hot, grad_dispatch, preferred_element_type=jnp.float32)
    back_rows = back_rows + jnp.dot(second_hot, grad_dispatch, preferred_element_type=jnp.float32)
    grad_normed_two = grads_out(
        back_rows.reshape(images, length, model_width)
    ) + router_back.reshape(images, quarter, model_width)
    unused_two, norm_two_pull = jax.vjp(layer_norm, middle, gain_two)
    grad_middle_norm, grad_gain_two = norm_two_pull(grad_normed_two)
    grad_middle = grad_output + grad_middle_norm
    grad_branch = (live_own[:, :, None] * grad_middle).astype(jnp.bfloat16)
    grad_branch_all = grads_in(grad_branch).reshape(all_rows, model_width)
    grad_outproj = jnp.einsum(
        "rc,rd->cd", attended, grad_branch_all, preferred_element_type=jnp.float32
    )
    grad_attended = jnp.einsum(
        "rd,cd->rc", grad_branch_all, outproj_all, preferred_element_type=jnp.float32
    )
    grad_attended = grad_attended.astype(jnp.bfloat16).reshape(
        images, length, local_heads, HEAD_DIM
    )
    masked_again = attention_scores(queries, keys_all, key_live, scale_factor)
    probs_again = jnp.exp(masked_again - log_total)
    grad_values = jnp.einsum(
        "ihlm,ilhe->imhe",
        probs_again.astype(jnp.bfloat16),
        grad_attended,
        preferred_element_type=jnp.float32,
    )
    grad_values = grad_values.astype(jnp.bfloat16)
    grad_probs = jnp.einsum(
        "ilhe,imhe->ihlm", grad_attended, values_all, preferred_element_type=jnp.float32
    )
    grad_scores = probs_again * (grad_probs - jnp.sum(probs_again * grad_probs, -1, keepdims=True))
    grad_scores = grad_scores.astype(jnp.bfloat16)
    grad_queries = (
        jnp.einsum("ihlm,imhe->ilhe", grad_scores, keys_all, preferred_element_type=jnp.float32)
        * scale_factor
    ).astype(jnp.bfloat16)
    grad_keys = (
        jnp.einsum("ihlm,ilhe->imhe", grad_scores, queries, preferred_element_type=jnp.float32)
        * scale_factor
    ).astype(jnp.bfloat16)
    grad_project = jnp.stack([grad_queries, grad_keys, grad_values], 2).reshape(
        all_rows, 3, head_cols
    )
    grad_qkv = jnp.einsum(
        "rd,rjc->djc", normed_all, grad_project, preferred_element_type=jnp.float32
    )
    normed_back = jnp.einsum(
        "rjc,djc->rd", grad_project, qkv_all, preferred_element_type=jnp.float32
    )
    grad_normed = grads_out(normed_back.reshape(images, length, model_width))
    unused_one, norm_one_pull = jax.vjp(layer_norm, x_float, gain_one)
    grad_x_norm, grad_gain_one = norm_one_pull(grad_normed)
    grad_input = grad_middle + grad_x_norm
    router_sum, gain_sum = lax.psum(
        (grad_router, jnp.stack([grad_gain_one, grad_gain_two], 1)), "tensor"
    )
    expert_fractions = (
        lax.psum_scatter(gain_sum, "dp", scatter_dimension=0, tiled=True),
        lax.psum_scatter(grad_qkv, "dp", scatter_dimension=0, tiled=True),
        lax.psum_scatter(grad_outproj, "dp", scatter_dimension=1, tiled=True),
        lax.psum_scatter(router_sum, "dp", scatter_dimension=0, tiled=True),
        lax.psum_scatter(grad_expin, "dp", scatter_dimension=0, tiled=True),
        lax.psum_scatter(grad_expout, "dp", scatter_dimension=2, tiled=True),
    )
    return (
        output.astype(jnp.bfloat16),
        grad_input,
        expert_fractions[0],
        expert_fractions[1],
        expert_fractions[2],
        expert_fractions[3],
        expert_fractions[4],
        expert_fractions[5],
    )


MESH = pl.DeviceIdType.MESH
BF = jnp.bfloat16
F32 = jnp.float32
VMEM_BYTES = 62 << 20


class Sizes(NamedTuple):
    n_dp: int
    n_t: int
    images: int
    quarter: int
    rows: int
    irows: int
    width: int
    shard: int
    heads: int
    experts: int
    ff: int
    lanes: int

    @property
    def half(self):
        return self.experts // 2

    @property
    def slots(self):
        return self.half * CAP


def up(value, step):
    return -(-value // step) * step


def norm_parts(values):
    centre = values - jnp.mean(values, -1, keepdims=True)
    scale = lax.rsqrt(jnp.mean(centre * centre, -1, keepdims=True) + epsilon)
    return centre * scale, scale


def norm_back(values, gain, grad):
    unit, scale = norm_parts(values)
    inner = grad * gain
    mean_a = jnp.mean(inner, -1, keepdims=True)
    mean_b = jnp.mean(inner * unit, -1, keepdims=True)
    return scale * (inner - mean_a - unit * mean_b), unit


def dot(a, b):
    return jnp.dot(a, b, preferred_element_type=F32)


def dot_nt(a, b):
    return lax.dot_general(a, b, (((1,), (1,)), ((), ())), preferred_element_type=F32)


def dot_tn(a, b):
    return lax.dot_general(a, b, (((0,), (0,)), ((), ())), preferred_element_type=F32)


class Place:
    def __init__(self, s):
        self.s = s
        self.dp = lax.axis_index("dp")
        self.t = lax.axis_index("tensor")
        self.c = lax.rem(self.dp, 2)
        self.x = lax.rem(self.dp // 2, 2)
        self.y = self.dp // 4
        self.chip = self.dp // 2
        self.chip_x = self.y * 2 + (1 - self.x)
        self.chip_y = (1 - self.y) * 2 + self.x
        self.sib = (self.chip * 2 + (1 - self.c), self.t)
        self.nx_other = (self.chip_x * 2 + (1 - self.c), self.t)
        self.ny_other = (self.chip_y * 2 + (1 - self.c), self.t)
        self.pair = lax.rem(self.t, 2) * (-2) + self.t + 1
        self.far = lax.rem(self.t + 2, 4)
        self.cross = lax.rem(self.pair + 2, 4)
        self.nx = (self.chip_x * 2 + self.c, self.t)
        self.ny = (self.chip_y * 2 + self.c, self.t)

    def ring_dp(self, k):
        return lax.rem(self.dp + k, self.s.n_dp)

    def ring_t(self, k):
        return lax.rem(self.t + k, self.s.n_t)

    def from_t(self, k):
        return lax.rem(self.t + self.s.n_t - k, self.s.n_t)

    def greet(self):
        barrier = pltpu.get_barrier_semaphore()
        for k in range(1, self.s.n_dp):
            pl.semaphore_signal(barrier, inc=1, device_id=(self.ring_dp(k), self.t), device_id_type=MESH)
        for k in range(1, self.s.n_t):
            pl.semaphore_signal(barrier, inc=1, device_id=(self.dp, self.ring_t(k)), device_id_type=MESH)
        pl.semaphore_wait(barrier, self.s.n_dp + self.s.n_t - 2)


class Copies:
    def __init__(self, send, recv, local):
        self.send, self.recv, self.local = send, recv, local
        self.n = 0
        self.m = 0
        self.sent = []

    def make(self, k, src, dst, device):
        return pltpu.make_async_remote_copy(
            src_ref=src,
            dst_ref=dst,
            send_sem=self.send.at[k],
            recv_sem=self.recv.at[k],
            device_id=device,
            device_id_type=MESH,
        )

    def to(self, src, dst, device):
        copy = self.make(self.n, src, dst, device)
        self.n += 1
        copy.start()
        self.sent.append(copy)
        return copy

    def here(self, src, dst):
        copy = pltpu.make_async_copy(src, dst, self.local.at[self.m])
        self.m += 1
        copy.start()
        return copy

    def reserve(self, count):
        self.n += count
        return self.n - count

    def at(self, k, src, dst, device):
        copy = self.make(k, src, dst, device)
        self.sent.append(copy)
        return copy

    def start_at(self, k, src, dst, device):
        self.make(k, src, dst, device).start()

    def sent_now(self, copies):
        for copy in copies:
            copy.wait_send()
        self.sent = [copy for copy in self.sent if not any(copy is done for done in copies)]

    def finish(self):
        for copy in self.sent:
            copy.wait_send()


def pieces_of(rows):
    first = up(rows // 2, 16)
    return [pl.ds(0, first), pl.ds(first, rows - first)]


class Gather:
    def __init__(self, go, here, own, full):
        self.go, self.here, self.full = go, here, full
        self.pieces = pieces_of(here.s.rows)
        mine = full(here.t)
        self.to_far = [go.to(own.at[p], mine.at[p], (here.dp, here.far)) for p in self.pieces]
        self.to_pair = [go.to(own.at[p], mine.at[p], (here.dp, here.pair)) for p in self.pieces]

    def relay(self):
        block = self.full(self.here.far)
        self.passed = []
        for p, copy in zip(self.pieces, self.to_far):
            copy.wait_recv()
            self.passed.append(self.go.to(block.at[p], block.at[p], (self.here.dp, self.here.pair)))

    def sent_on(self):
        self.go.sent_now(self.passed)

    def wait_pair(self):
        for copy in self.to_pair:
            copy.wait_recv()

    def wait_cross(self):
        for copy in self.passed:
            copy.wait_recv()

    def share(self, block):
        return self.go.to(self.full(block), self.full(block), self.here.sib)


class Reduce:
    def __init__(self, go, here, send, recv):
        self.go, self.here, self.send, self.recv = go, here, send, recv
        self.pieces = pieces_of(here.s.rows)
        self.copies = [[], [], []]

    def put(self, k, p, device):
        self.copies[k].append(self.go.to(self.send.at[k, p], self.recv.at[k, p], (self.here.dp, device)))

    def pair(self, k, value):
        self.send[k] = value.astype(BF)
        for p in self.pieces:
            self.put(k, p, self.here.pair)

    def across(self, part):
        for i, p in enumerate(self.pieces):
            self.copies[0][i].wait_recv()
            self.send[2, p] = (part[p] + self.recv[0, p].astype(F32)).astype(BF)
            self.put(2, p, self.here.far)

    def sent(self):
        self.go.sent_now([copy for copies in self.copies for copy in copies])

    def total(self, part):
        for copy in self.copies[1] + self.copies[2]:
            copy.wait_recv()
        return part + self.recv[1].astype(F32) + self.recv[2].astype(F32)


def head_masks(s):
    lane = lax.broadcasted_iota(jnp.int32, (s.irows, s.heads), 1)
    return [(lane // HEAD_DIM) == h for h in range(s.heads // HEAD_DIM)]


def stack_heads(values, masks):
    zero = jnp.zeros_like(values)
    return jnp.concatenate([jnp.where(mask, values, zero) for mask in masks], 0)


def pick_heads(stacked, masks, irows):
    out = stacked[:irows]
    for h in range(1, len(masks)):
        out = jnp.where(masks[h], stacked[h * irows : (h + 1) * irows], out)
    return out


def block_kernel(s, names, *refs):
    r = SimpleNamespace(**dict(zip(names, refs)))
    here = Place(s)
    dp, t, c, x, y = here.dp, here.t, here.c, here.x, here.y
    here.greet()
    go = Copies(r.send, r.recv, r.local)
    nt = s.n_t
    length = s.quarter * nt
    used = s.images * s.quarter
    per = s.half // 2
    masks = head_masks(s)

    def to_image_rows(q, block, images):
        for i in range(s.images):
            images[i, pl.ds(q * s.quarter, s.quarter), :] = block[pl.ds(i * s.quarter, s.quarter), : images.shape[2]]

    def to_block_rows(q, images, block):
        for i in range(s.images):
            block[pl.ds(i * s.quarter, s.quarter), : images.shape[2]] = images[i, pl.ds(q * s.quarter, s.quarter), :]

    def clear(images):
        images[:, pl.ds(length, s.irows - length), :] = jnp.zeros((s.images, s.irows - length, images.shape[2]), F32)

    clear(r.img)
    clear(r.oimg)
    r.row[pl.ds(used, s.rows - used), :] = jnp.zeros((s.rows - used, 3 * s.heads), F32)

    wo_copies = [go.to(r.wo, r.wo_z.at[t], (dp, here.ring_t(k))) for k in range(1, nt)]
    x_blocks = Gather(go, here, r.x, lambda block: r.n1.at[block])
    sm_copies = [go.to(r.sm, r.sm_all.at[dp], (here.ring_dp(k), t)) for k in range(1, s.n_dp)]
    wq_copies = [go.to(r.wq, r.wq_all.at[dp], (here.ring_dp(k), t)) for k in range(1, s.n_dp)]

    def spread(shard, full):
        to = full.at[:, y, x, pl.ds(pl.multiple_of(c * s.shard, s.shard), s.shard)]
        half, rest = shard.at[c], shard.at[1 - c]
        from_x = [go.to(half, to, here.nx), go.to(rest, to, here.nx_other)]
        from_y = [go.to(half, to, here.ny), go.to(rest, to, here.ny_other)]
        return from_x, from_y, go.to(rest, to, here.sib), go.here(half, to)

    in_x, in_y, in_sib, keep_in = spread(r.win, r.win_all)
    keep_sm = go.here(r.sm, r.sm_all.at[dp])
    keep_wq = go.here(r.wq, r.wq_all.at[dp])
    keep_wo = go.here(r.wo, r.wo_z.at[t])
    tgt_copy = go.to(r.tgt, r.tgt_all.at[c], here.sib)
    keep_tgt = go.here(r.tgt, r.tgt_all.at[c])

    def dz_block(block):
        return r.ge.at[c, pl.ds(pl.multiple_of(block * s.rows, 16), s.rows)]

    dz_sib = go.to(r.dz, dz_block(t), here.sib)
    keep_dz = go.here(r.dz, dz_block(t))

    keep_sm.wait()
    for copy in sm_copies:
        copy.wait_recv()
    small = jnp.concatenate([r.sm_all[k][:, : s.shard].astype(F32) for k in range(s.n_dp)], 1)
    r.small[...] = small
    gain_one = small[s.experts : s.experts + 1]
    gain_two = small[s.experts + 1 : s.experts + 2]
    keep_wq.wait()
    for copy in wq_copies:
        copy.wait_recv()

    keep_wo.wait()
    for copy in wo_copies:
        copy.wait_recv()
    keep_wo_all = go.here(r.wo_z, r.wo_all.at[dp])
    wo_out = [go.to(r.wo_z, r.wo_all.at[dp], (here.ring_dp(k), t)) for k in range(1, s.n_dp)]

    def project(slot, values):
        unit, _ = norm_parts(values.astype(F32))
        normed = (unit * gain_one).astype(BF)
        r.n1[slot] = normed
        r.comb[slot, :, : 3 * s.heads] = dot(normed, r.wq_all[...].reshape(s.width, 3 * s.heads))

    project(t, r.x[...])
    x_blocks.relay()
    out_x, out_y, out_sib, keep_out = spread(r.wout, r.wout_all)
    x_blocks.wait_pair()
    project(here.pair, r.n1[here.pair])
    x_blocks.sent_on()
    project(here.far, r.n1[here.far])
    x_blocks.wait_cross()
    project(here.cross, r.n1[here.cross])
    dz_blocks = Gather(go, here, r.dz, dz_block)

    low_half, high_half = pl.ds(0, per), pl.ds(per, per)

    def pass_on(full, by_x, by_y):
        for copy in by_x:
            copy.wait_recv()
        from_x = full.at[low_half, y, 1 - x]
        on_y = go.to(from_x, from_x, here.ny)
        for copy in by_y:
            copy.wait_recv()
        from_y = full.at[high_half, 1 - y, x]
        return on_y, go.to(from_y, from_y, here.nx)

    in_on = pass_on(r.win_all, in_x, in_y)
    for q in range(nt):
        to_image_rows(q, r.comb.at[q], r.img)

    def attend(i, carry):
        block = r.img[i].astype(BF)
        r.qkv[i] = block
        queries = stack_heads(block[:, : s.heads], masks)
        scores = dot_nt(queries, block[:, s.heads : 2 * s.heads]) * (1.0 / math.sqrt(HEAD_DIM))
        key = lax.broadcasted_iota(jnp.int32, scores.shape, 1)
        scores = jnp.where(key < TOK_IMG, scores, negative_fill)
        expd = jnp.exp(scores - jnp.max(scores, -1, keepdims=True))
        probs = (expd / jnp.sum(expd, -1, keepdims=True)).astype(BF)
        r.p[i] = probs
        r.oimg[i] = pick_heads(dot(probs, block[:, 2 * s.heads :]), masks, s.irows)
        return carry

    lax.fori_loop(0, s.images, attend, 0)
    for q in range(nt):
        to_block_rows(q, r.oimg, r.row)
        r.o_send[q] = r.row[:, : s.heads].astype(BF)
    o_copies = [go.to(r.o_send.at[here.ring_t(k)], r.o.at[t], (dp, here.ring_t(k))) for k in range(1, nt)]
    r.o[t] = r.o_send[t]
    dz_blocks.relay()
    keep_wo_all.wait()
    for copy in wo_out:
        copy.wait_recv()
    for copy in o_copies:
        copy.wait_recv()
    branch = jnp.zeros((s.rows, s.width), F32)
    for q in range(nt):
        branch = branch + dot_nt(r.o[q], r.wo_all[:, q].reshape(s.width, s.heads))
    middle = r.x[...].astype(F32) + r.live[...] * branch
    r.y[...] = middle
    unit, _ = norm_parts(middle)
    normed_two = (unit * gain_two).astype(BF)
    n2_own = r.n2_all.at[c, t]
    n2_own[...] = normed_two
    n2_sib = go.to(n2_own, n2_own, here.sib)
    n2_blocks = Gather(go, here, n2_own, lambda block: r.n2_all.at[c, block])
    logits = dot_nt(small[: s.experts].astype(BF), normed_two)
    expd = jnp.exp(logits - jnp.max(logits, 0, keepdims=True))
    r.prob[...] = jnp.zeros((s.experts, s.lanes), F32)
    r.prob[:, : s.rows] = expd / jnp.sum(expd, 0, keepdims=True)
    r.prob_all[c, t] = r.prob[...]
    pr_sib = go.to(r.prob, r.prob_all.at[c, t], here.sib)
    pr_copies = [go.to(r.prob, r.prob_all.at[c, t], (dp, here.ring_t(k))) for k in range(1, nt)]

    n2_blocks.relay()
    on_n2 = [n2_blocks.share(here.far)]
    on_dz = [dz_blocks.share(here.far)]
    dz_blocks.wait_pair()
    on_dz.append(dz_blocks.share(here.pair))
    dz_blocks.wait_cross()
    on_dz.append(dz_blocks.share(here.cross))
    n2_blocks.wait_pair()
    on_n2.append(n2_blocks.share(here.pair))
    for k, copy in enumerate(pr_copies, 1):
        copy.wait_recv()
        slot = r.prob_all.at[c, here.from_t(k)]
        on_n2.append(go.to(slot, slot, here.sib))
    out_on = pass_on(r.wout_all, out_x, out_y)
    keep_tgt.wait()
    keep_dz.wait()
    for copy in [tgt_copy, dz_sib] + on_dz:
        copy.wait_recv()

    tokens = nt * s.rows
    few = 2
    for q in range(2):
        first_id = (c * s.half + lax.broadcasted_iota(jnp.int32, (s.half, tokens), 0)) * CAP
        found = jnp.full((s.half, tokens), -1, jnp.int32)
        for k in range(2):
            slot = r.tgt_all[q, k : k + 1, :] - first_id
            found = jnp.where((slot >= 0) & (slot < CAP), slot, found)
        r.slot[q] = found.astype(F32)
    slot_ids = lax.broadcasted_iota(jnp.int32, (CAP, tokens), 0).astype(F32)

    def dispatch(q, j, rows, out):
        for i in range(few):
            hits = r.slot[q, pl.ds(few * j + i, 1), :] == slot_ids
            r.hot[i] = jnp.where(hits, 1.0, 0.0).astype(BF)
        found = dot(r.hot[...].reshape(few * CAP, tokens), rows)
        out[...] = found.astype(BF).reshape(out.shape)

    def dispatch_z(j, carry):
        for q in range(2):
            dispatch(q, j, r.ge[q, :tokens], r.zin.at[q, pl.ds(few * j, few)])
        return carry

    lax.fori_loop(0, s.half // few, dispatch_z, 0)
    n2_blocks.wait_cross()
    on_n2.append(n2_blocks.share(here.cross))
    keep_in.wait()
    keep_out.wait()
    for copy in [n2_sib, pr_sib, in_sib, out_sib, *in_on] + on_n2:
        copy.wait_recv()
    mine = pl.ds(pl.multiple_of(c * s.half, s.half), s.half)
    for q in range(2):
        r.pr[q] = jnp.concatenate([r.prob_all[q, k, mine][:, : s.rows] for k in range(nt)], 1)
    for copy in out_on:
        copy.wait_recv()
    go.sent_now([*in_on, *out_on, dz_sib, *dz_blocks.passed, *on_dz])
    k_in, k_out, k_dx, k_ge = (go.reserve(s.half) for _ in range(4))

    def grad_in_copy(e):
        return r.win_all.at[e, :, 1 - x], r.ra.at[e], here.nx

    def grad_out_copy(e):
        return r.wout_all.at[e, 1 - y], r.rb.at[e], here.ny

    def dx_copy(e):
        return r.xin.at[1 - c, e], r.dxv.at[e], here.sib

    def slots_of(e):
        return pl.ds(pl.multiple_of(e * CAP, CAP), CAP)

    def ge_copy(e):
        return r.ge.at[1 - c, slots_of(e)], r.gev.at[slots_of(e)], here.sib

    def expert(e):
        x_in = r.xin[:, e].reshape(2 * CAP, s.width)
        w_in = r.win_all[e].reshape(s.width, s.ff)
        w_out = r.wout_all[e].reshape(s.width, s.ff)
        hidden = dot(x_in, w_in)
        bell = jnp.exp(-0.5 * hidden * hidden)
        u = 1.0 / (1.0 + (0.3275911 / math.sqrt(2.0)) * jnp.abs(hidden))
        poly = u * (0.254829592 + u * (-0.284496736 + u * (1.421413741 + u * (-1.453152027 + u * 1.061405429))))
        tail = 0.5 * poly * bell
        phi = jnp.where(hidden >= 0, 1.0 - tail, tail)
        active = (hidden * phi).astype(BF)
        slope = phi + hidden * bell * (1.0 / math.sqrt(2.0 * math.pi))
        out = dot_nt(active, w_out).astype(BF).astype(F32)
        for q in range(2):
            hits = r.slot[q, pl.ds(e, 1), :] == slot_ids
            gate = jnp.sum(jnp.where(hits, r.pr[q, pl.ds(e, 1), :], 0.0), 1, keepdims=True)
            part = out[q * CAP : (q + 1) * CAP]
            wide = r.zin[q, e].astype(F32)
            dgate = jnp.sum(wide * part, 1, keepdims=True)
            r.dpr[q, pl.ds(e, 1), :] = jnp.sum(jnp.where(hits, dgate, 0.0), 0, keepdims=True)
            r.zin[q, e] = (gate * wide).astype(BF)
            r.ge[q, slots_of(e)] = (gate * part).astype(BF)
        grad = r.zin[:, e].reshape(2 * CAP, s.width)
        dhidden = (dot(grad, w_out) * slope).astype(BF)
        r.wout_all[e] = dot_tn(grad, active).astype(BF).reshape(r.wout_all.shape[1:])
        grad_in = dot_tn(x_in, dhidden).astype(BF)
        r.xin[:, e] = dot_nt(dhidden, w_in).astype(BF).reshape(2, CAP, s.width)
        r.win_all[e] = grad_in.reshape(r.win_all.shape[1:])

    def expert_few(j, carry):
        for q in range(2):
            dispatch(q, j, r.n2_all[q].reshape(tokens, s.width), r.xin.at[q, pl.ds(few * j, few)])
        for i in range(few):
            expert(few * j + i)
        for i in range(few):
            e = few * j + i
            for k, copy in ((k_out, grad_out_copy), (k_in, grad_in_copy), (k_dx, dx_copy), (k_ge, ge_copy)):
                go.start_at(k + e, *copy(e))
        return carry

    lax.fori_loop(0, s.half // few, expert_few, 0)
    ge_copies = [go.at(k_ge + e, *ge_copy(e)) for e in range(s.half)]
    dx_copies = [go.at(k_dx + e, *dx_copy(e)) for e in range(s.half)]
    in_copies = [go.at(k_in + e, *grad_in_copy(e)) for e in range(s.half)]
    out_copies = [go.at(k_out + e, *grad_out_copy(e)) for e in range(s.half)]

    r.dprs[...] = jnp.zeros(r.dprs.shape, F32)
    for q in range(2):
        for k in range(nt):
            r.dprs[q, k, :, : s.rows] = r.dpr[q][:, k * s.rows : (k + 1) * s.rows]
    dpr_sib = go.to(r.dprs.at[1 - c], r.dprf.at[:, c], here.sib)
    r.dprf[:, c] = r.dprs[c]
    zero_rows = jnp.zeros((s.rows, s.width), F32)
    span = 512

    def combine(values, half, q, total):
        first = r.tcol[q, :, 0:1] - half * s.slots
        second = r.tcol[q, :, 1:2] - half * s.slots
        lane = lax.broadcasted_iota(jnp.int32, (s.rows, span), 1)
        for j in range(s.slots // span):
            hot = jnp.where((first - j * span == lane) | (second - j * span == lane), 1.0, 0.0).astype(BF)
            total = total + dot(hot, values[pl.ds(j * span, span)])
        return total

    dx_own, dxv = r.xin.at[c].reshape(s.slots, s.width), r.dxv.reshape(s.slots, s.width)
    r.comb[0] = combine(dx_own, c, here.cross, zero_rows)
    for copy in dx_copies:
        copy.wait_recv()
    dn2_sum = Reduce(go, here, r.rs_send, r.rs_recv)
    dn2_sum.pair(0, combine(dxv, 1 - c, here.cross, r.comb[0]))
    dn2_sum.pair(1, combine(dxv, 1 - c, here.pair, combine(dx_own, c, here.pair, zero_rows)))
    dpr_sib.wait_recv()
    dpr_copies = [go.to(r.dprf.at[here.ring_t(k)], r.dprz.at[k - 1], (dp, here.ring_t(k))) for k in range(1, nt)]
    dn2_sum.across(combine(dxv, 1 - c, here.far, combine(dx_own, c, here.far, zero_rows)))
    r.comb[0] = combine(dxv, 1 - c, t, combine(dx_own, c, t, zero_rows))

    for copy in ge_copies:
        copy.wait_recv()
    ge_own = r.ge.at[c]
    m_sum = Reduce(go, here, r.m_send, r.m_recv)

    def forward_sum(q):
        return combine(r.gev, 1 - c, q, combine(ge_own, c, q, zero_rows))

    m_sum.pair(0, forward_sum(here.cross))
    m_sum.pair(1, forward_sum(here.pair))
    r.comb[2] = forward_sum(here.far)
    r.gx[...] = forward_sum(t) + r.y[...]

    dprobs = r.dprf[t]
    for k, copy in enumerate(dpr_copies):
        copy.wait_recv()
        dprobs = dprobs + r.dprz[k]
    dprobs = dprobs.reshape(s.experts, s.lanes)
    probs = r.prob[...]
    dlogits = (probs * (dprobs - jnp.sum(probs * dprobs, 0, keepdims=True))).astype(BF)[:, : s.rows]
    small = r.small[...]
    gain_one = small[s.experts : s.experts + 1]
    gain_two = small[s.experts + 1 : s.experts + 2]
    grad_router = dot_tn(r.n2_all[c, t], dlogits.T).T
    dn2 = r.comb[0] + dot_tn(dlogits, small[: s.experts].astype(BF))
    dn2 = dn2_sum.total(dn2)
    middle = r.y[...]
    dy_ln, unit = norm_back(middle, gain_two, dn2)
    dgain_two = jnp.sum(dn2 * unit, 0, keepdims=True)
    dy = r.dz[...].astype(F32) + dy_ln
    r.comb[0] = dy
    da = (r.live[...] * dy).astype(BF)
    go.sent_now(o_copies)
    for q in range(nt):
        r.o_send[q] = dot(da, r.wo_all[:, q].reshape(s.width, s.heads)).astype(BF)
    do_copies = [go.to(r.o_send.at[here.ring_t(k)], r.do.at[t], (dp, here.ring_t(k))) for k in range(1, nt)]
    r.do[t] = r.o_send[t]
    for q in range(nt):
        part = dot_tn(da, r.o[q]).reshape(*r.grads.shape[:3], s.shard, s.heads)
        r.grads[:, :, :, :, (3 + q) * s.heads : (4 + q) * s.heads] = part.astype(BF)

    fa_copies, fb_copies = [], []

    def pump(j):
        first, second = in_copies[j * per : (j + 1) * per], out_copies[j * per : (j + 1) * per]
        for copy in first:
            copy.wait_recv()

        def step_a(i, carry):
            e = j * per + i
            r.win_all[e, 1 - y, x] = (r.win_all[e, 1 - y, x].astype(F32) + r.ra[e, 1 - y].astype(F32)).astype(BF)
            return carry

        lax.fori_loop(0, per, step_a, 0)
        piece = pl.ds(j * per, per)
        fa_copies.append(go.to(r.win_all.at[piece, 1 - y, x], r.fa.at[piece], here.ny))
        for copy in second:
            copy.wait_recv()

        def step_b(i, carry):
            e = j * per + i
            r.wout_all[e, y, 1 - x] = (r.wout_all[e, y, 1 - x].astype(F32) + r.rb[e, 1 - x].astype(F32)).astype(BF)
            return carry

        lax.fori_loop(0, per, step_b, 0)
        fb_copies.append(go.to(r.wout_all.at[piece, y, 1 - x], r.fb.at[piece], here.nx))

    for copy in do_copies:
        copy.wait_recv()
    m_sum.across(r.comb[2])
    clear(r.oimg)
    for q in range(nt):
        r.row[:, : s.heads] = r.do[q].astype(F32)
        to_image_rows(q, r.row, r.oimg)

    def attend_back(i, carry):
        block = r.qkv[i]
        queries = stack_heads(block[:, : s.heads], masks)
        grads = stack_heads(r.oimg[i].astype(BF), masks)
        probs = r.p[i]
        dvalues = dot_tn(probs, grads)
        dprob = dot_nt(grads, block[:, 2 * s.heads :])
        wide = probs.astype(F32)
        both = wide * dprob
        dscore = (both - wide * jnp.sum(both, -1, keepdims=True)).astype(BF)
        dqueries = pick_heads(dot(dscore, block[:, s.heads : 2 * s.heads]), masks, s.irows)
        dkeys = dot_tn(dscore, queries)
        r.img[i, :, : s.heads] = dqueries * (1.0 / math.sqrt(HEAD_DIM))
        r.img[i, :, s.heads : 2 * s.heads] = dkeys * (1.0 / math.sqrt(HEAD_DIM))
        r.img[i, :, 2 * s.heads :] = dvalues
        return carry

    lax.fori_loop(0, s.images, attend_back, 0)
    pump(0)
    r.row[pl.ds(used, s.rows - used), :] = jnp.zeros((s.rows - used, 3 * s.heads), F32)
    for q in range(nt):
        to_block_rows(q, r.img, r.row)
        r.dqkv[q] = r.row[...].astype(BF)
    w_qkv = r.wq_all[...].reshape(s.width, 3 * s.heads)
    dn2_sum.sent()
    dn1_sum = Reduce(go, here, r.rs_send, r.rs_recv)
    dgain_one = jnp.zeros((1, s.width), F32)
    for k, q in enumerate((here.cross, here.pair, here.far, t)):
        part = dot_nt(r.dqkv[q], w_qkv)
        dgain_one = dgain_one + jnp.sum(part * r.n1[q].astype(F32), 0, keepdims=True)
        if k < 2:
            dn1_sum.pair(k, part)
        else:
            r.comb[2 * k - 3] = part
    dgain_one = dgain_one / gain_one

    pump(1)

    grad_qkv = jnp.zeros((s.width, 3 * s.heads), F32)
    for q in range(nt):
        grad_qkv = grad_qkv + dot_tn(r.n1[q], r.dqkv[q])
    grads = r.grads
    grads[:, :, :, :, : 3 * s.heads] = grad_qkv.astype(BF).reshape(*grads.shape[:3], s.shard, 3 * s.heads)
    r.sm_send[0] = jnp.concatenate(
        [grad_router, dgain_one, dgain_two, jnp.zeros((r.sm_send.shape[1] - s.experts - 2, s.width), F32)], 0
    )
    step = [go.to(grads.at[:, :, 1 - c], r.gs_recv, here.sib), go.to(r.sm_send.at[0], r.sm_recv.at[0], here.sib)]
    dn1_sum.across(r.comb[1])

    def add_small(k):
        r.sm_send[k + 1] = r.sm_send[k] + r.sm_recv[k]

    for copy in step:
        copy.wait_recv()

    def add_in(mine, came):
        return (mine.astype(F32) + came.astype(F32)).astype(BF)

    grads[:, :, c] = add_in(grads[:, :, c], r.gs_recv[...])
    add_small(0)
    step = [go.to(grads.at[:, 1 - x, c], r.gx_recv, here.nx), go.to(r.sm_send.at[1], r.sm_recv.at[1], here.nx)]
    for copy in step:
        copy.wait_recv()
    grads[:, x, c] = add_in(grads[:, x, c], r.gx_recv[...])
    add_small(1)
    step = [go.to(grads.at[1 - y, x, c], r.gy_recv, here.ny), go.to(r.sm_send.at[2], r.sm_recv.at[2], here.ny)]
    for copy in step:
        copy.wait_recv()
    add_small(2)
    summed = grads[y, x, c].astype(F32) + r.gy_recv[...].astype(F32)
    r.gqo[:, : 3 * s.heads] = summed[:, : 3 * s.heads]
    for q in range(nt):
        r.gz_send[q] = summed[:, (3 + q) * s.heads : (4 + q) * s.heads].astype(BF)
    gz_copies = [go.to(r.gz_send.at[here.ring_t(k)], r.gz_recv.at[k - 1], (dp, here.ring_t(k))) for k in range(1, nt)]
    sm_copies = [go.to(r.sm_send.at[3], r.sm_recv.at[2 + k], (dp, here.ring_t(k))) for k in range(1, nt)]
    r.out[...] = m_sum.total(r.gx[...]).astype(BF)

    dn1 = dn1_sum.total(r.comb[3])
    dx_ln, _ = norm_back(r.x[...].astype(F32), gain_one, dn1)
    r.gx[...] = r.comb[0] + dx_ln
    total = r.gz_send[t].astype(F32)
    for k, copy in enumerate(gz_copies):
        copy.wait_recv()
        total = total + r.gz_recv[k].astype(F32)
    r.gqo[:, 3 * s.heads :] = total
    total = r.sm_send[3]
    for k, copy in enumerate(sm_copies):
        copy.wait_recv()
        total = total + r.sm_recv[3 + k]
    r.gsm[...] = total

    mine = pl.ds(pl.multiple_of(c * s.shard, s.shard), s.shard)
    other = pl.ds(pl.multiple_of((1 - c) * s.shard, s.shard), s.shard)
    fin_copies = []
    parts = ((r.win_all, r.ra, y, r.fa, fa_copies), (r.wout_all, r.rb, x, r.fb, fb_copies))
    for w, (own, first, place, second, copies) in enumerate(parts):
        for j in range(2):
            copies[j].wait_recv()

            def last(i, carry, w=w, own=own, first=first, place=place, second=second, j=j):
                e = j * per + i

                def total(rows):
                    return (
                        own[e, y, x, rows, :].astype(F32)
                        + first[e, place, rows, :].astype(F32)
                        + second[e, rows, :].astype(F32)
                    )

                own[e, y, x, other, :] = total(other).astype(BF)
                r.gw[w, c, e] = total(mine).astype(BF)
                return carry

            lax.fori_loop(0, per, last, 0)
            piece = pl.ds(j * per, per)
            fin_copies.append(go.to(own.at[piece, y, x, other], r.gw.at[w, c, piece], here.sib))
    for copy in fin_copies:
        copy.wait_recv()
    go.finish()


VSPEC = pl.BlockSpec(memory_space=pltpu.VMEM)
ASPEC = pl.BlockSpec(memory_space=pl.ANY)


def shape(dims, kind):
    return jax.ShapeDtypeStruct(dims, kind)


def linked_body(
    block_input,
    gains,
    w_qkv,
    w_o,
    w_router,
    w_in,
    w_out,
    pictures_alive_per_shard,
    expert_ids,
    slot_index,
    cotangent,
):
    images, quarter, width = block_input.shape
    n_dp, n_t = lax.axis_size("dp"), lax.axis_size("tensor")
    shard, experts, ff = w_in.shape
    heads = w_qkv.shape[2]
    length = quarter * n_t
    used = images * quarter
    rows = up(used, 16)
    s = Sizes(n_dp, n_t, images, quarter, rows, up(length, 16), width, shard, heads, experts, ff, up(rows, 128))
    dp, t = lax.axis_index("dp"), lax.axis_index("tensor")

    def by_rows(values):
        return jnp.pad(values.reshape(used, width), ((0, rows - used), (0, 0)))

    x_own, dz_own = by_rows(block_input), by_rows(cotangent)
    wq = w_qkv.reshape(shard, 3 * heads)
    wo = w_o.T
    sm_rows = up(experts + 2, 16)
    small = jnp.concatenate([w_router.T, gains.T], 0)
    small = jnp.pad(small, ((0, sm_rows - experts - 2), (0, up(shard, 128) - shard)))
    win_t = w_in.transpose(1, 0, 2).reshape(2, s.half, shard, ff)
    wout_t = w_out.transpose(1, 2, 0).reshape(2, s.half, shard, ff)
    place = t * quarter + jnp.arange(quarter)
    live = (jnp.arange(images) < pictures_alive_per_shard[0])[:, None] & (place < TOK_IMG)[None, :]
    live = jnp.pad(live.astype(F32).reshape(used, 1), ((0, rows - used), (0, 0)))
    targets = jnp.where(slot_index >= 0, expert_ids * CAP + slot_index, -1)
    targets = targets.reshape(images, n_t, quarter, 2).transpose(1, 0, 2, 3).reshape(n_t, used, 2)
    targets = jnp.pad(targets, ((0, 0), (0, rows - used), (0, 0)), constant_values=-1)
    tgt_rows = jnp.pad(targets.reshape(n_t * rows, 2).T, ((0, 6), (0, 0)), constant_values=-1)

    two_y, two_x = n_dp // 4, 2
    gsm_rows = up(experts + 2, 8)
    tokens = n_t * rows
    inputs = dict(
        x=x_own, dz=dz_own, wq=wq, wo=wo, sm=small, live=live, tgt=tgt_rows, tcol=targets, win=win_t, wout=wout_t
    )
    outputs = dict(
        out=shape((rows, width), BF),
        gx=shape((rows, width), F32),
        gqo=shape((shard, 4 * heads), F32),
        gsm=shape((gsm_rows, width), F32),
        gw=shape((2, 2, s.half, shard, ff), BF),
    )
    wide = (two_y, two_x, 2 * shard, ff)
    per = s.half // 2
    scratch = dict(
        win_all=((s.half, *wide), BF),
        wout_all=((s.half, *wide), BF),
        n2_all=((2, n_t, rows, width), BF),
        prob_all=((2, n_t, experts, s.lanes), F32),
        tgt_all=((2, 8, tokens), jnp.int32),
        y=((rows, width), F32),
        prob=((experts, s.lanes), F32),
        qkv=((images, s.irows, 3 * heads), BF),
        p=((images, heads // HEAD_DIM * s.irows, s.irows), BF),
        n1=((n_t, rows, width), BF),
        o=((n_t, rows, heads), BF),
        do=((n_t, rows, heads), BF),
        wq_all=((n_dp, shard, 3 * heads), BF),
        wo_all=((n_dp, n_t, shard, heads), BF),
        wo_z=((n_t, shard, heads), BF),
        sm_all=((n_dp, *small.shape), BF),
        small=((sm_rows, width), F32),
        row=((rows, 3 * heads), F32),
        img=((images, s.irows, 3 * heads), F32),
        oimg=((images, s.irows, heads), F32),
        o_send=((n_t, rows, heads), BF),
        dqkv=((n_t, rows, 3 * heads), BF),
        pr=((2, s.half, tokens), F32),
        dpr=((2, s.half, tokens), F32),
        dprs=((2, n_t, s.half, s.lanes), F32),
        dprf=((n_t, 2, s.half, s.lanes), F32),
        dprz=((n_t - 1, 2, s.half, s.lanes), F32),
        hot=((2, CAP, tokens), BF),
        xin=((2, s.half, CAP, width), BF),
        slot=((2, s.half, tokens), F32),
        zin=((2, s.half, CAP, width), BF),
        ge=((2, s.slots, width), BF),
        dxv=((s.half, CAP, width), BF),
        gev=((s.slots, width), BF),
        comb=((n_t, rows, width), F32),
        rs_send=((n_t - 1, rows, width), BF),
        rs_recv=((n_t - 1, rows, width), BF),
        m_send=((n_t - 1, rows, width), BF),
        m_recv=((n_t - 1, rows, width), BF),
        grads=((two_y, two_x, 2, shard, 7 * heads), BF),
        gs_recv=((two_y, two_x, shard, 7 * heads), BF),
        gx_recv=((two_y, shard, 7 * heads), BF),
        gy_recv=((shard, 7 * heads), BF),
        gz_send=((n_t, shard, heads), BF),
        gz_recv=((n_t - 1, shard, heads), BF),
        sm_send=((4, gsm_rows, width), F32),
        sm_recv=((n_t + 2, gsm_rows, width), F32),
        ra=((s.half, two_y, 2 * shard, ff), BF),
        rb=((s.half, two_x, 2 * shard, ff), BF),
        fa=((s.half, 2 * shard, ff), BF),
        fb=((s.half, 2 * shard, ff), BF),
    )
    links = 160
    names = [*inputs, *outputs, *scratch, "send", "recv", "local"]
    out, gx, gqo, gsm, gw = pl.pallas_call(
        lambda *refs: block_kernel(s, names, *refs),
        out_shape=tuple(outputs.values()),
        in_specs=[VSPEC] * (len(inputs) - 2) + [ASPEC] * 2,
        out_specs=[VSPEC] * len(outputs),
        scratch_shapes=[pltpu.VMEM(dims, kind) for dims, kind in scratch.values()]
        + [pltpu.SemaphoreType.DMA((links,)), pltpu.SemaphoreType.DMA((links,)), pltpu.SemaphoreType.DMA((10,))],
        compiler_params=pltpu.CompilerParams(collective_id=1, has_side_effects=True, vmem_limit_bytes=VMEM_BYTES),
        name="block",
    )(*inputs.values())

    def by_image(values):
        return values[:used].reshape(images, quarter, width)

    gw = gw.reshape(2, experts, shard, ff)
    own_small = lax.dynamic_slice(gsm, (0, dp * shard), (gsm_rows, shard))
    return (
        by_image(out),
        by_image(gx),
        own_small[experts : experts + 2].T,
        gqo[:, : 3 * heads].reshape(shard, 3, heads),
        gqo[:, 3 * heads :].T,
        own_small[:experts].T,
        gw[0].transpose(1, 0, 2).astype(F32),
        gw[1].transpose(2, 0, 1).astype(F32),
    )


def solution(mesh):
    placed = (
        P("dp", "tensor", None),
        P("dp", None),
        P("dp", None, "tensor"),
        P("tensor", "dp"),
        P("dp", None),
        P("dp", None, "tensor"),
        P("tensor", None, "dp"),
        P("dp"),
        P("dp", None, None),
        P("dp", None, None),
        P("dp", "tensor", None),
    )
    linked = mesh.shape["dp"] == 8 and mesh.shape["tensor"] == 4
    return jax.shard_map(
        linked_body if linked else body,
        mesh=mesh,
        in_specs=placed,
        out_specs=(
            P("dp", "tensor", None),
            P("dp", "tensor", None),
            P("dp", None),
            P("dp", None, "tensor"),
            P("tensor", "dp"),
            P("dp", None),
            P("dp", None, "tensor"),
            P("tensor", None, "dp"),
        ),
        check_vma=False,
    )
```

```python
import math
from types import SimpleNamespace
from typing import NamedTuple

import jax
import jax.numpy as jnp
from jax import lax
from jax.experimental import pallas as pl
from jax.experimental.pallas import tpu as pltpu
from jax.sharding import PartitionSpec as P

HEAD_DIM = 64
TOK_IMG = 197
CAP = 192


epsilon = 1e-06
negative_fill = -1e30


def as_sent(shard):
    return jax.tree.map(lambda a: a.astype(jnp.bfloat16) if a.dtype == jnp.float32 else a, shard)


def layer_norm(values, gain):
    centre = values - jnp.mean(values, -1, keepdims=True)
    spread = jnp.mean(centre * centre, -1, keepdims=True)
    return centre * lax.rsqrt(spread + epsilon) * gain


def gelu_exact(values):
    return jax.nn.gelu(values, approximate=False)


def gate_values(logits, chosen):
    router_probs = jax.nn.softmax(logits, axis=-1)
    return jnp.einsum("re,rke->rk", router_probs, chosen)


def rows_in(values):
    return lax.all_gather(values, "tensor", axis=1, tiled=True)


def rows_out(values):
    return lax.psum_scatter(values, "tensor", scatter_dimension=1, tiled=True)


def grads_in(values):
    return jax.tree.map(
        lambda part, own: part.astype(own.dtype),
        lax.all_gather(as_sent(values), "tensor", axis=1, tiled=True),
        values,
    )


def grads_out(values):
    return lax.psum_scatter(values, "tensor", scatter_dimension=1, tiled=True)


def attention_scores(queries, keys_all, key_live, scale_factor):
    gating_logits_matrix = (
        jnp.einsum("ilhe,imhe->ihlm", queries, keys_all, preferred_element_type=jnp.float32)
        * scale_factor
    )
    return jnp.where(key_live[None, None, None, :], gating_logits_matrix, negative_fill)


def body(
    block_input,
    gains,
    w_qkv,
    w_o,
    w_router,
    w_in,
    w_out,
    pictures_alive_per_shard,
    expert_ids,
    slot_index,
    cotangent,
):
    tensor_size = lax.axis_size("tensor")
    tensor_pos = lax.axis_index("tensor")
    images, quarter, model_width = block_input.shape
    length = quarter * tensor_size
    all_rows = images * length
    own_rows = images * quarter
    start_row = tensor_pos * quarter
    experts = w_in.shape[1]
    slot_count = experts * CAP
    key_live = jnp.arange(length) < TOK_IMG
    live_all = (
        (jnp.arange(images) < pictures_alive_per_shard[0])[:, None] & key_live[None, :]
    ).astype(jnp.float32)
    live_own = lax.dynamic_slice_in_dim(live_all, start_row, quarter, 1)
    gathered = (
        lax.all_gather(gains, "dp", axis=0, tiled=True),
        lax.all_gather(w_qkv, "dp", axis=0, tiled=True),
        lax.all_gather(w_o, "dp", axis=1, tiled=True),
        lax.all_gather(w_router, "dp", axis=0, tiled=True),
        lax.all_gather(w_in, "dp", axis=0, tiled=True),
        lax.all_gather(w_out, "dp", axis=2, tiled=True),
    )
    gain_all, qkv_all, outproj_all, router_all, expin_all, expout_all = gathered
    head_cols = qkv_all.shape[2]
    local_heads = head_cols // HEAD_DIM
    scale_factor = 1.0 / math.sqrt(HEAD_DIM)
    gain_one = gain_all[:, 0].astype(jnp.float32)
    gain_two = gain_all[:, 1].astype(jnp.float32)
    x_float = block_input.astype(jnp.float32)
    normed = layer_norm(x_float, gain_one).astype(jnp.bfloat16)
    normed_all = rows_in(normed).reshape(all_rows, model_width)
    project = jnp.einsum(
        "rd,djc->rjc", normed_all, qkv_all, preferred_element_type=jnp.float32
    ).astype(jnp.bfloat16)
    queries = project[:, 0].reshape(images, length, local_heads, HEAD_DIM)
    keys_all = project[:, 1].reshape(images, length, local_heads, HEAD_DIM)
    values_all = project[:, 2].reshape(images, length, local_heads, HEAD_DIM)
    masked = attention_scores(queries, keys_all, key_live, scale_factor)
    top_score = jnp.max(masked, -1, keepdims=True)
    expd = jnp.exp(masked - top_score)
    total = jnp.sum(expd, -1, keepdims=True)
    att_probs = expd / total
    log_total = top_score + jnp.log(total)
    attended = jnp.einsum(
        "ihlm,imhe->ilhe",
        att_probs.astype(jnp.bfloat16),
        values_all,
        preferred_element_type=jnp.float32,
    )
    attended = attended.astype(jnp.bfloat16).reshape(all_rows, head_cols)
    branch_part = jnp.dot(attended, outproj_all, preferred_element_type=jnp.float32).reshape(
        images, length, model_width
    )
    middle = x_float + live_own[:, :, None] * rows_out(branch_part)
    normed_two = layer_norm(middle, gain_two).astype(jnp.bfloat16)
    normed_two_all = rows_in(normed_two).reshape(all_rows, model_width)
    own_flat = normed_two.reshape(own_rows, model_width)
    expert_range = jnp.arange(experts)
    own_ids = lax.dynamic_slice_in_dim(expert_ids, start_row, quarter, 1).reshape(own_rows, 2)
    chosen = (own_ids[:, :, None] == expert_range[None, None, :]).astype(jnp.float32)
    targets = jnp.where(slot_index >= 0, expert_ids * CAP + slot_index, -1).reshape(all_rows, 2)
    slot_ids = jnp.arange(slot_count)
    first_hot = (targets[:, 0:1] == slot_ids[None, :]).astype(jnp.bfloat16)
    second_hot = (targets[:, 1:2] == slot_ids[None, :]).astype(jnp.bfloat16)
    dispatched = jnp.einsum(
        "rs,rd->sd", first_hot, normed_two_all, preferred_element_type=jnp.float32
    )
    dispatched = dispatched + jnp.einsum(
        "rs,rd->sd", second_hot, normed_two_all, preferred_element_type=jnp.float32
    )
    dispatched = dispatched.astype(jnp.bfloat16).reshape(experts, CAP, model_width)
    hidden = jnp.einsum("ecd,def->ecf", dispatched, expin_all, preferred_element_type=jnp.float32)
    active = gelu_exact(hidden).astype(jnp.bfloat16)
    expert_part = jnp.einsum("ecf,fed->ecd", active, expout_all, preferred_element_type=jnp.float32)
    expert_part = expert_part.astype(jnp.bfloat16).reshape(slot_count, model_width)
    first_rows = jnp.dot(first_hot, expert_part, preferred_element_type=jnp.float32)
    second_rows = jnp.dot(second_hot, expert_part, preferred_element_type=jnp.float32)
    logits = jnp.dot(own_flat, router_all, preferred_element_type=jnp.float32)
    gates = gate_values(logits, chosen)
    first_own, second_own = rows_out(
        (
            first_rows.reshape(images, length, model_width),
            second_rows.reshape(images, length, model_width),
        )
    )
    gate_grid = gates.reshape(images, quarter, 2)
    output = middle + gate_grid[:, :, 0:1] * first_own + gate_grid[:, :, 1:2] * second_own
    grad_output = cotangent.astype(jnp.float32)
    grad_first = (gate_grid[:, :, 0:1] * grad_output).astype(jnp.bfloat16)
    grad_second = (gate_grid[:, :, 1:2] * grad_output).astype(jnp.bfloat16)
    grad_gates = jnp.stack(
        [jnp.sum(grad_output * first_own, -1), jnp.sum(grad_output * second_own, -1)], -1
    ).reshape(own_rows, 2)
    leading_cotangent, second_back = grads_in((grad_first, grad_second))
    leading_cotangent = leading_cotangent.reshape(all_rows, model_width)
    second_back = second_back.reshape(all_rows, model_width)
    unused_gates, gate_pull = jax.vjp(lambda values: gate_values(values, chosen), logits)
    grad_logits = gate_pull(grad_gates)[0].astype(jnp.bfloat16)
    grad_router = jnp.einsum("rd,re->de", own_flat, grad_logits, preferred_element_type=jnp.float32)
    router_back = jnp.einsum(
        "re,de->rd", grad_logits, router_all, preferred_element_type=jnp.float32
    )
    grad_expert = jnp.einsum(
        "rs,rd->sd", first_hot, leading_cotangent, preferred_element_type=jnp.float32
    )
    grad_expert = grad_expert + jnp.einsum(
        "rs,rd->sd", second_hot, second_back, preferred_element_type=jnp.float32
    )
    grad_expert = grad_expert.astype(jnp.bfloat16).reshape(experts, CAP, model_width)
    grad_active = jnp.einsum(
        "ecd,fed->ecf", grad_expert, expout_all, preferred_element_type=jnp.float32
    )
    grad_expout = jnp.einsum(
        "ecf,ecd->fed", active, grad_expert, preferred_element_type=jnp.float32
    )
    unused_gelu, gelu_pull = jax.vjp(gelu_exact, hidden)
    grad_hidden = gelu_pull(grad_active)[0].astype(jnp.bfloat16)
    grad_expin = jnp.einsum(
        "ecd,ecf->def", dispatched, grad_hidden, preferred_element_type=jnp.float32
    )
    grad_dispatch = jnp.einsum(
        "ecf,def->ecd", grad_hidden, expin_all, preferred_element_type=jnp.float32
    )
    grad_dispatch = grad_dispatch.astype(jnp.bfloat16).reshape(slot_count, model_width)
    back_rows = jnp.dot(first_hot, grad_dispatch, preferred_element_type=jnp.float32)
    back_rows = back_rows + jnp.dot(second_hot, grad_dispatch, preferred_element_type=jnp.float32)
    grad_normed_two = grads_out(
        back_rows.reshape(images, length, model_width)
    ) + router_back.reshape(images, quarter, model_width)
    unused_two, norm_two_pull = jax.vjp(layer_norm, middle, gain_two)
    grad_middle_norm, grad_gain_two = norm_two_pull(grad_normed_two)
    grad_middle = grad_output + grad_middle_norm
    grad_branch = (live_own[:, :, None] * grad_middle).astype(jnp.bfloat16)
    grad_branch_all = grads_in(grad_branch).reshape(all_rows, model_width)
    grad_outproj = jnp.einsum(
        "rc,rd->cd", attended, grad_branch_all, preferred_element_type=jnp.float32
    )
    grad_attended = jnp.einsum(
        "rd,cd->rc", grad_branch_all, outproj_all, preferred_element_type=jnp.float32
    )
    grad_attended = grad_attended.astype(jnp.bfloat16).reshape(
        images, length, local_heads, HEAD_DIM
    )
    masked_again = attention_scores(queries, keys_all, key_live, scale_factor)
    probs_again = jnp.exp(masked_again - log_total)
    grad_values = jnp.einsum(
        "ihlm,ilhe->imhe",
        probs_again.astype(jnp.bfloat16),
        grad_attended,
        preferred_element_type=jnp.float32,
    )
    grad_values = grad_values.astype(jnp.bfloat16)
    grad_probs = jnp.einsum(
        "ilhe,imhe->ihlm", grad_attended, values_all, preferred_element_type=jnp.float32
    )
    grad_scores = probs_again * (grad_probs - jnp.sum(probs_again * grad_probs, -1, keepdims=True))
    grad_scores = grad_scores.astype(jnp.bfloat16)
    grad_queries = (
        jnp.einsum("ihlm,imhe->ilhe", grad_scores, keys_all, preferred_element_type=jnp.float32)
        * scale_factor
    ).astype(jnp.bfloat16)
    grad_keys = (
        jnp.einsum("ihlm,ilhe->imhe", grad_scores, queries, preferred_element_type=jnp.float32)
        * scale_factor
    ).astype(jnp.bfloat16)
    grad_project = jnp.stack([grad_queries, grad_keys, grad_values], 2).reshape(
        all_rows, 3, head_cols
    )
    grad_qkv = jnp.einsum(
        "rd,rjc->djc", normed_all, grad_project, preferred_element_type=jnp.float32
    )
    normed_back = jnp.einsum(
        "rjc,djc->rd", grad_project, qkv_all, preferred_element_type=jnp.float32
    )
    grad_normed = grads_out(normed_back.reshape(images, length, model_width))
    unused_one, norm_one_pull = jax.vjp(layer_norm, x_float, gain_one)
    grad_x_norm, grad_gain_one = norm_one_pull(grad_normed)
    grad_input = grad_middle + grad_x_norm
    router_sum, gain_sum = lax.psum(
        (grad_router, jnp.stack([grad_gain_one, grad_gain_two], 1)), "tensor"
    )
    expert_fractions = (
        lax.psum_scatter(gain_sum, "dp", scatter_dimension=0, tiled=True),
        lax.psum_scatter(grad_qkv, "dp", scatter_dimension=0, tiled=True),
        lax.psum_scatter(grad_outproj, "dp", scatter_dimension=1, tiled=True),
        lax.psum_scatter(router_sum, "dp", scatter_dimension=0, tiled=True),
        lax.psum_scatter(grad_expin, "dp", scatter_dimension=0, tiled=True),
        lax.psum_scatter(grad_expout, "dp", scatter_dimension=2, tiled=True),
    )
    return (
        output.astype(jnp.bfloat16),
        grad_input,
        expert_fractions[0],
        expert_fractions[1],
        expert_fractions[2],
        expert_fractions[3],
        expert_fractions[4],
        expert_fractions[5],
    )


MESH = pl.DeviceIdType.MESH
BF = jnp.bfloat16
F32 = jnp.float32
VMEM_BYTES = 62 << 20


class Sizes(NamedTuple):
    n_dp: int
    n_t: int
    images: int
    quarter: int
    rows: int
    irows: int
    width: int
    shard: int
    heads: int
    experts: int
    ff: int
    lanes: int

    @property
    def half(self):
        return self.experts // 2

    @property
    def slots(self):
        return self.half * CAP


def up(value, step):
    return -(-value // step) * step


def norm_parts(values):
    centre = values - jnp.mean(values, -1, keepdims=True)
    scale = lax.rsqrt(jnp.mean(centre * centre, -1, keepdims=True) + epsilon)
    return centre * scale, scale


def norm_back(values, gain, grad):
    unit, scale = norm_parts(values)
    inner = grad * gain
    mean_a = jnp.mean(inner, -1, keepdims=True)
    mean_b = jnp.mean(inner * unit, -1, keepdims=True)
    return scale * (inner - mean_a - unit * mean_b), unit


def dot(a, b):
    return jnp.dot(a, b, preferred_element_type=F32)


def dot_nt(a, b):
    return lax.dot_general(a, b, (((1,), (1,)), ((), ())), preferred_element_type=F32)


def dot_tn(a, b):
    return lax.dot_general(a, b, (((0,), (0,)), ((), ())), preferred_element_type=F32)


class Place:
    def __init__(self, s):
        self.s = s
        self.dp = lax.axis_index("dp")
        self.t = lax.axis_index("tensor")
        self.c = lax.rem(self.dp, 2)
        self.x = lax.rem(self.dp // 2, 2)
        self.y = self.dp // 4
        self.chip = self.dp // 2
        self.chip_x = self.y * 2 + (1 - self.x)
        self.chip_y = (1 - self.y) * 2 + self.x
        self.sib = (self.chip * 2 + (1 - self.c), self.t)
        self.nxy = (((1 - self.y) * 2 + 1 - self.x) * 2 + self.c, self.t)
        self.nx_other = (self.chip_x * 2 + (1 - self.c), self.t)
        self.ny_other = (self.chip_y * 2 + (1 - self.c), self.t)
        self.pair = lax.rem(self.t, 2) * (-2) + self.t + 1
        self.far = lax.rem(self.t + 2, 4)
        self.cross = lax.rem(self.pair + 2, 4)
        self.nx = (self.chip_x * 2 + self.c, self.t)
        self.ny = (self.chip_y * 2 + self.c, self.t)

    def ring_dp(self, k):
        return lax.rem(self.dp + k, self.s.n_dp)

    def ring_t(self, k):
        return lax.rem(self.t + k, self.s.n_t)

    def from_t(self, k):
        return lax.rem(self.t + self.s.n_t - k, self.s.n_t)

    def greet(self):
        barrier = pltpu.get_barrier_semaphore()
        for k in range(1, self.s.n_dp):
            pl.semaphore_signal(barrier, inc=1, device_id=(self.ring_dp(k), self.t), device_id_type=MESH)
        for k in range(1, self.s.n_t):
            pl.semaphore_signal(barrier, inc=1, device_id=(self.dp, self.ring_t(k)), device_id_type=MESH)
        pl.semaphore_wait(barrier, self.s.n_dp + self.s.n_t - 2)


class Copies:
    def __init__(self, send, recv, local):
        self.send, self.recv, self.local = send, recv, local
        self.n = 0
        self.m = 0
        self.sent = []

    def make(self, k, src, dst, device):
        return pltpu.make_async_remote_copy(
            src_ref=src,
            dst_ref=dst,
            send_sem=self.send.at[k],
            recv_sem=self.recv.at[k],
            device_id=device,
            device_id_type=MESH,
        )

    def to(self, src, dst, device):
        copy = self.make(self.n, src, dst, device)
        self.n += 1
        copy.start()
        self.sent.append(copy)
        return copy

    def here(self, src, dst):
        copy = pltpu.make_async_copy(src, dst, self.local.at[self.m])
        self.m += 1
        copy.start()
        return copy

    def reserve(self, count):
        self.n += count
        return self.n - count

    def at(self, k, src, dst, device):
        copy = self.make(k, src, dst, device)
        self.sent.append(copy)
        return copy

    def start_at(self, k, src, dst, device):
        self.make(k, src, dst, device).start()

    def sent_now(self, copies):
        for copy in copies:
            copy.wait_send()
        self.sent = [copy for copy in self.sent if not any(copy is done for done in copies)]

    def finish(self):
        for copy in self.sent:
            copy.wait_send()


def pieces_of(rows):
    first = up(rows // 2, 16)
    return [pl.ds(0, first), pl.ds(first, rows - first)]


class Gather:
    def __init__(self, go, here, own, full):
        self.go, self.here, self.full = go, here, full
        self.pieces = pieces_of(here.s.rows)
        mine = full(here.t)
        self.to_far = [go.to(own.at[p], mine.at[p], (here.dp, here.far)) for p in self.pieces]
        self.to_pair = [go.to(own.at[p], mine.at[p], (here.dp, here.pair)) for p in self.pieces]

    def relay(self):
        block = self.full(self.here.far)
        self.passed = []
        for p, copy in zip(self.pieces, self.to_far):
            copy.wait_recv()
            self.passed.append(self.go.to(block.at[p], block.at[p], (self.here.dp, self.here.pair)))

    def sent_on(self):
        self.go.sent_now(self.passed)

    def wait_pair(self):
        for copy in self.to_pair:
            copy.wait_recv()

    def wait_cross(self):
        for copy in self.passed:
            copy.wait_recv()

    def share(self, block):
        return self.go.to(self.full(block), self.full(block), self.here.sib)


class PlaneGather:
    def __init__(self, go, here, full):
        self.go, self.here, self.full = go, here, full
        mine = full.at[here.y, here.x, here.c]
        self.copies = [go.to(mine, mine, device) for device in (here.nx, here.ny, here.nxy)]

    def share(self):
        for copy in self.copies:
            copy.wait_recv()
        mine = self.full.at[:, :, self.here.c]
        self.shared = self.go.to(mine, mine, self.here.sib)

    def wait(self):
        self.shared.wait_recv()


class Reduce:
    def __init__(self, go, here, send, recv):
        self.go, self.here, self.send, self.recv = go, here, send, recv
        self.pieces = pieces_of(here.s.rows)
        self.copies = [[], [], []]

    def put(self, k, p, device):
        self.copies[k].append(self.go.to(self.send.at[k, p], self.recv.at[k, p], (self.here.dp, device)))

    def pair(self, k, value):
        self.send[k] = value.astype(BF)
        for p in self.pieces:
            self.put(k, p, self.here.pair)

    def across(self, part):
        for i, p in enumerate(self.pieces):
            self.copies[0][i].wait_recv()
            self.send[2, p] = (part[p] + self.recv[0, p].astype(F32)).astype(BF)
            self.put(2, p, self.here.far)

    def sent(self):
        self.go.sent_now([copy for copies in self.copies for copy in copies])

    def total(self, part):
        for copy in self.copies[1] + self.copies[2]:
            copy.wait_recv()
        return part + self.recv[1].astype(F32) + self.recv[2].astype(F32)


def head_masks(s):
    lane = lax.broadcasted_iota(jnp.int32, (s.irows, s.heads), 1)
    return [(lane // HEAD_DIM) == h for h in range(s.heads // HEAD_DIM)]


def stack_heads(values, masks):
    zero = jnp.zeros_like(values)
    return jnp.concatenate([jnp.where(mask, values, zero) for mask in masks], 0)


def pick_heads(stacked, masks, irows):
    out = stacked[:irows]
    for h in range(1, len(masks)):
        out = jnp.where(masks[h], stacked[h * irows : (h + 1) * irows], out)
    return out


def block_kernel(s, names, *refs):
    r = SimpleNamespace(**dict(zip(names, refs)))
    here = Place(s)
    dp, t, c, x, y = here.dp, here.t, here.c, here.x, here.y
    here.greet()
    go = Copies(r.send, r.recv, r.local)
    nt = s.n_t
    length = s.quarter * nt
    used = s.images * s.quarter
    per = s.half // 2
    masks = head_masks(s)

    def to_image_rows(q, block, images):
        for i in range(s.images):
            images[i, pl.ds(q * s.quarter, s.quarter), :] = block[pl.ds(i * s.quarter, s.quarter), : images.shape[2]]

    def to_block_rows(q, images, block):
        for i in range(s.images):
            block[pl.ds(i * s.quarter, s.quarter), : images.shape[2]] = images[i, pl.ds(q * s.quarter, s.quarter), :]

    def clear(images):
        images[:, pl.ds(length, s.irows - length), :] = jnp.zeros((s.images, s.irows - length, images.shape[2]), F32)

    clear(r.img)
    clear(r.oimg)
    line = r.comb.at[3]

    rows_at = [pl.ds(i * s.quarter, s.quarter) for i in range(s.images)]

    def rows_of(images, out):
        r.tmp[pl.ds(used, s.rows - used), :] = jnp.zeros((s.rows - used, s.width), F32)
        for i, at in enumerate(rows_at):
            r.tmp[at, :] = images[i].astype(F32)
        out[...] = r.tmp[...].astype(BF)

    wo_copies = [go.to(r.wo, r.wo_z.at[t], (dp, here.ring_t(k))) for k in range(1, nt)]
    keep_wo = go.here(r.wo, r.wo_z.at[t])
    pack_own = r.pack.at[y, x, c]
    cols = 3 * s.shard
    for k in range(3):
        pack_own[pl.ds(k * s.shard, s.shard), :] = r.wq[k]
    pack_own[pl.ds(cols, s.experts), : s.shard] = r.wr[...]
    gains = jnp.concatenate([r.gains[...].astype(F32), jnp.zeros((14, s.shard), F32)], 0)
    pack_own[pl.ds(cols + s.experts, 16), : s.shard] = gains.astype(BF)
    packs = PlaneGather(go, here, r.pack)
    rows_of(r.x_in, r.x)
    x_blocks = Gather(go, here, r.x, lambda block: r.n1.at[block])
    rows_of(r.dz_in, r.dz)

    def spread(shard, full):
        to = full.at[:, y, x, pl.ds(pl.multiple_of(c * s.shard, s.shard), s.shard)]
        half, rest = shard.at[c], shard.at[1 - c]
        from_x = [go.to(half, to, here.nx), go.to(rest, to, here.nx_other)]
        from_y = [go.to(half, to, here.ny), go.to(rest, to, here.ny_other)]
        return from_x, from_y, go.to(rest, to, here.sib), go.here(half, to)

    in_x, in_y, in_sib, keep_in = spread(r.win, r.win_all)
    tgt_copy = go.to(r.tgt, r.tgt_all.at[c], here.sib)
    keep_tgt = go.here(r.tgt, r.tgt_all.at[c])

    def dz_block(block):
        return r.ge.at[c, pl.ds(pl.multiple_of(block * s.rows, 16), s.rows)]

    dz_sib = go.to(r.dz, dz_block(t), here.sib)
    keep_dz = go.here(r.dz, dz_block(t))

    keep_wo.wait()
    for copy in wo_copies:
        copy.wait_recv()
    r.wo_all[y, x, c] = r.wo_z[...]
    wos = PlaneGather(go, here, r.wo_all)
    packs.share()
    packs.wait()
    small = jnp.concatenate(
        [r.pack[k // 4, k // 2 % 2, k % 2, cols:, : s.shard].astype(F32) for k in range(s.n_dp)], 1
    )
    r.small[...] = small
    gain_one = small[s.experts : s.experts + 1]
    gain_two = small[s.experts + 1 : s.experts + 2]

    def qkv_weights(k):
        return r.pack[:, :, :, k * s.shard : (k + 1) * s.shard].reshape(s.width, s.heads)

    def project(slot, values):
        unit, _ = norm_parts(values.astype(F32))
        normed = (unit * gain_one).astype(BF)
        r.n1[slot] = normed
        weights = jnp.concatenate([qkv_weights(k) for k in range(3)], 1)
        r.comb[slot, :, : 3 * s.heads] = dot(normed, weights)

    project(t, r.x[...])
    x_blocks.relay()
    out_x, out_y, out_sib, keep_out = spread(r.wout, r.wout_all)
    x_blocks.wait_pair()
    project(here.pair, r.n1[here.pair])
    x_blocks.sent_on()
    project(here.far, r.n1[here.far])
    x_blocks.wait_cross()
    project(here.cross, r.n1[here.cross])
    wos.share()
    dz_blocks = Gather(go, here, r.dz, dz_block)

    low_half, high_half = pl.ds(0, per), pl.ds(per, per)

    def pass_on(full, by_x, by_y):
        for copy in by_x:
            copy.wait_recv()
        from_x = full.at[low_half, y, 1 - x]
        on_y = go.to(from_x, from_x, here.ny)
        for copy in by_y:
            copy.wait_recv()
        from_y = full.at[high_half, 1 - y, x]
        return on_y, go.to(from_y, from_y, here.nx)

    in_on = pass_on(r.win_all, in_x, in_y)
    for q in range(nt):
        to_image_rows(q, r.comb.at[q], r.img)

    def attend(i, carry):
        block = r.img[i].astype(BF)
        r.qkv[i] = block
        queries = stack_heads(block[:, : s.heads], masks)
        scores = dot_nt(queries, block[:, s.heads : 2 * s.heads]) * (1.0 / math.sqrt(HEAD_DIM))
        key = lax.broadcasted_iota(jnp.int32, scores.shape, 1)
        scores = jnp.where(key < TOK_IMG, scores, negative_fill)
        expd = jnp.exp(scores - jnp.max(scores, -1, keepdims=True))
        probs = (expd / jnp.sum(expd, -1, keepdims=True)).astype(BF)
        r.p[i] = probs
        r.oimg[i] = pick_heads(dot(probs, block[:, 2 * s.heads :]), masks, s.irows)
        return carry

    lax.fori_loop(0, s.images, attend, 0)
    line[pl.ds(used, s.rows - used), :] = jnp.zeros((s.rows - used, s.width), F32)
    for q in range(nt):
        to_block_rows(q, r.oimg, line)
        r.o_send[q] = line[:, : s.heads].astype(BF)
    o_copies = [go.to(r.o_send.at[here.ring_t(k)], r.o.at[t], (dp, here.ring_t(k))) for k in range(1, nt)]
    r.o[t] = r.o_send[t]
    dz_blocks.relay()
    wos.wait()
    for copy in o_copies:
        copy.wait_recv()
    branch = jnp.zeros((s.rows, s.width), F32)
    for q in range(nt):
        branch = branch + dot_nt(r.o[q], r.wo_all[:, :, :, q].reshape(s.width, s.heads))
    row = lax.broadcasted_iota(jnp.int32, (s.rows, 1), 0)
    place = t * s.quarter + row
    for _ in range(1, s.images):
        place = jnp.where(place >= t * s.quarter + s.quarter, place - s.quarter, place)
    live = jnp.where((row < r.alive[0] * s.quarter) & (place < TOK_IMG) & (row < used), 1.0, 0.0)
    r.live[...] = live
    middle = r.x[...].astype(F32) + live * branch
    r.y[...] = middle
    unit, _ = norm_parts(middle)
    normed_two = (unit * gain_two).astype(BF)
    n2_own = r.n2_all.at[c, t]
    n2_own[...] = normed_two
    n2_sib = go.to(n2_own, n2_own, here.sib)
    n2_blocks = Gather(go, here, n2_own, lambda block: r.n2_all.at[c, block])
    logits = dot_nt(small[: s.experts].astype(BF), normed_two)
    expd = jnp.exp(logits - jnp.max(logits, 0, keepdims=True))
    r.prob[...] = jnp.zeros((s.experts, s.lanes), F32)
    r.prob[:, : s.rows] = expd / jnp.sum(expd, 0, keepdims=True)
    r.prob_all[c, t] = r.prob[...]
    pr_sib = go.to(r.prob, r.prob_all.at[c, t], here.sib)
    pr_copies = [go.to(r.prob, r.prob_all.at[c, t], (dp, here.ring_t(k))) for k in range(1, nt)]

    out_on = pass_on(r.wout_all, out_x, out_y)
    n2_blocks.relay()
    on_n2 = [n2_blocks.share(here.far)]
    on_dz = [dz_blocks.share(here.far)]
    dz_blocks.wait_pair()
    on_dz.append(dz_blocks.share(here.pair))
    dz_blocks.wait_cross()
    on_dz.append(dz_blocks.share(here.cross))
    n2_blocks.wait_pair()
    on_n2.append(n2_blocks.share(here.pair))
    for k, copy in enumerate(pr_copies, 1):
        copy.wait_recv()
        slot = r.prob_all.at[c, here.from_t(k)]
        on_n2.append(go.to(slot, slot, here.sib))
    keep_tgt.wait()
    keep_dz.wait()
    for copy in [tgt_copy, dz_sib] + on_dz:
        copy.wait_recv()

    tokens = nt * s.rows
    few = 2
    for q in range(2):
        first_id = (c * s.half + lax.broadcasted_iota(jnp.int32, (s.half, tokens), 0)) * CAP
        found = jnp.full((s.half, tokens), -1, jnp.int32)
        for k in range(2):
            slot = r.tgt_all[q, k : k + 1, :] - first_id
            found = jnp.where((slot >= 0) & (slot < CAP), slot, found)
        r.slot[q] = found.astype(F32)
    slot_ids = lax.broadcasted_iota(jnp.int32, (CAP, tokens), 0).astype(F32)

    def dispatch(q, j, rows, out):
        for i in range(few):
            hits = r.slot[q, pl.ds(few * j + i, 1), :] == slot_ids
            r.hot[i] = jnp.where(hits, 1.0, 0.0).astype(BF)
        found = dot(r.hot[...].reshape(few * CAP, tokens), rows)
        out[...] = found.astype(BF).reshape(out.shape)

    def dispatch_z(j, carry):
        for q in range(2):
            dispatch(q, j, r.ge[q, :tokens], r.zin.at[q, pl.ds(few * j, few)])
        return carry

    lax.fori_loop(0, s.half // few, dispatch_z, 0)
    n2_blocks.wait_cross()
    on_n2.append(n2_blocks.share(here.cross))
    keep_in.wait()
    keep_out.wait()
    for copy in [n2_sib, pr_sib, in_sib, out_sib, *in_on] + on_n2:
        copy.wait_recv()
    mine = pl.ds(pl.multiple_of(c * s.half, s.half), s.half)
    for q in range(2):
        r.pr[q] = jnp.concatenate([r.prob_all[q, k, mine][:, : s.rows] for k in range(nt)], 1)
    for copy in out_on:
        copy.wait_recv()
    go.sent_now([*in_on, *out_on, dz_sib, *dz_blocks.passed, *on_dz])
    k_in, k_out, k_dx, k_ge = (go.reserve(s.half) for _ in range(4))

    def grad_in_copy(e):
        return r.win_all.at[e, :, 1 - x], r.ra.at[e], here.nx

    def grad_out_copy(e):
        return r.wout_all.at[e, 1 - y], r.rb.at[e], here.ny

    def dx_copy(e):
        return r.xin.at[1 - c, e], r.dxv.at[e], here.sib

    def slots_of(e):
        return pl.ds(pl.multiple_of(e * CAP, CAP), CAP)

    def ge_copy(e):
        return r.ge.at[1 - c, slots_of(e)], r.gev.at[slots_of(e)], here.sib

    def expert(e):
        x_in = r.xin[:, e].reshape(2 * CAP, s.width)
        w_in = r.win_all[e].reshape(s.width, s.ff)
        w_out = r.wout_all[e].reshape(s.width, s.ff)
        hidden = dot(x_in, w_in)
        bell = jnp.exp(-0.5 * hidden * hidden)
        u = 1.0 / (1.0 + (0.3275911 / math.sqrt(2.0)) * jnp.abs(hidden))
        poly = u * (0.254829592 + u * (-0.284496736 + u * (1.421413741 + u * (-1.453152027 + u * 1.061405429))))
        tail = 0.5 * poly * bell
        phi = jnp.where(hidden >= 0, 1.0 - tail, tail)
        active = (hidden * phi).astype(BF)
        slope = phi + hidden * bell * (1.0 / math.sqrt(2.0 * math.pi))
        out = dot_nt(active, w_out).astype(BF).astype(F32)
        for q in range(2):
            hits = r.slot[q, pl.ds(e, 1), :] == slot_ids
            gate = jnp.sum(jnp.where(hits, r.pr[q, pl.ds(e, 1), :], 0.0), 1, keepdims=True)
            part = out[q * CAP : (q + 1) * CAP]
            wide = r.zin[q, e].astype(F32)
            dgate = jnp.sum(wide * part, 1, keepdims=True)
            r.dpr[q, pl.ds(e, 1), :] = jnp.sum(jnp.where(hits, dgate, 0.0), 0, keepdims=True)
            r.zin[q, e] = (gate * wide).astype(BF)
            r.ge[q, slots_of(e)] = (gate * part).astype(BF)
        grad = r.zin[:, e].reshape(2 * CAP, s.width)
        dhidden = (dot(grad, w_out) * slope).astype(BF)
        r.wout_all[e] = dot_tn(grad, active).astype(BF).reshape(r.wout_all.shape[1:])
        grad_in = dot_tn(x_in, dhidden).astype(BF)
        r.xin[:, e] = dot_nt(dhidden, w_in).astype(BF).reshape(2, CAP, s.width)
        r.win_all[e] = grad_in.reshape(r.win_all.shape[1:])

    def expert_few(j, carry):
        for q in range(2):
            dispatch(q, j, r.n2_all[q].reshape(tokens, s.width), r.xin.at[q, pl.ds(few * j, few)])
        for i in range(few):
            expert(few * j + i)
        for i in range(few):
            e = few * j + i
            for k, copy in ((k_out, grad_out_copy), (k_in, grad_in_copy), (k_dx, dx_copy), (k_ge, ge_copy)):
                go.start_at(k + e, *copy(e))
        return carry

    lax.fori_loop(0, s.half // few, expert_few, 0)
    ge_copies = [go.at(k_ge + e, *ge_copy(e)) for e in range(s.half)]
    dx_copies = [go.at(k_dx + e, *dx_copy(e)) for e in range(s.half)]
    in_copies = [go.at(k_in + e, *grad_in_copy(e)) for e in range(s.half)]
    out_copies = [go.at(k_out + e, *grad_out_copy(e)) for e in range(s.half)]

    r.dprs[...] = jnp.zeros(r.dprs.shape, F32)
    for q in range(2):
        for k in range(nt):
            r.dprs[q, k, :, : s.rows] = r.dpr[q][:, k * s.rows : (k + 1) * s.rows]
    dpr_sib = go.to(r.dprs.at[1 - c], r.dprf.at[:, c], here.sib)
    r.dprf[:, c] = r.dprs[c]
    zero_rows = jnp.zeros((s.rows, s.width), F32)
    span = 512

    def combine(values, half, q, total):
        first = r.tcol[q, :, 0:1] - half * s.slots
        second = r.tcol[q, :, 1:2] - half * s.slots
        lane = lax.broadcasted_iota(jnp.int32, (s.rows, span), 1)
        for j in range(s.slots // span):
            hot = jnp.where((first - j * span == lane) | (second - j * span == lane), 1.0, 0.0).astype(BF)
            total = total + dot(hot, values[pl.ds(j * span, span)])
        return total

    dx_own, dxv = r.xin.at[c].reshape(s.slots, s.width), r.dxv.reshape(s.slots, s.width)
    r.comb[0] = combine(dx_own, c, here.cross, zero_rows)
    for copy in dx_copies:
        copy.wait_recv()
    dn2_sum = Reduce(go, here, r.rs_send, r.rs_recv)
    dn2_sum.pair(0, combine(dxv, 1 - c, here.cross, r.comb[0]))
    dn2_sum.pair(1, combine(dxv, 1 - c, here.pair, combine(dx_own, c, here.pair, zero_rows)))
    dpr_sib.wait_recv()
    dpr_copies = [go.to(r.dprf.at[here.ring_t(k)], r.dprz.at[k - 1], (dp, here.ring_t(k))) for k in range(1, nt)]
    dn2_sum.across(combine(dxv, 1 - c, here.far, combine(dx_own, c, here.far, zero_rows)))
    r.comb[0] = combine(dxv, 1 - c, t, combine(dx_own, c, t, zero_rows))

    for copy in ge_copies:
        copy.wait_recv()
    ge_own = r.ge.at[c]
    m_sum = Reduce(go, here, r.m_send, r.m_recv)

    def forward_sum(q):
        return combine(r.gev, 1 - c, q, combine(ge_own, c, q, zero_rows))

    r.m_send[0] = forward_sum(here.cross).astype(BF)
    r.m_send[1] = forward_sum(here.pair).astype(BF)
    r.comb[2] = forward_sum(here.far)
    r.tmp[...] = forward_sum(t) + r.y[...]

    dprobs = r.dprf[t]
    for k, copy in enumerate(dpr_copies):
        copy.wait_recv()
        dprobs = dprobs + r.dprz[k]
    dprobs = dprobs.reshape(s.experts, s.lanes)
    probs = r.prob[...]
    dlogits = (probs * (dprobs - jnp.sum(probs * dprobs, 0, keepdims=True))).astype(BF)[:, : s.rows]
    small = r.small[...]
    gain_one = small[s.experts : s.experts + 1]
    gain_two = small[s.experts + 1 : s.experts + 2]
    grad_router = dot_tn(r.n2_all[c, t], dlogits.T).T
    dn2 = r.comb[0] + dot_tn(dlogits, small[: s.experts].astype(BF))
    dn2 = dn2_sum.total(dn2)
    for k in range(2):
        for p in m_sum.pieces:
            m_sum.put(k, p, here.pair)
    middle = r.y[...]
    dy_ln, unit = norm_back(middle, gain_two, dn2)
    dgain_two = jnp.sum(dn2 * unit, 0, keepdims=True)
    dy = r.dz[...].astype(F32) + dy_ln
    r.comb[0] = dy
    da = (r.live[...] * dy).astype(BF)
    go.sent_now(o_copies)
    for q in range(nt):
        r.o_send[q] = dot(da, r.wo_all[:, :, :, q].reshape(s.width, s.heads)).astype(BF)
    do_copies = [go.to(r.o_send.at[here.ring_t(k)], r.do.at[t], (dp, here.ring_t(k))) for k in range(1, nt)]
    r.do[t] = r.o_send[t]
    for q in range(nt):
        part = dot_tn(da, r.o[q]).reshape(*r.grads.shape[:3], s.shard, s.heads)
        r.grads[:, :, :, :, (3 + q) * s.heads : (4 + q) * s.heads] = part.astype(BF)

    fa_copies, fb_copies = [], []

    def pump(j):
        first, second = in_copies[j * per : (j + 1) * per], out_copies[j * per : (j + 1) * per]
        for copy in first:
            copy.wait_recv()

        def step_a(i, carry):
            e = j * per + i
            r.win_all[e, 1 - y, x] = (r.win_all[e, 1 - y, x].astype(F32) + r.ra[e, 1 - y].astype(F32)).astype(BF)
            return carry

        lax.fori_loop(0, per, step_a, 0)
        piece = pl.ds(j * per, per)
        fa_copies.append(go.to(r.win_all.at[piece, 1 - y, x], r.fa.at[piece], here.ny))
        for copy in second:
            copy.wait_recv()

        def step_b(i, carry):
            e = j * per + i
            r.wout_all[e, y, 1 - x] = (r.wout_all[e, y, 1 - x].astype(F32) + r.rb[e, 1 - x].astype(F32)).astype(BF)
            return carry

        lax.fori_loop(0, per, step_b, 0)
        fb_copies.append(go.to(r.wout_all.at[piece, y, 1 - x], r.fb.at[piece], here.nx))

    pump(0)
    for copy in do_copies:
        copy.wait_recv()
    clear(r.oimg)
    for q in range(nt):
        line[:, : s.heads] = r.do[q].astype(F32)
        to_image_rows(q, line, r.oimg)

    def attend_back(i, carry):
        block = r.qkv[i]
        queries = stack_heads(block[:, : s.heads], masks)
        grads = stack_heads(r.oimg[i].astype(BF), masks)
        probs = r.p[i]
        dvalues = dot_tn(probs, grads)
        dprob = dot_nt(grads, block[:, 2 * s.heads :])
        wide = probs.astype(F32)
        both = wide * dprob
        dscore = (both - wide * jnp.sum(both, -1, keepdims=True)).astype(BF)
        dqueries = pick_heads(dot(dscore, block[:, s.heads : 2 * s.heads]), masks, s.irows)
        dkeys = dot_tn(dscore, queries)
        r.img[i, :, : s.heads] = dqueries * (1.0 / math.sqrt(HEAD_DIM))
        r.img[i, :, s.heads : 2 * s.heads] = dkeys * (1.0 / math.sqrt(HEAD_DIM))
        r.img[i, :, 2 * s.heads :] = dvalues
        return carry

    lax.fori_loop(0, s.images, attend_back, 0)
    m_sum.across(r.comb[2])
    line[pl.ds(used, s.rows - used), :] = jnp.zeros((s.rows - used, s.width), F32)
    for q in range(nt):
        to_block_rows(q, r.img, line)
        r.dqkv[q] = line[:, : 3 * s.heads].astype(BF)
    w_qkv = jnp.concatenate([qkv_weights(k) for k in range(3)], 1)
    dn2_sum.sent()
    dn1_sum = Reduce(go, here, r.rs_send, r.rs_recv)
    dgain_one = jnp.zeros((1, s.width), F32)
    for k, q in enumerate((here.cross, here.pair, here.far, t)):
        part = dot_nt(r.dqkv[q], w_qkv)
        dgain_one = dgain_one + jnp.sum(part * r.n1[q].astype(F32), 0, keepdims=True)
        if k < 2:
            dn1_sum.pair(k, part)
        else:
            r.comb[2 * k - 3] = part
    dgain_one = dgain_one / gain_one

    pump(1)

    grad_qkv = jnp.zeros((s.width, 3 * s.heads), F32)
    for q in range(nt):
        grad_qkv = grad_qkv + dot_tn(r.n1[q], r.dqkv[q])
    grads = r.grads
    grads[:, :, :, :, : 3 * s.heads] = grad_qkv.astype(BF).reshape(*grads.shape[:3], s.shard, 3 * s.heads)
    r.sm_send[0] = jnp.concatenate(
        [grad_router, dgain_one, dgain_two, jnp.zeros((r.sm_send.shape[1] - s.experts - 2, s.width), F32)], 0
    )
    step = [go.to(grads.at[:, :, 1 - c], r.gs_recv, here.sib), go.to(r.sm_send.at[0], r.sm_recv.at[0], here.sib)]

    def add_small(k):
        r.sm_send[k + 1] = r.sm_send[k] + r.sm_recv[k]

    for copy in step:
        copy.wait_recv()

    def add_in(mine, came):
        return (mine.astype(F32) + came.astype(F32)).astype(BF)

    grads[:, :, c] = add_in(grads[:, :, c], r.gs_recv[...])
    add_small(0)
    step = [go.to(grads.at[:, 1 - x, c], r.gx_recv, here.nx), go.to(r.sm_send.at[1], r.sm_recv.at[1], here.nx)]
    dn1_sum.across(r.comb[1])
    for copy in step:
        copy.wait_recv()
    grads[:, x, c] = add_in(grads[:, x, c], r.gx_recv[...])
    add_small(1)
    step = [go.to(grads.at[1 - y, x, c], r.gy_recv, here.ny), go.to(r.sm_send.at[2], r.sm_recv.at[2], here.ny)]
    for copy in step:
        copy.wait_recv()
    add_small(2)
    summed = grads[y, x, c].astype(F32) + r.gy_recv[...].astype(F32)
    for k in range(3):
        r.gq[k] = summed[:, k * s.heads : (k + 1) * s.heads]
    for q in range(nt):
        r.gz_send[q] = summed[:, (3 + q) * s.heads : (4 + q) * s.heads].astype(BF)
    gz_copies = [go.to(r.gz_send.at[here.ring_t(k)], r.gz_recv.at[k - 1], (dp, here.ring_t(k))) for k in range(1, nt)]
    sums = r.sm_send[3]
    pieces = [jnp.where(dp == k, sums[:, k * s.shard : (k + 1) * s.shard], 0.0) for k in range(s.n_dp)]
    r.sz_send[...] = jnp.zeros(r.sz_send.shape, F32)
    r.sz_send[:, : s.shard] = sum(pieces[1:], pieces[0])
    sm_copies = [go.to(r.sz_send, r.sz_recv.at[k - 1], (dp, here.ring_t(k))) for k in range(1, nt)]
    r.tmp[...] = m_sum.total(r.tmp[...])
    for i, at in enumerate(rows_at):
        r.out[i] = r.tmp[at, :].astype(BF)

    mine = pl.ds(pl.multiple_of(c * s.shard, s.shard), s.shard)
    other = pl.ds(pl.multiple_of((1 - c) * s.shard, s.shard), s.shard)
    fin_copies = []
    parts = ((r.win_all, r.ra, y, r.fa, fa_copies, r.gwi), (r.wout_all, r.rb, x, r.fb, fb_copies, r.gwo))
    for own, first, place, second, copies, gw in parts:
        for j in range(2):
            copies[j].wait_recv()

            def last(i, carry, own=own, first=first, place=place, second=second, gw=gw, j=j):
                e = j * per + i

                def total(rows):
                    return (
                        own[e, y, x, rows, :].astype(F32)
                        + first[e, place, rows, :].astype(F32)
                        + second[e, rows, :].astype(F32)
                    )

                own[e, y, x, other, :] = total(other).astype(BF)
                gw[c, e] = total(mine).astype(BF)
                return carry

            lax.fori_loop(0, per, last, 0)
            piece = pl.ds(j * per, per)
            fin_copies.append(go.to(own.at[piece, y, x, other], gw.at[c, piece], here.sib))
    dn1 = dn1_sum.total(r.comb[3])
    dx_ln, _ = norm_back(r.x[...].astype(F32), gain_one, dn1)
    r.tmp[...] = r.comb[0] + dx_ln
    for i, at in enumerate(rows_at):
        r.gx[i] = r.tmp[at, :]
    total = r.gz_send[t].astype(F32)
    for k, copy in enumerate(gz_copies):
        copy.wait_recv()
        total = total + r.gz_recv[k].astype(F32)
    r.go[...] = total
    total = r.sz_send[...]
    for k, copy in enumerate(sm_copies):
        copy.wait_recv()
        total = total + r.sz_recv[k]
    r.gr[...] = total[: s.experts, : s.shard]
    r.gg[...] = total[s.experts : s.experts + 2, : s.shard]

    for copy in fin_copies:
        copy.wait_recv()
    go.finish()


VSPEC = pl.BlockSpec(memory_space=pltpu.VMEM)
ASPEC = pl.BlockSpec(memory_space=pl.ANY)


def shape(dims, kind):
    return jax.ShapeDtypeStruct(dims, kind)


def linked_body(
    block_input,
    gains,
    w_qkv,
    w_o,
    w_router,
    w_in,
    w_out,
    pictures_alive_per_shard,
    expert_ids,
    slot_index,
    cotangent,
):
    images, quarter, width = block_input.shape
    n_dp, n_t = lax.axis_size("dp"), lax.axis_size("tensor")
    shard, experts, ff = w_in.shape
    heads = w_qkv.shape[2]
    length = quarter * n_t
    used = images * quarter
    rows = up(used, 16)
    s = Sizes(n_dp, n_t, images, quarter, rows, up(length, 16), width, shard, heads, experts, ff, up(rows, 128))
    win_t = w_in.transpose(1, 0, 2).reshape(2, s.half, shard, ff)
    wout_t = w_out.transpose(1, 2, 0).reshape(2, s.half, shard, ff)
    targets = jnp.where(slot_index >= 0, expert_ids * CAP + slot_index, -1)
    targets = targets.reshape(images, n_t, quarter, 2).transpose(1, 0, 2, 3).reshape(n_t, used, 2)
    targets = jnp.pad(targets, ((0, 0), (0, rows - used), (0, 0)), constant_values=-1)
    tgt_rows = jnp.pad(targets.reshape(n_t * rows, 2).T, ((0, 6), (0, 0)), constant_values=-1)

    two_y, two_x = n_dp // 4, 2
    gsm_rows = up(experts + 2, 8)
    tokens = n_t * rows
    inputs = dict(
        x_in=block_input,
        dz_in=cotangent,
        wq=w_qkv.transpose(1, 0, 2),
        wo=w_o.T,
        wr=w_router.T,
        gains=gains.T,
        tgt=tgt_rows,
        tcol=targets,
        alive=pictures_alive_per_shard,
        win=win_t,
        wout=wout_t,
    )
    in_specs = {"win": ASPEC, "wout": ASPEC, "alive": pl.BlockSpec(memory_space=pltpu.SMEM)}
    outputs = dict(
        out=shape((images, quarter, width), BF),
        gx=shape((images, quarter, width), F32),
        gq=shape((3, shard, heads), F32),
        go=shape((shard, heads), F32),
        gr=shape((experts, shard), F32),
        gg=shape((2, shard), F32),
        gwi=shape((2, s.half, shard, ff), BF),
        gwo=shape((2, s.half, shard, ff), BF),
    )
    wide = (two_y, two_x, 2 * shard, ff)
    per = s.half // 2
    scratch = dict(
        win_all=((s.half, *wide), BF),
        wout_all=((s.half, *wide), BF),
        n2_all=((2, n_t, rows, width), BF),
        prob_all=((2, n_t, experts, s.lanes), F32),
        tgt_all=((2, 8, tokens), jnp.int32),
        y=((rows, width), F32),
        prob=((experts, s.lanes), F32),
        qkv=((images, s.irows, 3 * heads), BF),
        p=((images, heads // HEAD_DIM * s.irows, s.irows), BF),
        n1=((n_t, rows, width), BF),
        o=((n_t, rows, heads), BF),
        do=((n_t, rows, heads), BF),
        x=((rows, width), BF),
        dz=((rows, width), BF),
        tmp=((rows, width), F32),
        live=((rows, 1), F32),
        pack=((two_y, two_x, 2, 3 * shard + up(experts + 2, 16), heads), BF),
        wo_all=((two_y, two_x, 2, n_t, shard, heads), BF),
        wo_z=((n_t, shard, heads), BF),
        small=((up(experts + 2, 16), width), F32),
        img=((images, s.irows, 3 * heads), F32),
        oimg=((images, s.irows, heads), F32),
        o_send=((n_t, rows, heads), BF),
        dqkv=((n_t, rows, 3 * heads), BF),
        pr=((2, s.half, tokens), F32),
        dpr=((2, s.half, tokens), F32),
        dprs=((2, n_t, s.half, s.lanes), F32),
        dprf=((n_t, 2, s.half, s.lanes), F32),
        dprz=((n_t - 1, 2, s.half, s.lanes), F32),
        hot=((2, CAP, tokens), BF),
        xin=((2, s.half, CAP, width), BF),
        slot=((2, s.half, tokens), F32),
        zin=((2, s.half, CAP, width), BF),
        ge=((2, s.slots, width), BF),
        dxv=((s.half, CAP, width), BF),
        gev=((s.slots, width), BF),
        comb=((n_t, rows, width), F32),
        rs_send=((n_t - 1, rows, width), BF),
        rs_recv=((n_t - 1, rows, width), BF),
        m_send=((n_t - 1, rows, width), BF),
        m_recv=((n_t - 1, rows, width), BF),
        grads=((two_y, two_x, 2, shard, 7 * heads), BF),
        gs_recv=((two_y, two_x, shard, 7 * heads), BF),
        gx_recv=((two_y, shard, 7 * heads), BF),
        gy_recv=((shard, 7 * heads), BF),
        gz_send=((n_t, shard, heads), BF),
        gz_recv=((n_t - 1, shard, heads), BF),
        sm_send=((4, gsm_rows, width), F32),
        sm_recv=((3, gsm_rows, width), F32),
        sz_send=((gsm_rows, up(shard, 128)), F32),
        sz_recv=((n_t - 1, gsm_rows, up(shard, 128)), F32),
        ra=((s.half, two_y, 2 * shard, ff), BF),
        rb=((s.half, two_x, 2 * shard, ff), BF),
        fa=((s.half, 2 * shard, ff), BF),
        fb=((s.half, 2 * shard, ff), BF),
    )
    links = 160
    names = [*inputs, *outputs, *scratch, "send", "recv", "local"]
    out, gx, gq, grad_o, gr, gg, gwi, gwo = pl.pallas_call(
        lambda *refs: block_kernel(s, names, *refs),
        out_shape=tuple(outputs.values()),
        in_specs=[in_specs.get(name, VSPEC) for name in inputs],
        out_specs=[VSPEC] * len(outputs),
        scratch_shapes=[pltpu.VMEM(dims, kind) for dims, kind in scratch.values()]
        + [pltpu.SemaphoreType.DMA((links,)), pltpu.SemaphoreType.DMA((links,)), pltpu.SemaphoreType.DMA((10,))],
        compiler_params=pltpu.CompilerParams(collective_id=1, has_side_effects=True, vmem_limit_bytes=VMEM_BYTES),
        name="block",
    )(*inputs.values())

    return (
        out,
        gx,
        gg.T,
        gq.transpose(1, 0, 2),
        grad_o.T,
        gr.T,
        gwi.reshape(experts, shard, ff).transpose(1, 0, 2).astype(F32),
        gwo.reshape(experts, shard, ff).transpose(2, 0, 1).astype(F32),
    )


def solution(mesh):
    placed = (
        P("dp", "tensor", None),
        P("dp", None),
        P("dp", None, "tensor"),
        P("tensor", "dp"),
        P("dp", None),
        P("dp", None, "tensor"),
        P("tensor", None, "dp"),
        P("dp"),
        P("dp", None, None),
        P("dp", None, None),
        P("dp", "tensor", None),
    )
    linked = mesh.shape["dp"] == 8 and mesh.shape["tensor"] == 4
    return jax.shard_map(
        linked_body if linked else body,
        mesh=mesh,
        in_specs=placed,
        out_specs=(
            P("dp", "tensor", None),
            P("dp", "tensor", None),
            P("dp", None),
            P("dp", None, "tensor"),
            P("tensor", "dp"),
            P("dp", None),
            P("dp", None, "tensor"),
            P("tensor", None, "dp"),
        ),
        check_vma=False,
    )
```

```python
import math
from types import SimpleNamespace
from typing import NamedTuple

import jax
import jax.numpy as jnp
from jax import lax
from jax.experimental import pallas as pl
from jax.experimental.pallas import tpu as pltpu
from jax.sharding import PartitionSpec as P

HEAD_DIM = 64
TOK_IMG = 197
CAP = 192


epsilon = 1e-06
negative_fill = -1e30


def as_sent(shard):
    return jax.tree.map(lambda a: a.astype(jnp.bfloat16) if a.dtype == jnp.float32 else a, shard)


def layer_norm(values, gain):
    centre = values - jnp.mean(values, -1, keepdims=True)
    spread = jnp.mean(centre * centre, -1, keepdims=True)
    return centre * lax.rsqrt(spread + epsilon) * gain


def gelu_exact(values):
    return jax.nn.gelu(values, approximate=False)


def gate_values(logits, chosen):
    router_probs = jax.nn.softmax(logits, axis=-1)
    return jnp.einsum("re,rke->rk", router_probs, chosen)


def rows_in(values):
    return lax.all_gather(values, "tensor", axis=1, tiled=True)


def rows_out(values):
    return lax.psum_scatter(values, "tensor", scatter_dimension=1, tiled=True)


def grads_in(values):
    return jax.tree.map(
        lambda part, own: part.astype(own.dtype),
        lax.all_gather(as_sent(values), "tensor", axis=1, tiled=True),
        values,
    )


def grads_out(values):
    return lax.psum_scatter(values, "tensor", scatter_dimension=1, tiled=True)


def attention_scores(queries, keys_all, key_live, scale_factor):
    gating_logits_matrix = (
        jnp.einsum("ilhe,imhe->ihlm", queries, keys_all, preferred_element_type=jnp.float32)
        * scale_factor
    )
    return jnp.where(key_live[None, None, None, :], gating_logits_matrix, negative_fill)


def body(
    block_input,
    gains,
    w_qkv,
    w_o,
    w_router,
    w_in,
    w_out,
    pictures_alive_per_shard,
    expert_ids,
    slot_index,
    cotangent,
):
    tensor_size = lax.axis_size("tensor")
    tensor_pos = lax.axis_index("tensor")
    images, quarter, model_width = block_input.shape
    length = quarter * tensor_size
    all_rows = images * length
    own_rows = images * quarter
    start_row = tensor_pos * quarter
    experts = w_in.shape[1]
    slot_count = experts * CAP
    key_live = jnp.arange(length) < TOK_IMG
    live_all = (
        (jnp.arange(images) < pictures_alive_per_shard[0])[:, None] & key_live[None, :]
    ).astype(jnp.float32)
    live_own = lax.dynamic_slice_in_dim(live_all, start_row, quarter, 1)
    gathered = (
        lax.all_gather(gains, "dp", axis=0, tiled=True),
        lax.all_gather(w_qkv, "dp", axis=0, tiled=True),
        lax.all_gather(w_o, "dp", axis=1, tiled=True),
        lax.all_gather(w_router, "dp", axis=0, tiled=True),
        lax.all_gather(w_in, "dp", axis=0, tiled=True),
        lax.all_gather(w_out, "dp", axis=2, tiled=True),
    )
    gain_all, qkv_all, outproj_all, router_all, expin_all, expout_all = gathered
    head_cols = qkv_all.shape[2]
    local_heads = head_cols // HEAD_DIM
    scale_factor = 1.0 / math.sqrt(HEAD_DIM)
    gain_one = gain_all[:, 0].astype(jnp.float32)
    gain_two = gain_all[:, 1].astype(jnp.float32)
    x_float = block_input.astype(jnp.float32)
    normed = layer_norm(x_float, gain_one).astype(jnp.bfloat16)
    normed_all = rows_in(normed).reshape(all_rows, model_width)
    project = jnp.einsum(
        "rd,djc->rjc", normed_all, qkv_all, preferred_element_type=jnp.float32
    ).astype(jnp.bfloat16)
    queries = project[:, 0].reshape(images, length, local_heads, HEAD_DIM)
    keys_all = project[:, 1].reshape(images, length, local_heads, HEAD_DIM)
    values_all = project[:, 2].reshape(images, length, local_heads, HEAD_DIM)
    masked = attention_scores(queries, keys_all, key_live, scale_factor)
    top_score = jnp.max(masked, -1, keepdims=True)
    expd = jnp.exp(masked - top_score)
    total = jnp.sum(expd, -1, keepdims=True)
    att_probs = expd / total
    log_total = top_score + jnp.log(total)
    attended = jnp.einsum(
        "ihlm,imhe->ilhe",
        att_probs.astype(jnp.bfloat16),
        values_all,
        preferred_element_type=jnp.float32,
    )
    attended = attended.astype(jnp.bfloat16).reshape(all_rows, head_cols)
    branch_part = jnp.dot(attended, outproj_all, preferred_element_type=jnp.float32).reshape(
        images, length, model_width
    )
    middle = x_float + live_own[:, :, None] * rows_out(branch_part)
    normed_two = layer_norm(middle, gain_two).astype(jnp.bfloat16)
    normed_two_all = rows_in(normed_two).reshape(all_rows, model_width)
    own_flat = normed_two.reshape(own_rows, model_width)
    expert_range = jnp.arange(experts)
    own_ids = lax.dynamic_slice_in_dim(expert_ids, start_row, quarter, 1).reshape(own_rows, 2)
    chosen = (own_ids[:, :, None] == expert_range[None, None, :]).astype(jnp.float32)
    targets = jnp.where(slot_index >= 0, expert_ids * CAP + slot_index, -1).reshape(all_rows, 2)
    slot_ids = jnp.arange(slot_count)
    first_hot = (targets[:, 0:1] == slot_ids[None, :]).astype(jnp.bfloat16)
    second_hot = (targets[:, 1:2] == slot_ids[None, :]).astype(jnp.bfloat16)
    dispatched = jnp.einsum(
        "rs,rd->sd", first_hot, normed_two_all, preferred_element_type=jnp.float32
    )
    dispatched = dispatched + jnp.einsum(
        "rs,rd->sd", second_hot, normed_two_all, preferred_element_type=jnp.float32
    )
    dispatched = dispatched.astype(jnp.bfloat16).reshape(experts, CAP, model_width)
    hidden = jnp.einsum("ecd,def->ecf", dispatched, expin_all, preferred_element_type=jnp.float32)
    active = gelu_exact(hidden).astype(jnp.bfloat16)
    expert_part = jnp.einsum("ecf,fed->ecd", active, expout_all, preferred_element_type=jnp.float32)
    expert_part = expert_part.astype(jnp.bfloat16).reshape(slot_count, model_width)
    first_rows = jnp.dot(first_hot, expert_part, preferred_element_type=jnp.float32)
    second_rows = jnp.dot(second_hot, expert_part, preferred_element_type=jnp.float32)
    logits = jnp.dot(own_flat, router_all, preferred_element_type=jnp.float32)
    gates = gate_values(logits, chosen)
    first_own, second_own = rows_out(
        (
            first_rows.reshape(images, length, model_width),
            second_rows.reshape(images, length, model_width),
        )
    )
    gate_grid = gates.reshape(images, quarter, 2)
    output = middle + gate_grid[:, :, 0:1] * first_own + gate_grid[:, :, 1:2] * second_own
    grad_output = cotangent.astype(jnp.float32)
    grad_first = (gate_grid[:, :, 0:1] * grad_output).astype(jnp.bfloat16)
    grad_second = (gate_grid[:, :, 1:2] * grad_output).astype(jnp.bfloat16)
    grad_gates = jnp.stack(
        [jnp.sum(grad_output * first_own, -1), jnp.sum(grad_output * second_own, -1)], -1
    ).reshape(own_rows, 2)
    leading_cotangent, second_back = grads_in((grad_first, grad_second))
    leading_cotangent = leading_cotangent.reshape(all_rows, model_width)
    second_back = second_back.reshape(all_rows, model_width)
    unused_gates, gate_pull = jax.vjp(lambda values: gate_values(values, chosen), logits)
    grad_logits = gate_pull(grad_gates)[0].astype(jnp.bfloat16)
    grad_router = jnp.einsum("rd,re->de", own_flat, grad_logits, preferred_element_type=jnp.float32)
    router_back = jnp.einsum(
        "re,de->rd", grad_logits, router_all, preferred_element_type=jnp.float32
    )
    grad_expert = jnp.einsum(
        "rs,rd->sd", first_hot, leading_cotangent, preferred_element_type=jnp.float32
    )
    grad_expert = grad_expert + jnp.einsum(
        "rs,rd->sd", second_hot, second_back, preferred_element_type=jnp.float32
    )
    grad_expert = grad_expert.astype(jnp.bfloat16).reshape(experts, CAP, model_width)
    grad_active = jnp.einsum(
        "ecd,fed->ecf", grad_expert, expout_all, preferred_element_type=jnp.float32
    )
    grad_expout = jnp.einsum(
        "ecf,ecd->fed", active, grad_expert, preferred_element_type=jnp.float32
    )
    unused_gelu, gelu_pull = jax.vjp(gelu_exact, hidden)
    grad_hidden = gelu_pull(grad_active)[0].astype(jnp.bfloat16)
    grad_expin = jnp.einsum(
        "ecd,ecf->def", dispatched, grad_hidden, preferred_element_type=jnp.float32
    )
    grad_dispatch = jnp.einsum(
        "ecf,def->ecd", grad_hidden, expin_all, preferred_element_type=jnp.float32
    )
    grad_dispatch = grad_dispatch.astype(jnp.bfloat16).reshape(slot_count, model_width)
    back_rows = jnp.dot(first_hot, grad_dispatch, preferred_element_type=jnp.float32)
    back_rows = back_rows + jnp.dot(second_hot, grad_dispatch, preferred_element_type=jnp.float32)
    grad_normed_two = grads_out(
        back_rows.reshape(images, length, model_width)
    ) + router_back.reshape(images, quarter, model_width)
    unused_two, norm_two_pull = jax.vjp(layer_norm, middle, gain_two)
    grad_middle_norm, grad_gain_two = norm_two_pull(grad_normed_two)
    grad_middle = grad_output + grad_middle_norm
    grad_branch = (live_own[:, :, None] * grad_middle).astype(jnp.bfloat16)
    grad_branch_all = grads_in(grad_branch).reshape(all_rows, model_width)
    grad_outproj = jnp.einsum(
        "rc,rd->cd", attended, grad_branch_all, preferred_element_type=jnp.float32
    )
    grad_attended = jnp.einsum(
        "rd,cd->rc", grad_branch_all, outproj_all, preferred_element_type=jnp.float32
    )
    grad_attended = grad_attended.astype(jnp.bfloat16).reshape(
        images, length, local_heads, HEAD_DIM
    )
    masked_again = attention_scores(queries, keys_all, key_live, scale_factor)
    probs_again = jnp.exp(masked_again - log_total)
    grad_values = jnp.einsum(
        "ihlm,ilhe->imhe",
        probs_again.astype(jnp.bfloat16),
        grad_attended,
        preferred_element_type=jnp.float32,
    )
    grad_values = grad_values.astype(jnp.bfloat16)
    grad_probs = jnp.einsum(
        "ilhe,imhe->ihlm", grad_attended, values_all, preferred_element_type=jnp.float32
    )
    grad_scores = probs_again * (grad_probs - jnp.sum(probs_again * grad_probs, -1, keepdims=True))
    grad_scores = grad_scores.astype(jnp.bfloat16)
    grad_queries = (
        jnp.einsum("ihlm,imhe->ilhe", grad_scores, keys_all, preferred_element_type=jnp.float32)
        * scale_factor
    ).astype(jnp.bfloat16)
    grad_keys = (
        jnp.einsum("ihlm,ilhe->imhe", grad_scores, queries, preferred_element_type=jnp.float32)
        * scale_factor
    ).astype(jnp.bfloat16)
    grad_project = jnp.stack([grad_queries, grad_keys, grad_values], 2).reshape(
        all_rows, 3, head_cols
    )
    grad_qkv = jnp.einsum(
        "rd,rjc->djc", normed_all, grad_project, preferred_element_type=jnp.float32
    )
    normed_back = jnp.einsum(
        "rjc,djc->rd", grad_project, qkv_all, preferred_element_type=jnp.float32
    )
    grad_normed = grads_out(normed_back.reshape(images, length, model_width))
    unused_one, norm_one_pull = jax.vjp(layer_norm, x_float, gain_one)
    grad_x_norm, grad_gain_one = norm_one_pull(grad_normed)
    grad_input = grad_middle + grad_x_norm
    router_sum, gain_sum = lax.psum(
        (grad_router, jnp.stack([grad_gain_one, grad_gain_two], 1)), "tensor"
    )
    expert_fractions = (
        lax.psum_scatter(gain_sum, "dp", scatter_dimension=0, tiled=True),
        lax.psum_scatter(grad_qkv, "dp", scatter_dimension=0, tiled=True),
        lax.psum_scatter(grad_outproj, "dp", scatter_dimension=1, tiled=True),
        lax.psum_scatter(router_sum, "dp", scatter_dimension=0, tiled=True),
        lax.psum_scatter(grad_expin, "dp", scatter_dimension=0, tiled=True),
        lax.psum_scatter(grad_expout, "dp", scatter_dimension=2, tiled=True),
    )
    return (
        output.astype(jnp.bfloat16),
        grad_input,
        expert_fractions[0],
        expert_fractions[1],
        expert_fractions[2],
        expert_fractions[3],
        expert_fractions[4],
        expert_fractions[5],
    )


MESH = pl.DeviceIdType.MESH
BF = jnp.bfloat16
F32 = jnp.float32
VMEM_BYTES = 62 << 20


class Sizes(NamedTuple):
    n_dp: int
    n_t: int
    images: int
    quarter: int
    rows: int
    irows: int
    width: int
    shard: int
    heads: int
    experts: int
    ff: int
    lanes: int

    @property
    def half(self):
        return self.experts // 2

    @property
    def slots(self):
        return self.half * CAP


def up(value, step):
    return -(-value // step) * step


def norm_parts(values):
    centre = values - jnp.mean(values, -1, keepdims=True)
    scale = lax.rsqrt(jnp.mean(centre * centre, -1, keepdims=True) + epsilon)
    return centre * scale, scale


def norm_back(values, gain, grad):
    unit, scale = norm_parts(values)
    inner = grad * gain
    mean_a = jnp.mean(inner, -1, keepdims=True)
    mean_b = jnp.mean(inner * unit, -1, keepdims=True)
    return scale * (inner - mean_a - unit * mean_b), unit


def dot(a, b):
    return jnp.dot(a, b, preferred_element_type=F32)


def dot_nt(a, b):
    return lax.dot_general(a, b, (((1,), (1,)), ((), ())), preferred_element_type=F32)


def dot_tn(a, b):
    return lax.dot_general(a, b, (((0,), (0,)), ((), ())), preferred_element_type=F32)


class Place:
    def __init__(self, s):
        self.s = s
        self.dp = lax.axis_index("dp")
        self.t = lax.axis_index("tensor")
        self.c = lax.rem(self.dp, 2)
        self.x = lax.rem(self.dp // 2, 2)
        self.y = self.dp // 4
        self.chip = self.dp // 2
        self.chip_x = self.y * 2 + (1 - self.x)
        self.chip_y = (1 - self.y) * 2 + self.x
        self.sib = (self.chip * 2 + (1 - self.c), self.t)
        self.nxy = (((1 - self.y) * 2 + 1 - self.x) * 2 + self.c, self.t)
        self.nx_other = (self.chip_x * 2 + (1 - self.c), self.t)
        self.ny_other = (self.chip_y * 2 + (1 - self.c), self.t)
        self.pair = lax.rem(self.t, 2) * (-2) + self.t + 1
        self.far = lax.rem(self.t + 2, 4)
        self.cross = lax.rem(self.pair + 2, 4)
        self.nx = (self.chip_x * 2 + self.c, self.t)
        self.ny = (self.chip_y * 2 + self.c, self.t)

    def ring_dp(self, k):
        return lax.rem(self.dp + k, self.s.n_dp)

    def ring_t(self, k):
        return lax.rem(self.t + k, self.s.n_t)

    def from_t(self, k):
        return lax.rem(self.t + self.s.n_t - k, self.s.n_t)

    def greet(self):
        barrier = pltpu.get_barrier_semaphore()
        for k in range(1, self.s.n_dp):
            pl.semaphore_signal(barrier, inc=1, device_id=(self.ring_dp(k), self.t), device_id_type=MESH)
        for k in range(1, self.s.n_t):
            pl.semaphore_signal(barrier, inc=1, device_id=(self.dp, self.ring_t(k)), device_id_type=MESH)
        return lambda: pl.semaphore_wait(barrier, self.s.n_dp + self.s.n_t - 2)


class Copies:
    def __init__(self, send, recv, local):
        self.send, self.recv, self.local = send, recv, local
        self.n = 0
        self.m = 0
        self.sent = []

    def make(self, k, src, dst, device):
        return pltpu.make_async_remote_copy(
            src_ref=src,
            dst_ref=dst,
            send_sem=self.send.at[k],
            recv_sem=self.recv.at[k],
            device_id=device,
            device_id_type=MESH,
        )

    def to(self, src, dst, device):
        copy = self.make(self.n, src, dst, device)
        self.n += 1
        copy.start()
        self.sent.append(copy)
        return copy

    def here(self, src, dst):
        copy = pltpu.make_async_copy(src, dst, self.local.at[self.m])
        self.m += 1
        copy.start()
        return copy

    def reserve(self, count):
        self.n += count
        return self.n - count

    def at(self, k, src, dst, device):
        copy = self.make(k, src, dst, device)
        self.sent.append(copy)
        return copy

    def start_at(self, k, src, dst, device):
        self.make(k, src, dst, device).start()

    def sent_now(self, copies):
        for copy in copies:
            copy.wait_send()
        self.sent = [copy for copy in self.sent if not any(copy is done for done in copies)]

    def finish(self):
        for copy in self.sent:
            copy.wait_send()


def pieces_of(rows):
    first = up(rows // 2, 16)
    return [pl.ds(0, first), pl.ds(first, rows - first)]


class Gather:
    def __init__(self, go, here, own, full):
        self.go, self.here, self.full = go, here, full
        self.pieces = pieces_of(here.s.rows)
        mine = full(here.t)
        self.to_far = [go.to(own.at[p], mine.at[p], (here.dp, here.far)) for p in self.pieces]
        self.to_pair = [go.to(own.at[p], mine.at[p], (here.dp, here.pair)) for p in self.pieces]

    def relay(self):
        block = self.full(self.here.far)
        self.passed = []
        for p, copy in zip(self.pieces, self.to_far):
            copy.wait_recv()
            self.passed.append(self.go.to(block.at[p], block.at[p], (self.here.dp, self.here.pair)))

    def sent_on(self):
        self.go.sent_now(self.passed)

    def wait_pair(self):
        for copy in self.to_pair:
            copy.wait_recv()

    def wait_cross(self):
        for copy in self.passed:
            copy.wait_recv()

    def share(self, block):
        return self.go.to(self.full(block), self.full(block), self.here.sib)


class PlaneGather:
    def __init__(self, go, here, full):
        self.go, self.here, self.full = go, here, full
        mine = full.at[here.y, here.x, here.c]
        self.copies = [go.to(mine, mine, device) for device in (here.nx, here.ny, here.nxy)]

    def share(self):
        for copy in self.copies:
            copy.wait_recv()
        mine = self.full.at[:, :, self.here.c]
        self.shared = self.go.to(mine, mine, self.here.sib)

    def wait(self):
        self.shared.wait_recv()


class Reduce:
    def __init__(self, go, here, send, recv):
        self.go, self.here, self.send, self.recv = go, here, send, recv
        self.pieces = pieces_of(here.s.rows)
        self.copies = [[], [], []]

    def put(self, k, p, device):
        self.copies[k].append(self.go.to(self.send.at[k, p], self.recv.at[k, p], (self.here.dp, device)))

    def pair(self, k, value):
        self.send[k] = value.astype(BF)
        for p in self.pieces:
            self.put(k, p, self.here.pair)

    def across(self, part):
        for i, p in enumerate(self.pieces):
            self.copies[0][i].wait_recv()
            self.send[2, p] = (part[p] + self.recv[0, p].astype(F32)).astype(BF)
            self.put(2, p, self.here.far)

    def sent(self):
        self.go.sent_now([copy for copies in self.copies for copy in copies])

    def total(self, part):
        for copy in self.copies[1] + self.copies[2]:
            copy.wait_recv()
        return part + self.recv[1].astype(F32) + self.recv[2].astype(F32)


def head_masks(s):
    lane = lax.broadcasted_iota(jnp.int32, (s.irows, s.heads), 1)
    return [(lane // HEAD_DIM) == h for h in range(s.heads // HEAD_DIM)]


def stack_heads(values, masks):
    zero = jnp.zeros_like(values)
    return jnp.concatenate([jnp.where(mask, values, zero) for mask in masks], 0)


def pick_heads(stacked, masks, irows):
    out = stacked[:irows]
    for h in range(1, len(masks)):
        out = jnp.where(masks[h], stacked[h * irows : (h + 1) * irows], out)
    return out


def block_kernel(s, names, *refs):
    r = SimpleNamespace(**dict(zip(names, refs)))
    here = Place(s)
    dp, t, c, x, y = here.dp, here.t, here.c, here.x, here.y
    all_there = here.greet()
    go = Copies(r.send, r.recv, r.local)
    nt = s.n_t
    length = s.quarter * nt
    used = s.images * s.quarter
    per = s.half // 2
    masks = head_masks(s)

    def to_image_rows(q, block, images):
        for i in range(s.images):
            images[i, pl.ds(q * s.quarter, s.quarter), :] = block[pl.ds(i * s.quarter, s.quarter), : images.shape[2]]

    def to_block_rows(q, images, block):
        for i in range(s.images):
            block[pl.ds(i * s.quarter, s.quarter), : images.shape[2]] = images[i, pl.ds(q * s.quarter, s.quarter), :]

    def clear(images):
        images[:, pl.ds(length, s.irows - length), :] = jnp.zeros((s.images, s.irows - length, images.shape[2]), F32)

    clear(r.img)
    clear(r.oimg)
    line = r.comb.at[3]

    rows_at = [pl.ds(i * s.quarter, s.quarter) for i in range(s.images)]

    def rows_of(images, out):
        r.tmp[pl.ds(used, s.rows - used), :] = jnp.zeros((s.rows - used, s.width), F32)
        for i, at in enumerate(rows_at):
            r.tmp[at, :] = images[i].astype(F32)
        out[...] = r.tmp[...].astype(BF)

    keep_wo = go.here(r.wo, r.wo_z.at[t])
    pack_own = r.pack.at[y, x, c]
    cols = 3 * s.shard
    for k in range(3):
        pack_own[pl.ds(k * s.shard, s.shard), :] = r.wq[k]
    pack_own[pl.ds(cols, s.experts), : s.shard] = r.wr[...]
    gains = jnp.concatenate([r.gains[...].astype(F32), jnp.zeros((14, s.shard), F32)], 0)
    pack_own[pl.ds(cols + s.experts, 16), : s.shard] = gains.astype(BF)
    rows_of(r.x_in, r.x)
    all_there()
    wo_copies = [go.to(r.wo, r.wo_z.at[t], (dp, here.ring_t(k))) for k in range(1, nt)]
    packs = PlaneGather(go, here, r.pack)
    x_blocks = Gather(go, here, r.x, lambda block: r.n1.at[block])
    rows_of(r.dz_in, r.dz)

    def spread(shard, full):
        to = full.at[:, y, x, pl.ds(pl.multiple_of(c * s.shard, s.shard), s.shard)]
        half, rest = shard.at[c], shard.at[1 - c]
        from_x = [go.to(half, to, here.nx), go.to(rest, to, here.nx_other)]
        from_y = [go.to(half, to, here.ny), go.to(rest, to, here.ny_other)]
        return from_x, from_y, go.to(rest, to, here.sib), go.here(half, to)

    in_x, in_y, in_sib, keep_in = spread(r.win, r.win_all)

    chosen = jnp.where(r.slots[...] >= 0, r.ids[...] * CAP + r.slots[...], -1)
    by_block = []
    for q in range(nt):
        parts = [chosen[i, :, q * s.quarter : (q + 1) * s.quarter] for i in range(s.images)]
        by_block.append(jnp.concatenate(parts + [jnp.full((2, s.rows - used), -1, jnp.int32)], 1))
        wide = jnp.concatenate([by_block[q], jnp.zeros((2, s.lanes - s.rows), jnp.int32)], 1)
        wide = jnp.concatenate([wide, jnp.zeros((6, s.lanes), jnp.int32)], 0)
        r.tcol[q] = wide.T[: s.rows, :2]
    tgt_own = r.tgt_all.at[c]
    tgt_own[:2, :] = jnp.concatenate(by_block, 1)
    tgt_copy = go.to(tgt_own, tgt_own, here.sib)

    def dz_block(block):
        return r.ge.at[c, pl.ds(pl.multiple_of(block * s.rows, 16), s.rows)]

    dz_sib = go.to(r.dz, dz_block(t), here.sib)
    keep_dz = go.here(r.dz, dz_block(t))

    keep_wo.wait()
    for copy in wo_copies:
        copy.wait_recv()
    r.wo_all[y, x, c] = r.wo_z[...]
    wos = PlaneGather(go, here, r.wo_all)
    packs.share()
    packs.wait()
    small = jnp.concatenate(
        [r.pack[k // 4, k // 2 % 2, k % 2, cols:, : s.shard].astype(F32) for k in range(s.n_dp)], 1
    )
    r.small[...] = small
    gain_one = small[s.experts : s.experts + 1]
    gain_two = small[s.experts + 1 : s.experts + 2]

    def qkv_weights(k):
        return r.pack[:, :, :, k * s.shard : (k + 1) * s.shard].reshape(s.width, s.heads)

    def project(slot, values):
        unit, _ = norm_parts(values.astype(F32))
        normed = (unit * gain_one).astype(BF)
        r.n1[slot] = normed
        weights = jnp.concatenate([qkv_weights(k) for k in range(3)], 1)
        r.comb[slot, :, : 3 * s.heads] = dot(normed, weights)

    project(t, r.x[...])
    x_blocks.relay()
    out_x, out_y, out_sib, keep_out = spread(r.wout, r.wout_all)
    x_blocks.wait_pair()
    project(here.pair, r.n1[here.pair])
    x_blocks.sent_on()
    project(here.far, r.n1[here.far])
    x_blocks.wait_cross()
    project(here.cross, r.n1[here.cross])
    dz_blocks = Gather(go, here, r.dz, dz_block)

    for q in range(nt):
        to_image_rows(q, r.comb.at[q], r.img)

    def attend(i, carry):
        block = r.img[i].astype(BF)
        r.qkv[i] = block
        queries = stack_heads(block[:, : s.heads], masks)
        scores = dot_nt(queries, block[:, s.heads : 2 * s.heads]) * (1.0 / math.sqrt(HEAD_DIM))
        key = lax.broadcasted_iota(jnp.int32, scores.shape, 1)
        scores = jnp.where(key < TOK_IMG, scores, negative_fill)
        expd = jnp.exp(scores - jnp.max(scores, -1, keepdims=True))
        probs = (expd / jnp.sum(expd, -1, keepdims=True)).astype(BF)
        r.p[i] = probs
        r.oimg[i] = pick_heads(dot(probs, block[:, 2 * s.heads :]), masks, s.irows)
        return carry

    lax.fori_loop(0, s.images, attend, 0, unroll=2)
    line[pl.ds(used, s.rows - used), :] = jnp.zeros((s.rows - used, s.width), F32)
    for q in range(nt):
        to_block_rows(q, r.oimg, line)
        r.o_send[q] = line[:, : s.heads].astype(BF)
    o_copies = [go.to(r.o_send.at[here.ring_t(k)], r.o.at[t], (dp, here.ring_t(k))) for k in range(1, nt)]
    r.o[t] = r.o_send[t]
    few = 2

    def pass_on(full, by_x, by_y):
        for copy in by_x + by_y:
            copy.wait_recv()
        copies = []
        for e in range(0, per, few):
            from_x = full.at[pl.ds(e, few), y, 1 - x]
            from_y = full.at[pl.ds(per + e, few), 1 - y, x]
            copies.append([go.to(from_x, from_x, here.ny), go.to(from_y, from_y, here.nx)])
        return copies

    in_on = pass_on(r.win_all, in_x, in_y)
    wos.share()
    dz_blocks.relay()
    on_dz = [dz_blocks.share(here.far)]
    tgt_copy.wait_recv()
    tokens = nt * s.rows
    half_rows = tokens // 2
    for q in range(2):
        first_id = (c * s.half + lax.broadcasted_iota(jnp.int32, (s.half, tokens), 0)) * CAP
        found = jnp.full((s.half, tokens), -1, jnp.int32)
        for k in range(2):
            slot = r.tgt_all[q, k : k + 1, :] - first_id
            found = jnp.where((slot >= 0) & (slot < CAP), slot, found)
        r.slot[q] = found.astype(F32)
        for h in range(2):
            r.sloth[h, q] = r.slot[q][:, h * half_rows : (h + 1) * half_rows]
    wos.wait()
    for copy in o_copies:
        copy.wait_recv()
    branch = jnp.zeros((s.rows, s.width), F32)
    for q in range(nt):
        branch = branch + dot_nt(r.o[q], r.wo_all[:, :, :, q].reshape(s.width, s.heads))
    row = lax.broadcasted_iota(jnp.int32, (s.rows, 1), 0)
    place = t * s.quarter + row
    for _ in range(1, s.images):
        place = jnp.where(place >= t * s.quarter + s.quarter, place - s.quarter, place)
    live = jnp.where((row < r.alive[0] * s.quarter) & (place < TOK_IMG) & (row < used), 1.0, 0.0)
    r.live[...] = live
    middle = r.x[...].astype(F32) + live * branch
    r.y[...] = middle
    unit, _ = norm_parts(middle)
    normed_two = (unit * gain_two).astype(BF)
    n2_own = r.n2_all.at[c, t]
    n2_own[...] = normed_two
    n2_sib = go.to(n2_own, n2_own, here.sib)
    n2_blocks = Gather(go, here, n2_own, lambda block: r.n2_all.at[c, block])
    logits = dot_nt(small[: s.experts].astype(BF), normed_two)
    expd = jnp.exp(logits - jnp.max(logits, 0, keepdims=True))
    r.prob[...] = jnp.zeros((s.experts, s.lanes), F32)
    r.prob[:, : s.rows] = expd / jnp.sum(expd, 0, keepdims=True)
    r.prob_all[c, t] = r.prob[...]
    pr_sib = go.to(r.prob, r.prob_all.at[c, t], here.sib)
    pr_copies = [go.to(r.prob, r.prob_all.at[c, t], (dp, here.ring_t(k))) for k in range(1, nt)]

    dz_blocks.wait_pair()
    dz_blocks.wait_cross()
    on_dz += [dz_blocks.share(here.pair), dz_blocks.share(here.cross)]
    keep_dz.wait()
    for copy in [dz_sib] + on_dz:
        copy.wait_recv()

    slot_ids = lax.broadcasted_iota(jnp.int32, (CAP, tokens), 0).astype(F32)

    def dispatch(q, j, rows, out):
        for i in range(few):
            hits = r.slot[q, pl.ds(few * j + i, 1), :] == slot_ids
            r.hot[i] = jnp.where(hits, 1.0, 0.0).astype(BF)
        found = dot(r.hot[...].reshape(few * CAP, tokens), rows)
        out[...] = found.astype(BF).reshape(out.shape)

    def dispatch_z(j, carry):
        for q in range(2):
            dispatch(q, j, r.ge[q, :tokens], r.zin.at[q, pl.ds(few * j, few)])
        return carry

    lax.fori_loop(0, s.half // few, dispatch_z, 0)
    n2_blocks.relay()
    out_on = pass_on(r.wout_all, out_x, out_y)
    on_n2 = [n2_blocks.share(here.far)]
    n2_blocks.wait_pair()
    on_n2.append(n2_blocks.share(here.pair))
    for k, copy in enumerate(pr_copies, 1):
        copy.wait_recv()
        slot = r.prob_all.at[c, here.from_t(k)]
        on_n2.append(go.to(slot, slot, here.sib))

    def dispatch_x(h, first):
        def step(j, carry):
            for q in range(2):
                for i in range(few):
                    hits = r.sloth[h, q, pl.ds(few * j + i, 1), :] == slot_ids[:, :half_rows]
                    r.hot[i, :, :half_rows] = jnp.where(hits, 1.0, 0.0).astype(BF)
                rows = r.n2_all[q, pl.ds(2 * h, 2)].reshape(half_rows, s.width)
                found = dot(r.hot[:, :, :half_rows].reshape(few * CAP, half_rows), rows)
                found = found.reshape(few, CAP, s.width)
                out = r.xin.at[q, pl.ds(few * j, few)]
                out[...] = (found if first else found + out[...].astype(F32)).astype(BF)
            return carry

        lax.fori_loop(0, s.half // few, step, 0)

    n2_sib.wait_recv()
    on_n2[1].wait_recv()
    dispatch_x(t // 2, True)
    n2_blocks.wait_cross()
    on_n2.append(n2_blocks.share(here.cross))
    keep_in.wait()
    keep_out.wait()
    for copy in [pr_sib, in_sib, out_sib, *in_on[0], *in_on[1], on_n2[0]] + on_n2[2:]:
        copy.wait_recv()
    mine = pl.ds(pl.multiple_of(c * s.half, s.half), s.half)
    for q in range(2):
        r.pr[q] = jnp.concatenate([r.prob_all[q, k, mine][:, : s.rows] for k in range(nt)], 1)
    dispatch_x(1 - t // 2, False)
    for copy in out_on[0]:
        copy.wait_recv()
    go.sent_now([*in_on[0], *in_on[1], *out_on[0], dz_sib, *dz_blocks.passed, *on_dz])
    k_in, k_out, k_dx, k_ge = (go.reserve(s.half) for _ in range(4))

    def grad_in_copy(e):
        return r.win_all.at[e, :, 1 - x], r.ra.at[e], here.nx

    def grad_out_copy(e):
        return r.wout_all.at[e, 1 - y], r.rb.at[e], here.ny

    def dx_copy(e):
        return r.xin.at[1 - c, e], r.dxv.at[e], here.sib

    def slots_of(e):
        return pl.ds(pl.multiple_of(e * CAP, CAP), CAP)

    def ge_copy(e):
        return r.ge.at[1 - c, slots_of(e)], r.gev.at[slots_of(e)], here.sib

    def expert(e):
        x_in = r.xin[:, e].reshape(2 * CAP, s.width)
        w_in = r.win_all[e].reshape(s.width, s.ff)
        w_out = r.wout_all[e].reshape(s.width, s.ff)
        hidden = dot(x_in, w_in)
        bell = jnp.exp(-0.5 * hidden * hidden)
        u = 1.0 / (1.0 + (0.3275911 / math.sqrt(2.0)) * jnp.abs(hidden))
        poly = u * (0.254829592 + u * (-0.284496736 + u * (1.421413741 + u * (-1.453152027 + u * 1.061405429))))
        tail = 0.5 * poly * bell
        phi = jnp.where(hidden >= 0, 1.0 - tail, tail)
        active = (hidden * phi).astype(BF)
        slope = phi + hidden * bell * (1.0 / math.sqrt(2.0 * math.pi))
        out = dot_nt(active, w_out).astype(BF).astype(F32)
        for q in range(2):
            hits = r.slot[q, pl.ds(e, 1), :] == slot_ids
            gate = jnp.sum(jnp.where(hits, r.pr[q, pl.ds(e, 1), :], 0.0), 1, keepdims=True)
            part = out[q * CAP : (q + 1) * CAP]
            wide = r.zin[q, e].astype(F32)
            dgate = jnp.sum(wide * part, 1, keepdims=True)
            r.dpr[q, pl.ds(e, 1), :] = jnp.sum(jnp.where(hits, dgate, 0.0), 0, keepdims=True)
            r.zin[q, e] = (gate * wide).astype(BF)
            r.ge[q, slots_of(e)] = (gate * part).astype(BF)
        grad = r.zin[:, e].reshape(2 * CAP, s.width)
        dhidden = (dot(grad, w_out) * slope).astype(BF)
        r.wout_all[e] = dot_tn(grad, active).astype(BF).reshape(r.wout_all.shape[1:])
        grad_in = dot_tn(x_in, dhidden).astype(BF)
        r.xin[:, e] = dot_nt(dhidden, w_in).astype(BF).reshape(2, CAP, s.width)
        r.win_all[e] = grad_in.reshape(r.win_all.shape[1:])

    def expert_few(k, carry):
        j = lax.rem(k, 2) * (per // few) + k // 2
        for i in range(few):
            expert(few * j + i)
        for i in range(few):
            e = few * j + i
            for k, copy in ((k_out, grad_out_copy), (k_in, grad_in_copy), (k_dx, dx_copy), (k_ge, ge_copy)):
                go.start_at(k + e, *copy(e))
        return carry

    lax.fori_loop(0, 2, expert_few, 0)
    for copies in out_on[1:]:
        for copy in copies:
            copy.wait_recv()
        go.sent_now(copies)
    lax.fori_loop(2, s.half // few, expert_few, 0)
    ge_copies = [go.at(k_ge + e, *ge_copy(e)) for e in range(s.half)]
    dx_copies = [go.at(k_dx + e, *dx_copy(e)) for e in range(s.half)]
    in_copies = [go.at(k_in + e, *grad_in_copy(e)) for e in range(s.half)]
    out_copies = [go.at(k_out + e, *grad_out_copy(e)) for e in range(s.half)]

    zero_rows = jnp.zeros((s.rows, s.width), F32)
    span = 512

    def combine(values, half, q, total):
        first = r.tcol[q, :, 0:1] - half * s.slots
        second = r.tcol[q, :, 1:2] - half * s.slots
        lane = lax.broadcasted_iota(jnp.int32, (s.rows, span), 1)
        for j in range(s.slots // span):
            hot = jnp.where((first - j * span == lane) | (second - j * span == lane), 1.0, 0.0).astype(BF)
            total = total + dot(hot, values[pl.ds(j * span, span)])
        return total

    dx_own, dxv = r.xin.at[c].reshape(s.slots, s.width), r.dxv.reshape(s.slots, s.width)
    r.comb[0] = combine(dx_own, c, here.cross, zero_rows)
    for copy in dx_copies:
        copy.wait_recv()
    dn2_sum = Reduce(go, here, r.rs_send, r.rs_recv)
    dn2_sum.pair(0, combine(dxv, 1 - c, here.cross, r.comb[0]))
    dn2_sum.pair(1, combine(dxv, 1 - c, here.pair, combine(dx_own, c, here.pair, zero_rows)))
    r.dprs[...] = jnp.zeros(r.dprs.shape, F32)
    for q in range(2):
        for k in range(nt):
            r.dprs[q, k, :, : s.rows] = r.dpr[q][:, k * s.rows : (k + 1) * s.rows]
    dpr_sib = go.to(r.dprs.at[1 - c], r.dprf.at[:, c], here.sib)
    r.dprf[:, c] = r.dprs[c]
    dpr_sib.wait_recv()
    r.dprb[...] = r.dprf[...].reshape(r.dprb.shape).astype(BF)
    dpr_copies = [go.to(r.dprb.at[here.ring_t(k)], r.dprz.at[k - 1], (dp, here.ring_t(k))) for k in range(1, nt)]
    dn2_sum.across(combine(dxv, 1 - c, here.far, combine(dx_own, c, here.far, zero_rows)))
    r.comb[0] = combine(dxv, 1 - c, t, combine(dx_own, c, t, zero_rows))

    for copy in ge_copies:
        copy.wait_recv()
    ge_own = r.ge.at[c]
    m_sum = Reduce(go, here, r.m_send, r.m_recv)

    def forward_sum(q):
        return combine(r.gev, 1 - c, q, combine(ge_own, c, q, zero_rows))

    r.m_send[0] = forward_sum(here.cross).astype(BF)
    r.m_send[1] = forward_sum(here.pair).astype(BF)
    r.comb[2] = forward_sum(here.far)
    r.tmp[...] = forward_sum(t) + r.y[...]

    dprobs = r.dprf[t].reshape(s.experts, s.lanes)
    for k, copy in enumerate(dpr_copies):
        copy.wait_recv()
        dprobs = dprobs + r.dprz[k].astype(F32)
    probs = r.prob[...]
    dlogits = (probs * (dprobs - jnp.sum(probs * dprobs, 0, keepdims=True))).astype(BF)[:, : s.rows]
    small = r.small[...]
    gain_one = small[s.experts : s.experts + 1]
    gain_two = small[s.experts + 1 : s.experts + 2]
    grad_router = dot_tn(r.n2_all[c, t], dlogits.T).T
    dn2 = r.comb[0] + dot_tn(dlogits, small[: s.experts].astype(BF))
    dn2 = dn2_sum.total(dn2)
    middle = r.y[...]
    dy_ln, unit = norm_back(middle, gain_two, dn2)
    dgain_two = jnp.sum(dn2 * unit, 0, keepdims=True)
    dy = r.dz[...].astype(F32) + dy_ln
    r.comb[0] = dy
    da = (r.live[...] * dy).astype(BF)
    go.sent_now(o_copies)
    for q in range(nt):
        r.o_send[q] = dot(da, r.wo_all[:, :, :, q].reshape(s.width, s.heads)).astype(BF)
    do_copies = [go.to(r.o_send.at[here.ring_t(k)], r.do.at[t], (dp, here.ring_t(k))) for k in range(1, nt)]
    for k in range(2):
        for p in m_sum.pieces:
            m_sum.put(k, p, here.pair)
    r.do[t] = r.o_send[t]
    for q in range(nt):
        part = dot_tn(da, r.o[q]).reshape(*r.grads.shape[:3], s.shard, s.heads)
        r.grads[:, :, :, :, (3 + q) * s.heads : (4 + q) * s.heads] = part.astype(BF)

    fa_copies, fb_copies = [], []

    def pump(j):
        first, second = in_copies[j * per : (j + 1) * per], out_copies[j * per : (j + 1) * per]
        for copy in first:
            copy.wait_recv()

        def step_a(i, carry):
            e = j * per + i
            r.win_all[e, 1 - y, x] = (r.win_all[e, 1 - y, x].astype(F32) + r.ra[e, 1 - y].astype(F32)).astype(BF)
            return carry

        lax.fori_loop(0, per, step_a, 0)
        piece = pl.ds(j * per, per)
        fa_copies.append(go.to(r.win_all.at[piece, 1 - y, x], r.fa.at[piece], here.ny))
        for copy in second:
            copy.wait_recv()

        def step_b(i, carry):
            e = j * per + i
            r.wout_all[e, y, 1 - x] = (r.wout_all[e, y, 1 - x].astype(F32) + r.rb[e, 1 - x].astype(F32)).astype(BF)
            return carry

        lax.fori_loop(0, per, step_b, 0)
        fb_copies.append(go.to(r.wout_all.at[piece, y, 1 - x], r.fb.at[piece], here.nx))

    pump(0)
    for copy in do_copies:
        copy.wait_recv()
    clear(r.oimg)
    for q in range(nt):
        line[:, : s.heads] = r.do[q].astype(F32)
        to_image_rows(q, line, r.oimg)

    def attend_back(i, carry):
        block = r.qkv[i]
        queries = stack_heads(block[:, : s.heads], masks)
        grads = stack_heads(r.oimg[i].astype(BF), masks)
        probs = r.p[i]
        dvalues = dot_tn(probs, grads)
        dprob = dot_nt(grads, block[:, 2 * s.heads :])
        wide = probs.astype(F32)
        both = wide * dprob
        dscore = (both - wide * jnp.sum(both, -1, keepdims=True)).astype(BF)
        dqueries = pick_heads(dot(dscore, block[:, s.heads : 2 * s.heads]), masks, s.irows)
        dkeys = dot_tn(dscore, queries)
        r.img[i, :, : s.heads] = dqueries * (1.0 / math.sqrt(HEAD_DIM))
        r.img[i, :, s.heads : 2 * s.heads] = dkeys * (1.0 / math.sqrt(HEAD_DIM))
        r.img[i, :, 2 * s.heads :] = dvalues
        return carry

    lax.fori_loop(0, s.images, attend_back, 0, unroll=2)
    line[pl.ds(used, s.rows - used), :] = jnp.zeros((s.rows - used, s.width), F32)
    for q in range(nt):
        to_block_rows(q, r.img, line)
        r.dqkv[q] = line[:, : 3 * s.heads].astype(BF)
    w_qkv = jnp.concatenate([qkv_weights(k) for k in range(3)], 1)
    dn2_sum.sent()
    dn1_sum = Reduce(go, here, r.rs_send, r.rs_recv)
    dgain_one = jnp.zeros((1, s.width), F32)
    for k, q in enumerate((here.cross, here.pair, here.far, t)):
        part = dot_nt(r.dqkv[q], w_qkv)
        dgain_one = dgain_one + jnp.sum(part * r.n1[q].astype(F32), 0, keepdims=True)
        if k < 2:
            dn1_sum.pair(k, part)
        else:
            r.comb[2 * k - 3] = part
    dgain_one = dgain_one / gain_one

    m_sum.across(r.comb[2])
    pump(1)

    grad_qkv = jnp.zeros((s.width, 3 * s.heads), F32)
    for q in range(nt):
        grad_qkv = grad_qkv + dot_tn(r.n1[q], r.dqkv[q])
    grads = r.grads
    grads[:, :, :, :, : 3 * s.heads] = grad_qkv.astype(BF).reshape(*grads.shape[:3], s.shard, 3 * s.heads)
    r.sm_send[0] = jnp.concatenate(
        [grad_router, dgain_one, dgain_two, jnp.zeros((r.sm_send.shape[1] - s.experts - 2, s.width), F32)], 0
    )
    step = [go.to(grads.at[:, :, 1 - c], r.gs_recv, here.sib), go.to(r.sm_send.at[0], r.sm_recv.at[0], here.sib)]

    def add_small(k):
        r.sm_send[k + 1] = r.sm_send[k] + r.sm_recv[k]

    for copy in step:
        copy.wait_recv()

    def add_in(mine, came):
        return (mine.astype(F32) + came.astype(F32)).astype(BF)

    grads[:, :, c] = add_in(grads[:, :, c], r.gs_recv[...])
    add_small(0)
    step = [go.to(grads.at[:, 1 - x, c], r.gx_recv, here.nx), go.to(r.sm_send.at[1], r.sm_recv.at[1], here.nx)]
    dn1_sum.across(r.comb[1])
    for copy in step:
        copy.wait_recv()
    grads[:, x, c] = add_in(grads[:, x, c], r.gx_recv[...])
    add_small(1)
    step = [go.to(grads.at[1 - y, x, c], r.gy_recv, here.ny), go.to(r.sm_send.at[2], r.sm_recv.at[2], here.ny)]
    for copy in step:
        copy.wait_recv()
    add_small(2)
    summed = grads[y, x, c].astype(F32) + r.gy_recv[...].astype(F32)
    for k in range(3):
        r.gq[k] = summed[:, k * s.heads : (k + 1) * s.heads]
    for q in range(nt):
        r.gz_send[q] = summed[:, (3 + q) * s.heads : (4 + q) * s.heads].astype(BF)
    gz_copies = [go.to(r.gz_send.at[here.ring_t(k)], r.gz_recv.at[k - 1], (dp, here.ring_t(k))) for k in range(1, nt)]
    sums = r.sm_send[3]
    pieces = [jnp.where(dp == k, sums[:, k * s.shard : (k + 1) * s.shard], 0.0) for k in range(s.n_dp)]
    r.sz_send[...] = jnp.zeros(r.sz_send.shape, F32)
    r.sz_send[:, : s.shard] = sum(pieces[1:], pieces[0])
    sm_copies = [go.to(r.sz_send, r.sz_recv.at[k - 1], (dp, here.ring_t(k))) for k in range(1, nt)]
    r.tmp[...] = m_sum.total(r.tmp[...])
    for i, at in enumerate(rows_at):
        r.out[i] = r.tmp[at, :].astype(BF)

    mine = pl.ds(pl.multiple_of(c * s.shard, s.shard), s.shard)
    other = pl.ds(pl.multiple_of((1 - c) * s.shard, s.shard), s.shard)
    fin_copies, kept = [], []
    parts = ((r.win_all, r.ra, y, r.fa, fa_copies, r.gwi), (r.wout_all, r.rb, x, r.fb, fb_copies, r.gwo))
    for own, first, place, second, copies, gw in parts:
        for j in range(2):
            copies[j].wait_recv()

            def last(i, carry, own=own, first=first, place=place, second=second, gw=gw, j=j):
                e = j * per + i

                def total(rows):
                    return (
                        own[e, y, x, rows, :].astype(F32)
                        + first[e, place, rows, :].astype(F32)
                        + second[e, rows, :].astype(F32)
                    )

                own[e, y, x, other, :] = total(other).astype(BF)
                own[e, y, x, mine, :] = total(mine).astype(BF)
                return carry

            lax.fori_loop(0, per, last, 0)
            piece = pl.ds(j * per, per)
            fin_copies.append(go.to(own.at[piece, y, x, other], gw.at[c, piece], here.sib))
            kept.append(go.here(own.at[piece, y, x, mine], gw.at[c, piece]))
    dn1 = dn1_sum.total(r.comb[3])
    dx_ln, _ = norm_back(r.x[...].astype(F32), gain_one, dn1)
    r.tmp[...] = r.comb[0] + dx_ln
    for i, at in enumerate(rows_at):
        r.gx[i] = r.tmp[at, :]
    total = r.gz_send[t].astype(F32)
    for k, copy in enumerate(gz_copies):
        copy.wait_recv()
        total = total + r.gz_recv[k].astype(F32)
    r.go[...] = total
    total = r.sz_send[...]
    for k, copy in enumerate(sm_copies):
        copy.wait_recv()
        total = total + r.sz_recv[k]
    r.gr[...] = total[: s.experts, : s.shard]
    r.gg[...] = total[s.experts : s.experts + 2, : s.shard]

    for copy in fin_copies:
        copy.wait_recv()
    for copy in kept:
        copy.wait()
    go.finish()


VSPEC = pl.BlockSpec(memory_space=pltpu.VMEM)
ASPEC = pl.BlockSpec(memory_space=pl.ANY)


def shape(dims, kind):
    return jax.ShapeDtypeStruct(dims, kind)


def linked_body(
    block_input,
    gains,
    w_qkv,
    w_o,
    w_router,
    w_in,
    w_out,
    pictures_alive_per_shard,
    expert_ids,
    slot_index,
    cotangent,
):
    images, quarter, width = block_input.shape
    n_dp, n_t = lax.axis_size("dp"), lax.axis_size("tensor")
    shard, experts, ff = w_in.shape
    heads = w_qkv.shape[2]
    length = quarter * n_t
    used = images * quarter
    rows = up(used, 16)
    s = Sizes(n_dp, n_t, images, quarter, rows, up(length, 16), width, shard, heads, experts, ff, up(rows, 128))
    win_t = w_in.transpose(1, 0, 2).reshape(2, s.half, shard, ff)
    wout_t = w_out.transpose(1, 2, 0).reshape(2, s.half, shard, ff)
    two_y, two_x = n_dp // 4, 2
    gsm_rows = up(experts + 2, 8)
    tokens = n_t * rows
    inputs = dict(
        x_in=block_input,
        dz_in=cotangent,
        wq=w_qkv.transpose(1, 0, 2),
        wo=w_o.T,
        wr=w_router.T,
        gains=gains.T,
        ids=expert_ids.transpose(0, 2, 1),
        slots=slot_index.transpose(0, 2, 1),
        alive=pictures_alive_per_shard,
        win=win_t,
        wout=wout_t,
    )
    in_specs = {"win": ASPEC, "wout": ASPEC, "alive": pl.BlockSpec(memory_space=pltpu.SMEM)}
    outputs = dict(
        out=shape((images, quarter, width), BF),
        gx=shape((images, quarter, width), F32),
        gq=shape((3, shard, heads), F32),
        go=shape((shard, heads), F32),
        gr=shape((experts, shard), F32),
        gg=shape((2, shard), F32),
        gwi=shape((2, s.half, shard, ff), BF),
        gwo=shape((2, s.half, shard, ff), BF),
    )
    wide = (two_y, two_x, 2 * shard, ff)
    per = s.half // 2
    scratch = dict(
        win_all=((s.half, *wide), BF),
        wout_all=((s.half, *wide), BF),
        n2_all=((2, n_t, rows, width), BF),
        prob_all=((2, n_t, experts, s.lanes), F32),
        tgt_all=((2, 8, tokens), jnp.int32),
        tcol=((n_t, rows, 2), jnp.int32),
        y=((rows, width), F32),
        prob=((experts, s.lanes), F32),
        qkv=((images, s.irows, 3 * heads), BF),
        p=((images, heads // HEAD_DIM * s.irows, s.irows), BF),
        n1=((n_t, rows, width), BF),
        o=((n_t, rows, heads), BF),
        do=((n_t, rows, heads), BF),
        x=((rows, width), BF),
        dz=((rows, width), BF),
        tmp=((rows, width), F32),
        live=((rows, 1), F32),
        pack=((two_y, two_x, 2, 3 * shard + up(experts + 2, 16), heads), BF),
        wo_all=((two_y, two_x, 2, n_t, shard, heads), BF),
        wo_z=((n_t, shard, heads), BF),
        small=((up(experts + 2, 16), width), F32),
        img=((images, s.irows, 3 * heads), F32),
        oimg=((images, s.irows, heads), F32),
        o_send=((n_t, rows, heads), BF),
        dqkv=((n_t, rows, 3 * heads), BF),
        pr=((2, s.half, tokens), F32),
        dpr=((2, s.half, tokens), F32),
        dprs=((2, n_t, s.half, s.lanes), F32),
        dprf=((n_t, 2, s.half, s.lanes), F32),
        dprb=((n_t, experts, s.lanes), BF),
        dprz=((n_t - 1, experts, s.lanes), BF),
        hot=((2, CAP, tokens), BF),
        xin=((2, s.half, CAP, width), BF),
        slot=((2, s.half, tokens), F32),
        sloth=((2, 2, s.half, tokens // 2), F32),
        zin=((2, s.half, CAP, width), BF),
        ge=((2, s.slots, width), BF),
        dxv=((s.half, CAP, width), BF),
        gev=((s.slots, width), BF),
        comb=((n_t, rows, width), F32),
        rs_send=((n_t - 1, rows, width), BF),
        rs_recv=((n_t - 1, rows, width), BF),
        m_send=((n_t - 1, rows, width), BF),
        m_recv=((n_t - 1, rows, width), BF),
        grads=((two_y, two_x, 2, shard, 7 * heads), BF),
        gs_recv=((two_y, two_x, shard, 7 * heads), BF),
        gx_recv=((two_y, shard, 7 * heads), BF),
        gy_recv=((shard, 7 * heads), BF),
        gz_send=((n_t, shard, heads), BF),
        gz_recv=((n_t - 1, shard, heads), BF),
        sm_send=((4, gsm_rows, width), F32),
        sm_recv=((3, gsm_rows, width), F32),
        sz_send=((gsm_rows, up(shard, 128)), F32),
        sz_recv=((n_t - 1, gsm_rows, up(shard, 128)), F32),
        ra=((s.half, two_y, 2 * shard, ff), BF),
        rb=((s.half, two_x, 2 * shard, ff), BF),
        fa=((s.half, 2 * shard, ff), BF),
        fb=((s.half, 2 * shard, ff), BF),
    )
    links = 160
    names = [*inputs, *outputs, *scratch, "send", "recv", "local"]
    out, gx, gq, grad_o, gr, gg, gwi, gwo = pl.pallas_call(
        lambda *refs: block_kernel(s, names, *refs),
        out_shape=tuple(outputs.values()),
        in_specs=[in_specs.get(name, VSPEC) for name in inputs],
        out_specs=[ASPEC if name in ("gwi", "gwo") else VSPEC for name in outputs],
        scratch_shapes=[pltpu.VMEM(dims, kind) for dims, kind in scratch.values()]
        + [pltpu.SemaphoreType.DMA((links,)), pltpu.SemaphoreType.DMA((links,)), pltpu.SemaphoreType.DMA((10,))],
        compiler_params=pltpu.CompilerParams(collective_id=1, has_side_effects=True, vmem_limit_bytes=VMEM_BYTES),
        name="block",
    )(*inputs.values())

    return (
        out,
        gx,
        gg.T,
        gq.transpose(1, 0, 2),
        grad_o.T,
        gr.T,
        lax.optimization_barrier(gwi.reshape(experts, shard, ff).transpose(1, 0, 2)).astype(F32),
        gwo.reshape(experts, shard, ff).transpose(2, 0, 1).astype(F32),
    )


def solution(mesh):
    placed = (
        P("dp", "tensor", None),
        P("dp", None),
        P("dp", None, "tensor"),
        P("tensor", "dp"),
        P("dp", None),
        P("dp", None, "tensor"),
        P("tensor", None, "dp"),
        P("dp"),
        P("dp", None, None),
        P("dp", None, None),
        P("dp", "tensor", None),
    )
    linked = mesh.shape["dp"] == 8 and mesh.shape["tensor"] == 4
    return jax.shard_map(
        linked_body if linked else body,
        mesh=mesh,
        in_specs=placed,
        out_specs=(
            P("dp", "tensor", None),
            P("dp", "tensor", None),
            P("dp", None),
            P("dp", None, "tensor"),
            P("tensor", "dp"),
            P("dp", None),
            P("dp", None, "tensor"),
            P("tensor", None, "dp"),
        ),
        check_vma=False,
    )
```

```python
import math
from types import SimpleNamespace
from typing import NamedTuple

import jax
import jax.numpy as jnp
from jax import lax
from jax.experimental import pallas as pl
from jax.experimental.pallas import tpu as pltpu
from jax.sharding import PartitionSpec as P

HEAD_DIM = 64
TOK_IMG = 197
CAP = 192


epsilon = 1e-06
negative_fill = -1e30


def as_sent(shard):
    return jax.tree.map(lambda a: a.astype(jnp.bfloat16) if a.dtype == jnp.float32 else a, shard)


def layer_norm(values, gain):
    centre = values - jnp.mean(values, -1, keepdims=True)
    spread = jnp.mean(centre * centre, -1, keepdims=True)
    return centre * lax.rsqrt(spread + epsilon) * gain


def gelu_exact(values):
    return jax.nn.gelu(values, approximate=False)


def gate_values(logits, chosen):
    router_probs = jax.nn.softmax(logits, axis=-1)
    return jnp.einsum("re,rke->rk", router_probs, chosen)


def rows_in(values):
    return lax.all_gather(values, "tensor", axis=1, tiled=True)


def rows_out(values):
    return lax.psum_scatter(values, "tensor", scatter_dimension=1, tiled=True)


def grads_in(values):
    return jax.tree.map(
        lambda part, own: part.astype(own.dtype),
        lax.all_gather(as_sent(values), "tensor", axis=1, tiled=True),
        values,
    )


def grads_out(values):
    return lax.psum_scatter(values, "tensor", scatter_dimension=1, tiled=True)


def attention_scores(queries, keys_all, key_live, scale_factor):
    gating_logits_matrix = (
        jnp.einsum("ilhe,imhe->ihlm", queries, keys_all, preferred_element_type=jnp.float32)
        * scale_factor
    )
    return jnp.where(key_live[None, None, None, :], gating_logits_matrix, negative_fill)


def body(
    block_input,
    gains,
    w_qkv,
    w_o,
    w_router,
    w_in,
    w_out,
    pictures_alive_per_shard,
    expert_ids,
    slot_index,
    cotangent,
):
    tensor_size = lax.axis_size("tensor")
    tensor_pos = lax.axis_index("tensor")
    images, quarter, model_width = block_input.shape
    length = quarter * tensor_size
    all_rows = images * length
    own_rows = images * quarter
    start_row = tensor_pos * quarter
    experts = w_in.shape[1]
    slot_count = experts * CAP
    key_live = jnp.arange(length) < TOK_IMG
    live_all = (
        (jnp.arange(images) < pictures_alive_per_shard[0])[:, None] & key_live[None, :]
    ).astype(jnp.float32)
    live_own = lax.dynamic_slice_in_dim(live_all, start_row, quarter, 1)
    gathered = (
        lax.all_gather(gains, "dp", axis=0, tiled=True),
        lax.all_gather(w_qkv, "dp", axis=0, tiled=True),
        lax.all_gather(w_o, "dp", axis=1, tiled=True),
        lax.all_gather(w_router, "dp", axis=0, tiled=True),
        lax.all_gather(w_in, "dp", axis=0, tiled=True),
        lax.all_gather(w_out, "dp", axis=2, tiled=True),
    )
    gain_all, qkv_all, outproj_all, router_all, expin_all, expout_all = gathered
    head_cols = qkv_all.shape[2]
    local_heads = head_cols // HEAD_DIM
    scale_factor = 1.0 / math.sqrt(HEAD_DIM)
    gain_one = gain_all[:, 0].astype(jnp.float32)
    gain_two = gain_all[:, 1].astype(jnp.float32)
    x_float = block_input.astype(jnp.float32)
    normed = layer_norm(x_float, gain_one).astype(jnp.bfloat16)
    normed_all = rows_in(normed).reshape(all_rows, model_width)
    project = jnp.einsum(
        "rd,djc->rjc", normed_all, qkv_all, preferred_element_type=jnp.float32
    ).astype(jnp.bfloat16)
    queries = project[:, 0].reshape(images, length, local_heads, HEAD_DIM)
    keys_all = project[:, 1].reshape(images, length, local_heads, HEAD_DIM)
    values_all = project[:, 2].reshape(images, length, local_heads, HEAD_DIM)
    masked = attention_scores(queries, keys_all, key_live, scale_factor)
    top_score = jnp.max(masked, -1, keepdims=True)
    expd = jnp.exp(masked - top_score)
    total = jnp.sum(expd, -1, keepdims=True)
    att_probs = expd / total
    log_total = top_score + jnp.log(total)
    attended = jnp.einsum(
        "ihlm,imhe->ilhe",
        att_probs.astype(jnp.bfloat16),
        values_all,
        preferred_element_type=jnp.float32,
    )
    attended = attended.astype(jnp.bfloat16).reshape(all_rows, head_cols)
    branch_part = jnp.dot(attended, outproj_all, preferred_element_type=jnp.float32).reshape(
        images, length, model_width
    )
    middle = x_float + live_own[:, :, None] * rows_out(branch_part)
    normed_two = layer_norm(middle, gain_two).astype(jnp.bfloat16)
    normed_two_all = rows_in(normed_two).reshape(all_rows, model_width)
    own_flat = normed_two.reshape(own_rows, model_width)
    expert_range = jnp.arange(experts)
    own_ids = lax.dynamic_slice_in_dim(expert_ids, start_row, quarter, 1).reshape(own_rows, 2)
    chosen = (own_ids[:, :, None] == expert_range[None, None, :]).astype(jnp.float32)
    targets = jnp.where(slot_index >= 0, expert_ids * CAP + slot_index, -1).reshape(all_rows, 2)
    slot_ids = jnp.arange(slot_count)
    first_hot = (targets[:, 0:1] == slot_ids[None, :]).astype(jnp.bfloat16)
    second_hot = (targets[:, 1:2] == slot_ids[None, :]).astype(jnp.bfloat16)
    dispatched = jnp.einsum(
        "rs,rd->sd", first_hot, normed_two_all, preferred_element_type=jnp.float32
    )
    dispatched = dispatched + jnp.einsum(
        "rs,rd->sd", second_hot, normed_two_all, preferred_element_type=jnp.float32
    )
    dispatched = dispatched.astype(jnp.bfloat16).reshape(experts, CAP, model_width)
    hidden = jnp.einsum("ecd,def->ecf", dispatched, expin_all, preferred_element_type=jnp.float32)
    active = gelu_exact(hidden).astype(jnp.bfloat16)
    expert_part = jnp.einsum("ecf,fed->ecd", active, expout_all, preferred_element_type=jnp.float32)
    expert_part = expert_part.astype(jnp.bfloat16).reshape(slot_count, model_width)
    first_rows = jnp.dot(first_hot, expert_part, preferred_element_type=jnp.float32)
    second_rows = jnp.dot(second_hot, expert_part, preferred_element_type=jnp.float32)
    logits = jnp.dot(own_flat, router_all, preferred_element_type=jnp.float32)
    gates = gate_values(logits, chosen)
    first_own, second_own = rows_out(
        (
            first_rows.reshape(images, length, model_width),
            second_rows.reshape(images, length, model_width),
        )
    )
    gate_grid = gates.reshape(images, quarter, 2)
    output = middle + gate_grid[:, :, 0:1] * first_own + gate_grid[:, :, 1:2] * second_own
    grad_output = cotangent.astype(jnp.float32)
    grad_first = (gate_grid[:, :, 0:1] * grad_output).astype(jnp.bfloat16)
    grad_second = (gate_grid[:, :, 1:2] * grad_output).astype(jnp.bfloat16)
    grad_gates = jnp.stack(
        [jnp.sum(grad_output * first_own, -1), jnp.sum(grad_output * second_own, -1)], -1
    ).reshape(own_rows, 2)
    leading_cotangent, second_back = grads_in((grad_first, grad_second))
    leading_cotangent = leading_cotangent.reshape(all_rows, model_width)
    second_back = second_back.reshape(all_rows, model_width)
    unused_gates, gate_pull = jax.vjp(lambda values: gate_values(values, chosen), logits)
    grad_logits = gate_pull(grad_gates)[0].astype(jnp.bfloat16)
    grad_router = jnp.einsum("rd,re->de", own_flat, grad_logits, preferred_element_type=jnp.float32)
    router_back = jnp.einsum(
        "re,de->rd", grad_logits, router_all, preferred_element_type=jnp.float32
    )
    grad_expert = jnp.einsum(
        "rs,rd->sd", first_hot, leading_cotangent, preferred_element_type=jnp.float32
    )
    grad_expert = grad_expert + jnp.einsum(
        "rs,rd->sd", second_hot, second_back, preferred_element_type=jnp.float32
    )
    grad_expert = grad_expert.astype(jnp.bfloat16).reshape(experts, CAP, model_width)
    grad_active = jnp.einsum(
        "ecd,fed->ecf", grad_expert, expout_all, preferred_element_type=jnp.float32
    )
    grad_expout = jnp.einsum(
        "ecf,ecd->fed", active, grad_expert, preferred_element_type=jnp.float32
    )
    unused_gelu, gelu_pull = jax.vjp(gelu_exact, hidden)
    grad_hidden = gelu_pull(grad_active)[0].astype(jnp.bfloat16)
    grad_expin = jnp.einsum(
        "ecd,ecf->def", dispatched, grad_hidden, preferred_element_type=jnp.float32
    )
    grad_dispatch = jnp.einsum(
        "ecf,def->ecd", grad_hidden, expin_all, preferred_element_type=jnp.float32
    )
    grad_dispatch = grad_dispatch.astype(jnp.bfloat16).reshape(slot_count, model_width)
    back_rows = jnp.dot(first_hot, grad_dispatch, preferred_element_type=jnp.float32)
    back_rows = back_rows + jnp.dot(second_hot, grad_dispatch, preferred_element_type=jnp.float32)
    grad_normed_two = grads_out(
        back_rows.reshape(images, length, model_width)
    ) + router_back.reshape(images, quarter, model_width)
    unused_two, norm_two_pull = jax.vjp(layer_norm, middle, gain_two)
    grad_middle_norm, grad_gain_two = norm_two_pull(grad_normed_two)
    grad_middle = grad_output + grad_middle_norm
    grad_branch = (live_own[:, :, None] * grad_middle).astype(jnp.bfloat16)
    grad_branch_all = grads_in(grad_branch).reshape(all_rows, model_width)
    grad_outproj = jnp.einsum(
        "rc,rd->cd", attended, grad_branch_all, preferred_element_type=jnp.float32
    )
    grad_attended = jnp.einsum(
        "rd,cd->rc", grad_branch_all, outproj_all, preferred_element_type=jnp.float32
    )
    grad_attended = grad_attended.astype(jnp.bfloat16).reshape(
        images, length, local_heads, HEAD_DIM
    )
    masked_again = attention_scores(queries, keys_all, key_live, scale_factor)
    probs_again = jnp.exp(masked_again - log_total)
    grad_values = jnp.einsum(
        "ihlm,ilhe->imhe",
        probs_again.astype(jnp.bfloat16),
        grad_attended,
        preferred_element_type=jnp.float32,
    )
    grad_values = grad_values.astype(jnp.bfloat16)
    grad_probs = jnp.einsum(
        "ilhe,imhe->ihlm", grad_attended, values_all, preferred_element_type=jnp.float32
    )
    grad_scores = probs_again * (grad_probs - jnp.sum(probs_again * grad_probs, -1, keepdims=True))
    grad_scores = grad_scores.astype(jnp.bfloat16)
    grad_queries = (
        jnp.einsum("ihlm,imhe->ilhe", grad_scores, keys_all, preferred_element_type=jnp.float32)
        * scale_factor
    ).astype(jnp.bfloat16)
    grad_keys = (
        jnp.einsum("ihlm,ilhe->imhe", grad_scores, queries, preferred_element_type=jnp.float32)
        * scale_factor
    ).astype(jnp.bfloat16)
    grad_project = jnp.stack([grad_queries, grad_keys, grad_values], 2).reshape(
        all_rows, 3, head_cols
    )
    grad_qkv = jnp.einsum(
        "rd,rjc->djc", normed_all, grad_project, preferred_element_type=jnp.float32
    )
    normed_back = jnp.einsum(
        "rjc,djc->rd", grad_project, qkv_all, preferred_element_type=jnp.float32
    )
    grad_normed = grads_out(normed_back.reshape(images, length, model_width))
    unused_one, norm_one_pull = jax.vjp(layer_norm, x_float, gain_one)
    grad_x_norm, grad_gain_one = norm_one_pull(grad_normed)
    grad_input = grad_middle + grad_x_norm
    router_sum, gain_sum = lax.psum(
        (grad_router, jnp.stack([grad_gain_one, grad_gain_two], 1)), "tensor"
    )
    expert_fractions = (
        lax.psum_scatter(gain_sum, "dp", scatter_dimension=0, tiled=True),
        lax.psum_scatter(grad_qkv, "dp", scatter_dimension=0, tiled=True),
        lax.psum_scatter(grad_outproj, "dp", scatter_dimension=1, tiled=True),
        lax.psum_scatter(router_sum, "dp", scatter_dimension=0, tiled=True),
        lax.psum_scatter(grad_expin, "dp", scatter_dimension=0, tiled=True),
        lax.psum_scatter(grad_expout, "dp", scatter_dimension=2, tiled=True),
    )
    return (
        output.astype(jnp.bfloat16),
        grad_input,
        expert_fractions[0],
        expert_fractions[1],
        expert_fractions[2],
        expert_fractions[3],
        expert_fractions[4],
        expert_fractions[5],
    )


MESH = pl.DeviceIdType.MESH
BF = jnp.bfloat16
F32 = jnp.float32
VMEM_BYTES = 63 << 20


class Sizes(NamedTuple):
    n_dp: int
    n_t: int
    images: int
    quarter: int
    rows: int
    irows: int
    width: int
    shard: int
    heads: int
    experts: int
    ff: int
    lanes: int

    @property
    def half(self):
        return self.experts // 2

    @property
    def slots(self):
        return self.half * CAP


def up(value, step):
    return -(-value // step) * step


def norm_parts(values):
    centre = values - jnp.mean(values, -1, keepdims=True)
    scale = lax.rsqrt(jnp.mean(centre * centre, -1, keepdims=True) + epsilon)
    return centre * scale, scale


def norm_back(values, gain, grad):
    unit, scale = norm_parts(values)
    inner = grad * gain
    mean_a = jnp.mean(inner, -1, keepdims=True)
    mean_b = jnp.mean(inner * unit, -1, keepdims=True)
    return scale * (inner - mean_a - unit * mean_b), unit


def dot(a, b):
    return jnp.dot(a, b, preferred_element_type=F32)


def dot_nt(a, b):
    return lax.dot_general(a, b, (((1,), (1,)), ((), ())), preferred_element_type=F32)


def dot_tn(a, b):
    return lax.dot_general(a, b, (((0,), (0,)), ((), ())), preferred_element_type=F32)


class Place:
    def __init__(self, s):
        self.s = s
        self.dp = lax.axis_index("dp")
        self.t = lax.axis_index("tensor")
        self.c = lax.rem(self.dp, 2)
        self.x = lax.rem(self.dp // 2, 2)
        self.y = self.dp // 4
        self.chip = self.dp // 2
        self.chip_x = self.y * 2 + (1 - self.x)
        self.chip_y = (1 - self.y) * 2 + self.x
        self.sib = (self.chip * 2 + (1 - self.c), self.t)
        self.nxy = (((1 - self.y) * 2 + 1 - self.x) * 2 + self.c, self.t)
        self.nx_other = (self.chip_x * 2 + (1 - self.c), self.t)
        self.ny_other = (self.chip_y * 2 + (1 - self.c), self.t)
        self.pair = lax.rem(self.t, 2) * (-2) + self.t + 1
        self.far = lax.rem(self.t + 2, 4)
        self.cross = lax.rem(self.pair + 2, 4)
        self.nx = (self.chip_x * 2 + self.c, self.t)
        self.ny = (self.chip_y * 2 + self.c, self.t)

    def ring_dp(self, k):
        return lax.rem(self.dp + k, self.s.n_dp)

    def ring_t(self, k):
        return lax.rem(self.t + k, self.s.n_t)

    def from_t(self, k):
        return lax.rem(self.t + self.s.n_t - k, self.s.n_t)

    def greet(self):
        barrier = pltpu.get_barrier_semaphore()
        for k in range(1, self.s.n_dp):
            pl.semaphore_signal(barrier, inc=1, device_id=(self.ring_dp(k), self.t), device_id_type=MESH)
        for k in range(1, self.s.n_t):
            pl.semaphore_signal(barrier, inc=1, device_id=(self.dp, self.ring_t(k)), device_id_type=MESH)
        return lambda: pl.semaphore_wait(barrier, self.s.n_dp + self.s.n_t - 2)


class Copies:
    def __init__(self, send, recv, local):
        self.send, self.recv, self.local = send, recv, local
        self.n = 0
        self.m = 0
        self.sent = []

    def make(self, k, src, dst, device):
        return pltpu.make_async_remote_copy(
            src_ref=src,
            dst_ref=dst,
            send_sem=self.send.at[k],
            recv_sem=self.recv.at[k],
            device_id=device,
            device_id_type=MESH,
        )

    def to(self, src, dst, device):
        copy = self.make(self.n, src, dst, device)
        self.n += 1
        copy.start()
        self.sent.append(copy)
        return copy

    def here(self, src, dst):
        copy = pltpu.make_async_copy(src, dst, self.local.at[self.m])
        self.m += 1
        copy.start()
        return copy

    def reserve(self, count):
        self.n += count
        return self.n - count

    def at(self, k, src, dst, device):
        copy = self.make(k, src, dst, device)
        self.sent.append(copy)
        return copy

    def start_at(self, k, src, dst, device):
        self.make(k, src, dst, device).start()

    def sent_now(self, copies):
        for copy in copies:
            copy.wait_send()
        self.sent = [copy for copy in self.sent if not any(copy is done for done in copies)]

    def finish(self):
        for copy in self.sent:
            copy.wait_send()


def pieces_of(rows):
    first = up(rows // 2, 16)
    return [pl.ds(0, first), pl.ds(first, rows - first)]


class Gather:
    def __init__(self, go, here, own, full):
        self.go, self.here, self.full = go, here, full
        self.pieces = pieces_of(here.s.rows)
        mine = full(here.t)
        self.to_far = [go.to(own.at[p], mine.at[p], (here.dp, here.far)) for p in self.pieces]
        self.to_pair = [go.to(own.at[p], mine.at[p], (here.dp, here.pair)) for p in self.pieces]

    def relay(self):
        block = self.full(self.here.far)
        self.passed = []
        for p, copy in zip(self.pieces, self.to_far):
            copy.wait_recv()
            self.passed.append(self.go.to(block.at[p], block.at[p], (self.here.dp, self.here.pair)))

    def sent_on(self):
        self.go.sent_now(self.passed)

    def wait_pair(self):
        for copy in self.to_pair:
            copy.wait_recv()

    def wait_cross(self):
        for copy in self.passed:
            copy.wait_recv()

    def share(self, block):
        return self.go.to(self.full(block), self.full(block), self.here.sib)


class PlaneGather:
    def __init__(self, go, here, full):
        self.go, self.here, self.full = go, here, full
        mine = full.at[here.y, here.x, here.c]
        self.copies = [go.to(mine, mine, device) for device in (here.nx, here.ny, here.nxy)]

    def share(self):
        for copy in self.copies:
            copy.wait_recv()
        mine = self.full.at[:, :, self.here.c]
        self.shared = self.go.to(mine, mine, self.here.sib)

    def wait(self):
        self.shared.wait_recv()


class Reduce:
    def __init__(self, go, here, send, recv):
        self.go, self.here, self.send, self.recv = go, here, send, recv
        self.pieces = pieces_of(here.s.rows)
        self.copies = [[], [], []]

    def put(self, k, p, device):
        self.copies[k].append(self.go.to(self.send.at[k, p], self.recv.at[k, p], (self.here.dp, device)))

    def pair(self, k, value):
        self.send[k] = value.astype(BF)
        for p in self.pieces:
            self.put(k, p, self.here.pair)

    def across(self, part):
        for i, p in enumerate(self.pieces):
            self.copies[0][i].wait_recv()
            self.send[2, p] = (part[p] + self.recv[0, p].astype(F32)).astype(BF)
            self.put(2, p, self.here.far)

    def sent(self):
        self.go.sent_now([copy for copies in self.copies for copy in copies])

    def total(self, part):
        for copy in self.copies[1] + self.copies[2]:
            copy.wait_recv()
        return part + self.recv[1].astype(F32) + self.recv[2].astype(F32)


def head_masks(s):
    lane = lax.broadcasted_iota(jnp.int32, (s.irows, s.heads), 1)
    return [(lane // HEAD_DIM) == h for h in range(s.heads // HEAD_DIM)]


def stack_heads(values, masks):
    zero = jnp.zeros_like(values)
    return jnp.concatenate([jnp.where(mask, values, zero) for mask in masks], 0)


def pick_heads(stacked, masks, irows):
    out = stacked[:irows]
    for h in range(1, len(masks)):
        out = jnp.where(masks[h], stacked[h * irows : (h + 1) * irows], out)
    return out


def block_kernel(s, names, *refs):
    r = SimpleNamespace(**dict(zip(names, refs)))
    here = Place(s)
    dp, t, c, x, y = here.dp, here.t, here.c, here.x, here.y
    all_there = here.greet()
    go = Copies(r.send, r.recv, r.local)
    nt = s.n_t
    length = s.quarter * nt
    used = s.images * s.quarter
    per = s.half // 2
    masks = head_masks(s)

    def to_image_rows(q, block, images):
        for i in range(s.images):
            images[i, pl.ds(q * s.quarter, s.quarter), :] = block[pl.ds(i * s.quarter, s.quarter), : images.shape[2]]

    def to_block_rows(q, images, block):
        for i in range(s.images):
            block[pl.ds(i * s.quarter, s.quarter), : images.shape[2]] = images[i, pl.ds(q * s.quarter, s.quarter), :]

    def clear(images):
        images[:, pl.ds(length, s.irows - length), :] = jnp.zeros((s.images, s.irows - length, images.shape[2]), F32)

    clear(r.img)
    clear(r.oimg)
    line = r.comb.at[3]

    rows_at = [pl.ds(i * s.quarter, s.quarter) for i in range(s.images)]

    def rows_of(images, out):
        r.tmp[pl.ds(used, s.rows - used), :] = jnp.zeros((s.rows - used, s.width), F32)
        for i, at in enumerate(rows_at):
            r.tmp[at, :] = images[i].astype(F32)
        out[...] = r.tmp[...].astype(BF)

    fetch = go.here(r.win, r.gwi)
    keep_wo = go.here(r.wo, r.wo_z.at[t])
    pack_own = r.pack.at[y, x, c]
    cols = 3 * s.shard
    for k in range(3):
        pack_own[pl.ds(k * s.shard, s.shard), :] = r.wq[k]
    pack_own[pl.ds(cols, s.experts), : s.shard] = r.wr[...]
    gains = jnp.concatenate([r.gains[...].astype(F32), jnp.zeros((14, s.shard), F32)], 0)
    pack_own[pl.ds(cols + s.experts, 16), : s.shard] = gains.astype(BF)
    rows_of(r.x_in, r.x)
    all_there()
    wo_copies = [go.to(r.wo, r.wo_z.at[t], (dp, here.ring_t(k))) for k in range(1, nt)]
    packs = PlaneGather(go, here, r.pack)
    x_blocks = Gather(go, here, r.x, lambda block: r.n1.at[block])
    rows_of(r.dz_in, r.dz)

    def spread(shard, full):
        to = full.at[:, y, x, pl.ds(pl.multiple_of(c * s.shard, s.shard), s.shard)]
        half, rest = shard.at[c], shard.at[1 - c]
        from_x = [go.to(half, to, here.nx), go.to(rest, to, here.nx_other)]
        from_y = [go.to(half, to, here.ny), go.to(rest, to, here.ny_other)]
        return from_x, from_y, go.to(rest, to, here.sib), go.here(half, to)

    fetch.wait()
    shards = r.xin.at[:, :, pl.ds(0, s.shard)]
    shards[...] = jnp.swapaxes(r.gwi[...], 0, 1).reshape(2, s.half, s.shard, s.ff)
    in_x, in_y, in_sib, keep_in = spread(shards, r.win_all)

    chosen = jnp.where(r.slots[...] >= 0, r.ids[...] * CAP + r.slots[...], -1)
    by_block = []
    for q in range(nt):
        parts = [chosen[i, :, q * s.quarter : (q + 1) * s.quarter] for i in range(s.images)]
        by_block.append(jnp.concatenate(parts + [jnp.full((2, s.rows - used), -1, jnp.int32)], 1))
        wide = jnp.concatenate([by_block[q], jnp.zeros((2, s.lanes - s.rows), jnp.int32)], 1)
        wide = jnp.concatenate([wide, jnp.zeros((6, s.lanes), jnp.int32)], 0)
        r.tcol[q] = wide.T[: s.rows, :2]
    tgt_own = r.tgt_all.at[c]
    tgt_own[:2, :] = jnp.concatenate(by_block, 1)
    tgt_copy = go.to(tgt_own, tgt_own, here.sib)

    def dz_block(block):
        return r.ge.at[c, pl.ds(pl.multiple_of(block * s.rows, 16), s.rows)]

    dz_sib = go.to(r.dz, dz_block(t), here.sib)
    keep_dz = go.here(r.dz, dz_block(t))

    keep_wo.wait()
    for copy in wo_copies:
        copy.wait_recv()
    r.wo_all[y, x, c] = r.wo_z[...]
    wos = PlaneGather(go, here, r.wo_all)
    packs.share()
    packs.wait()
    small = jnp.concatenate(
        [r.pack[k // 4, k // 2 % 2, k % 2, cols:, : s.shard].astype(F32) for k in range(s.n_dp)], 1
    )
    r.small[...] = small
    gain_one = small[s.experts : s.experts + 1]
    gain_two = small[s.experts + 1 : s.experts + 2]

    def qkv_weights(k):
        return r.pack[:, :, :, k * s.shard : (k + 1) * s.shard].reshape(s.width, s.heads)

    def project(slot, values):
        unit, _ = norm_parts(values.astype(F32))
        normed = (unit * gain_one).astype(BF)
        r.n1[slot] = normed
        weights = jnp.concatenate([qkv_weights(k) for k in range(3)], 1)
        r.comb[slot, :, : 3 * s.heads] = dot(normed, weights)

    project(t, r.x[...])
    x_blocks.relay()
    out_x, out_y, out_sib, keep_out = spread(r.wout, r.wout_all)
    x_blocks.wait_pair()
    project(here.pair, r.n1[here.pair])
    x_blocks.sent_on()
    project(here.far, r.n1[here.far])
    x_blocks.wait_cross()
    project(here.cross, r.n1[here.cross])
    dz_blocks = Gather(go, here, r.dz, dz_block)

    for q in range(nt):
        to_image_rows(q, r.comb.at[q], r.img)

    def attend(i, carry):
        block = r.img[i].astype(BF)
        r.qkv[i] = block
        queries = stack_heads(block[:, : s.heads], masks)
        scores = dot_nt(queries, block[:, s.heads : 2 * s.heads]) * (1.0 / math.sqrt(HEAD_DIM))
        key = lax.broadcasted_iota(jnp.int32, scores.shape, 1)
        scores = jnp.where(key < TOK_IMG, scores, negative_fill)
        expd = jnp.exp(scores - jnp.max(scores, -1, keepdims=True))
        probs = (expd / jnp.sum(expd, -1, keepdims=True)).astype(BF)
        r.p[i] = probs
        r.oimg[i] = pick_heads(dot(probs, block[:, 2 * s.heads :]), masks, s.irows)
        return carry

    lax.fori_loop(0, s.images, attend, 0, unroll=2)
    line[pl.ds(used, s.rows - used), :] = jnp.zeros((s.rows - used, s.width), F32)
    for q in range(nt):
        to_block_rows(q, r.oimg, line)
        r.o_send[q] = line[:, : s.heads].astype(BF)
    o_copies = [go.to(r.o_send.at[here.ring_t(k)], r.o.at[t], (dp, here.ring_t(k))) for k in range(1, nt)]
    r.o[t] = r.o_send[t]
    few = 2

    def pass_on(full, by_x, by_y):
        for copy in by_x + by_y:
            copy.wait_recv()
        copies = []
        for e in range(0, per, few):
            from_x = full.at[pl.ds(e, few), y, 1 - x]
            from_y = full.at[pl.ds(per + e, few), 1 - y, x]
            copies.append([go.to(from_x, from_x, here.ny), go.to(from_y, from_y, here.nx)])
        return copies

    in_on = pass_on(r.win_all, in_x, in_y)
    wos.share()
    dz_blocks.relay()
    on_dz = [dz_blocks.share(here.far)]
    tgt_copy.wait_recv()
    tokens = nt * s.rows
    half_rows = tokens // 2
    for q in range(2):
        first_id = (c * s.half + lax.broadcasted_iota(jnp.int32, (s.half, tokens), 0)) * CAP
        found = jnp.full((s.half, tokens), -1, jnp.int32)
        for k in range(2):
            slot = r.tgt_all[q, k : k + 1, :] - first_id
            found = jnp.where((slot >= 0) & (slot < CAP), slot, found)
        r.slot[q] = found.astype(F32)
        for h in range(2):
            r.sloth[h, q] = r.slot[q][:, h * half_rows : (h + 1) * half_rows]
    wos.wait()
    for copy in o_copies:
        copy.wait_recv()
    branch = jnp.zeros((s.rows, s.width), F32)
    for q in range(nt):
        branch = branch + dot_nt(r.o[q], r.wo_all[:, :, :, q].reshape(s.width, s.heads))
    row = lax.broadcasted_iota(jnp.int32, (s.rows, 1), 0)
    place = t * s.quarter + row
    for _ in range(1, s.images):
        place = jnp.where(place >= t * s.quarter + s.quarter, place - s.quarter, place)
    live = jnp.where((row < r.alive[0] * s.quarter) & (place < TOK_IMG) & (row < used), 1.0, 0.0)
    r.live[...] = live
    middle = r.x[...].astype(F32) + live * branch
    r.y[...] = middle
    unit, _ = norm_parts(middle)
    normed_two = (unit * gain_two).astype(BF)
    n2_own = r.n2_all.at[c, t]
    n2_own[...] = normed_two
    n2_sib = go.to(n2_own, n2_own, here.sib)
    n2_blocks = Gather(go, here, n2_own, lambda block: r.n2_all.at[c, block])
    logits = dot_nt(small[: s.experts].astype(BF), normed_two)
    expd = jnp.exp(logits - jnp.max(logits, 0, keepdims=True))
    r.prob[...] = jnp.zeros((s.experts, s.lanes), F32)
    r.prob[:, : s.rows] = expd / jnp.sum(expd, 0, keepdims=True)
    pr_own = r.prob_all.at[c, t]
    pr_own[...] = r.prob[...].astype(BF)
    pr_sib = go.to(pr_own, pr_own, here.sib)
    pr_copies = [go.to(pr_own, pr_own, (dp, here.ring_t(k))) for k in range(1, nt)]

    dz_blocks.wait_pair()
    dz_blocks.wait_cross()
    on_dz += [dz_blocks.share(here.pair), dz_blocks.share(here.cross)]
    keep_dz.wait()
    for copy in [dz_sib] + on_dz:
        copy.wait_recv()

    slot_ids = lax.broadcasted_iota(jnp.int32, (CAP, tokens), 0).astype(F32)

    def hot_rows(h, q, j):
        for i in range(few):
            hits = r.sloth[h, q, pl.ds(few * j + i, 1), :] == slot_ids[:, :half_rows]
            r.hot[i] = jnp.where(hits, 1.0, 0.0).astype(BF)
        return r.hot[...].reshape(few * CAP, half_rows)

    def dispatch_z(j, carry):
        for q in range(2):
            found = jnp.zeros((few * CAP, s.width), F32)
            for h in range(2):
                found = found + dot(hot_rows(h, q, j), r.ge[q, pl.ds(h * half_rows, half_rows)])
            r.zin[q, pl.ds(few * j, few)] = found.astype(BF).reshape(few, CAP, s.width)
        return carry

    lax.fori_loop(0, s.half // few, dispatch_z, 0)
    n2_blocks.relay()
    out_on = pass_on(r.wout_all, out_x, out_y)
    on_n2 = [n2_blocks.share(here.far)]
    n2_blocks.wait_pair()
    on_n2.append(n2_blocks.share(here.pair))
    for k, copy in enumerate(pr_copies, 1):
        copy.wait_recv()
        slot = r.prob_all.at[c, here.from_t(k)]
        on_n2.append(go.to(slot, slot, here.sib))

    def dispatch_x(h, first, only=None):
        def step(j, carry):
            for q in range(2):
                rows = r.n2_all[q, pl.ds(2 * h, 2)].reshape(half_rows, s.width)
                found = dot(hot_rows(h, q, j), rows)
                found = found.reshape(few, CAP, s.width)
                out = r.xin.at[q, pl.ds(few * j, few)]
                out[...] = (found if first else found + out[...].astype(F32)).astype(BF)
            return carry

        if only is None:
            lax.fori_loop(0, s.half // few, step, 0)
        else:
            step(only, 0)

    keep_in.wait()
    go.sent_now([*in_x, *in_y, in_sib])
    n2_sib.wait_recv()
    on_n2[1].wait_recv()
    dispatch_x(t // 2, True)
    n2_blocks.wait_cross()
    on_n2.append(n2_blocks.share(here.cross))
    keep_out.wait()
    for copy in [pr_sib, in_sib, out_sib, *in_on[0], *in_on[1], on_n2[0]] + on_n2[2:]:
        copy.wait_recv()
    for q in range(2):
        probs = jnp.concatenate([r.prob_all[q, k].astype(F32)[:, : s.rows] for k in range(nt)], 1)
        r.pr[q] = jnp.where(c == 0, probs[: s.half], probs[s.half :])
    for copy in out_on[0]:
        copy.wait_recv()
    go.sent_now([*in_on[0], *in_on[1], *out_on[0], dz_sib, *dz_blocks.passed, *on_dz])
    k_in, k_out, k_dx, k_ge = (go.reserve(s.half) for _ in range(4))

    def grad_in_copy(e):
        return r.win_all.at[e, :, 1 - x], r.ra.at[e], here.nx

    def grad_out_copy(e):
        return r.wout_all.at[e, 1 - y], r.rb.at[e], here.ny

    def dx_copy(e):
        return r.xin.at[1 - c, e], r.dxv.at[e], here.sib

    def slots_of(e):
        return pl.ds(pl.multiple_of(e * CAP, CAP), CAP)

    def ge_copy(e):
        return r.ge.at[1 - c, slots_of(e)], r.gev.at[slots_of(e)], here.sib

    def experts_at(first):
        es = [first + i for i in range(few)]
        x_in = [r.xin[:, e].reshape(2 * CAP, s.width) for e in es]
        w_in = [r.win_all[e].reshape(s.width, s.ff) for e in es]
        w_out = [r.wout_all[e].reshape(s.width, s.ff) for e in es]
        hidden = [dot(a, b) for a, b in zip(x_in, w_in)]
        active, slope = [], []
        for value in hidden:
            bell = jnp.exp(-0.5 * value * value)
            u = 1.0 / (1.0 + (0.3275911 / math.sqrt(2.0)) * jnp.abs(value))
            poly = u * (0.254829592 + u * (-0.284496736 + u * (1.421413741 + u * (-1.453152027 + u * 1.061405429))))
            tail = 0.5 * poly * bell
            phi = jnp.where(value >= 0, 1.0 - tail, tail)
            active.append((value * phi).astype(BF))
            slope.append(phi + value * bell * (1.0 / math.sqrt(2.0 * math.pi)))
        gates, wides = [], []
        for e in es:
            for q in range(2):
                hits = r.slot[q, pl.ds(e, 1), :] == slot_ids
                gate = jnp.sum(jnp.where(hits, r.pr[q, pl.ds(e, 1), :], 0.0), 1, keepdims=True)
                gates.append(gate)
                wides.append(r.zin[q, e].astype(F32))
                r.zin[q, e] = (gate * wides[-1]).astype(BF)
        grad = [r.zin[:, e].reshape(2 * CAP, s.width) for e in es]
        dactive = [dot(a, b) for a, b in zip(grad, w_out)]
        out = [dot_nt(a, b).astype(BF).astype(F32) for a, b in zip(active, w_out)]
        dhidden = [(a * b).astype(BF) for a, b in zip(dactive, slope)]
        grad_out = [dot_tn(a, b).astype(BF) for a, b in zip(grad, active)]
        for i, e in enumerate(es):
            for q in range(2):
                part = out[i][q * CAP : (q + 1) * CAP]
                dgate = jnp.sum(wides[2 * i + q] * part, 1, keepdims=True)
                hits = r.slot[q, pl.ds(e, 1), :] == slot_ids
                r.dpr[q, pl.ds(e, 1), :] = jnp.sum(jnp.where(hits, dgate, 0.0), 0, keepdims=True)
                r.ge[q, slots_of(e)] = (gates[2 * i + q] * part).astype(BF)
        dx = [dot_nt(a, b).astype(BF) for a, b in zip(dhidden, w_in)]
        grad_in = [dot_tn(a, b).astype(BF) for a, b in zip(x_in, dhidden)]
        for i, e in enumerate(es):
            r.wout_all[e] = grad_out[i].reshape(r.wout_all.shape[1:])
            r.xin[:, e] = dx[i].reshape(2, CAP, s.width)
            r.win_all[e] = grad_in[i].reshape(r.win_all.shape[1:])

    def expert_few(k, carry):
        j = lax.rem(k, 2) * (per // few) + k // 2
        dispatch_x(1 - t // 2, False, j)
        experts_at(few * j)
        for i in range(few):
            e = few * j + i
            for k, copy in ((k_out, grad_out_copy), (k_in, grad_in_copy), (k_dx, dx_copy), (k_ge, ge_copy)):
                go.start_at(k + e, *copy(e))
        return carry

    lax.fori_loop(0, 2, expert_few, 0)
    for copies in out_on[1:]:
        for copy in copies:
            copy.wait_recv()
        go.sent_now(copies)
    lax.fori_loop(2, s.half // few, expert_few, 0)
    ge_copies = [go.at(k_ge + e, *ge_copy(e)) for e in range(s.half)]
    dx_copies = [go.at(k_dx + e, *dx_copy(e)) for e in range(s.half)]
    in_copies = [go.at(k_in + e, *grad_in_copy(e)) for e in range(s.half)]
    out_copies = [go.at(k_out + e, *grad_out_copy(e)) for e in range(s.half)]

    zero_rows = jnp.zeros((s.rows, s.width), F32)
    span = 512

    def combine(values, half, q, total):
        first = r.tcol[q, :, 0:1] - half * s.slots
        second = r.tcol[q, :, 1:2] - half * s.slots
        lane = lax.broadcasted_iota(jnp.int32, (s.rows, span), 1)
        for j in range(s.slots // span):
            hot = jnp.where((first - j * span == lane) | (second - j * span == lane), 1.0, 0.0).astype(BF)
            total = total + dot(hot, values[pl.ds(j * span, span)])
        return total

    dx_own, dxv = r.xin.at[c].reshape(s.slots, s.width), r.dxv.reshape(s.slots, s.width)
    r.comb[0] = combine(dx_own, c, here.cross, zero_rows)
    for copy in dx_copies:
        copy.wait_recv()
    dn2_sum = Reduce(go, here, r.rs_send, r.rs_recv)
    dn2_sum.pair(0, combine(dxv, 1 - c, here.cross, r.comb[0]))
    dn2_sum.pair(1, combine(dxv, 1 - c, here.pair, combine(dx_own, c, here.pair, zero_rows)))
    r.dprs[...] = jnp.zeros(r.dprs.shape, F32)
    for q in range(2):
        for k in range(nt):
            r.dprs[q, k, :, : s.rows] = r.dpr[q][:, k * s.rows : (k + 1) * s.rows]
    dpr_sib = go.to(r.dprs.at[1 - c], r.dprf.at[:, c], here.sib)
    r.dprf[:, c] = r.dprs[c]
    dpr_sib.wait_recv()
    r.dprb[...] = r.dprf[...].reshape(r.dprb.shape).astype(BF)
    dpr_copies = [go.to(r.dprb.at[here.ring_t(k)], r.dprz.at[k - 1], (dp, here.ring_t(k))) for k in range(1, nt)]
    dn2_sum.across(combine(dxv, 1 - c, here.far, combine(dx_own, c, here.far, zero_rows)))
    r.comb[0] = combine(dxv, 1 - c, t, combine(dx_own, c, t, zero_rows))
    go.sent_now(dx_copies)

    for copy in ge_copies:
        copy.wait_recv()
    ge_own = r.ge.at[c]
    m_sum = Reduce(go, here, r.m_send, r.m_recv)

    def forward_sum(q):
        return combine(r.gev, 1 - c, q, combine(ge_own, c, q, zero_rows))

    r.m_send[0] = forward_sum(here.cross).astype(BF)
    r.m_send[1] = forward_sum(here.pair).astype(BF)
    r.comb[2] = forward_sum(here.far)
    r.tmp[...] = forward_sum(t) + r.y[...]

    dprobs = r.dprf[t].reshape(s.experts, s.lanes)
    for k, copy in enumerate(dpr_copies):
        copy.wait_recv()
        dprobs = dprobs + r.dprz[k].astype(F32)
    probs = r.prob[...]
    dlogits = (probs * (dprobs - jnp.sum(probs * dprobs, 0, keepdims=True))).astype(BF)[:, : s.rows]
    small = r.small[...]
    gain_one = small[s.experts : s.experts + 1]
    gain_two = small[s.experts + 1 : s.experts + 2]
    grad_router = dot_tn(r.n2_all[c, t], dlogits.T).T
    dn2 = r.comb[0] + dot_tn(dlogits, small[: s.experts].astype(BF))
    dn2 = dn2_sum.total(dn2)
    middle = r.y[...]
    dy_ln, unit = norm_back(middle, gain_two, dn2)
    dgain_two = jnp.sum(dn2 * unit, 0, keepdims=True)
    dy = r.dz[...].astype(F32) + dy_ln
    r.comb[0] = dy
    da = (r.live[...] * dy).astype(BF)
    go.sent_now(o_copies)
    for q in range(nt):
        r.o_send[q] = dot(da, r.wo_all[:, :, :, q].reshape(s.width, s.heads)).astype(BF)
    do_copies = [go.to(r.o_send.at[here.ring_t(k)], r.do.at[t], (dp, here.ring_t(k))) for k in range(1, nt)]
    for k in range(2):
        for p in m_sum.pieces:
            m_sum.put(k, p, here.pair)
    r.do[t] = r.o_send[t]
    for q in range(nt):
        part = dot_tn(da, r.o[q]).reshape(*r.grads.shape[:3], s.shard, s.heads)
        r.grads[:, :, :, :, (3 + q) * s.heads : (4 + q) * s.heads] = part.astype(BF)

    fa_copies, fb_copies = [], []

    def pump(j):
        first, second = in_copies[j * per : (j + 1) * per], out_copies[j * per : (j + 1) * per]
        for copy in first:
            copy.wait_recv()

        def step_a(i, carry):
            e = j * per + i
            r.win_all[e, 1 - y, x] = (r.win_all[e, 1 - y, x].astype(F32) + r.ra[e, 1 - y].astype(F32)).astype(BF)
            return carry

        lax.fori_loop(0, per, step_a, 0)
        piece = pl.ds(j * per, per)
        fa_copies.append(go.to(r.win_all.at[piece, 1 - y, x], r.fa.at[piece], here.ny))
        for copy in second:
            copy.wait_recv()

        def step_b(i, carry):
            e = j * per + i
            r.wout_all[e, y, 1 - x] = (r.wout_all[e, y, 1 - x].astype(F32) + r.rb[e, 1 - x].astype(F32)).astype(BF)
            return carry

        lax.fori_loop(0, per, step_b, 0)
        fb_copies.append(go.to(r.wout_all.at[piece, y, 1 - x], r.fb.at[piece], here.nx))

    pump(0)
    for copy in do_copies:
        copy.wait_recv()
    clear(r.oimg)
    for q in range(nt):
        line[:, : s.heads] = r.do[q].astype(F32)
        to_image_rows(q, line, r.oimg)

    def attend_back(i, carry):
        block = r.qkv[i]
        queries = stack_heads(block[:, : s.heads], masks)
        grads = stack_heads(r.oimg[i].astype(BF), masks)
        probs = r.p[i]
        dvalues = dot_tn(probs, grads)
        dprob = dot_nt(grads, block[:, 2 * s.heads :])
        wide = probs.astype(F32)
        both = wide * dprob
        dscore = (both - wide * jnp.sum(both, -1, keepdims=True)).astype(BF)
        dqueries = pick_heads(dot(dscore, block[:, s.heads : 2 * s.heads]), masks, s.irows)
        dkeys = dot_tn(dscore, queries)
        r.img[i, :, : s.heads] = dqueries * (1.0 / math.sqrt(HEAD_DIM))
        r.img[i, :, s.heads : 2 * s.heads] = dkeys * (1.0 / math.sqrt(HEAD_DIM))
        r.img[i, :, 2 * s.heads :] = dvalues
        return carry

    lax.fori_loop(0, s.images, attend_back, 0, unroll=2)
    line[pl.ds(used, s.rows - used), :] = jnp.zeros((s.rows - used, s.width), F32)
    for q in range(nt):
        to_block_rows(q, r.img, line)
        r.dqkv[q] = line[:, : 3 * s.heads].astype(BF)
    w_qkv = jnp.concatenate([qkv_weights(k) for k in range(3)], 1)
    dn2_sum.sent()
    dn1_sum = Reduce(go, here, r.rs_send, r.rs_recv)
    dgain_one = jnp.zeros((1, s.width), F32)
    for k, q in enumerate((here.cross, here.pair, here.far, t)):
        part = dot_nt(r.dqkv[q], w_qkv)
        dgain_one = dgain_one + jnp.sum(part * r.n1[q].astype(F32), 0, keepdims=True)
        if k < 2:
            dn1_sum.pair(k, part)
        else:
            r.comb[2 * k - 3] = part
    dgain_one = dgain_one / gain_one

    m_sum.across(r.comb[2])
    pump(1)

    grad_qkv = jnp.zeros((s.width, 3 * s.heads), F32)
    for q in range(nt):
        grad_qkv = grad_qkv + dot_tn(r.n1[q], r.dqkv[q])
    grads = r.grads
    grads[:, :, :, :, : 3 * s.heads] = grad_qkv.astype(BF).reshape(*grads.shape[:3], s.shard, 3 * s.heads)
    r.sm_send[0] = jnp.concatenate(
        [grad_router, dgain_one, dgain_two, jnp.zeros((r.sm_send.shape[1] - s.experts - 2, s.width), F32)], 0
    )
    step = [go.to(grads.at[:, :, 1 - c], r.gs_recv, here.sib), go.to(r.sm_send.at[0], r.sm_recv.at[0], here.sib)]

    def add_small(k):
        r.sm_send[k + 1] = r.sm_send[k] + r.sm_recv[k]

    for copy in step:
        copy.wait_recv()

    def add_in(mine, came):
        return (mine.astype(F32) + came.astype(F32)).astype(BF)

    grads[:, :, c] = add_in(grads[:, :, c], r.gs_recv[...])
    add_small(0)
    step = [go.to(grads.at[:, 1 - x, c], r.gx_recv, here.nx), go.to(r.sm_send.at[1], r.sm_recv.at[1], here.nx)]
    dn1_sum.across(r.comb[1])
    for copy in step:
        copy.wait_recv()
    grads[:, x, c] = add_in(grads[:, x, c], r.gx_recv[...])
    add_small(1)
    step = [go.to(grads.at[1 - y, x, c], r.gy_recv, here.ny), go.to(r.sm_send.at[2], r.sm_recv.at[2], here.ny)]
    for copy in step:
        copy.wait_recv()
    add_small(2)
    summed = grads[y, x, c].astype(F32) + r.gy_recv[...].astype(F32)
    for k in range(3):
        r.gq[k] = summed[:, k * s.heads : (k + 1) * s.heads]
    for q in range(nt):
        r.gz_send[q] = summed[:, (3 + q) * s.heads : (4 + q) * s.heads].astype(BF)
    gz_copies = [go.to(r.gz_send.at[here.ring_t(k)], r.gz_recv.at[k - 1], (dp, here.ring_t(k))) for k in range(1, nt)]
    sums = r.sm_send[3]
    pieces = [jnp.where(dp == k, sums[:, k * s.shard : (k + 1) * s.shard], 0.0) for k in range(s.n_dp)]
    r.sz_send[...] = jnp.zeros(r.sz_send.shape, F32)
    r.sz_send[:, : s.shard] = sum(pieces[1:], pieces[0])
    sm_copies = [go.to(r.sz_send, r.sz_recv.at[k - 1], (dp, here.ring_t(k))) for k in range(1, nt)]
    r.tmp[...] = m_sum.total(r.tmp[...])
    for i, at in enumerate(rows_at):
        r.out[i] = r.tmp[at, :].astype(BF)

    mine = pl.ds(pl.multiple_of(c * s.shard, s.shard), s.shard)
    other = pl.ds(pl.multiple_of((1 - c) * s.shard, s.shard), s.shard)
    fin_copies, kept = [], []
    parts = ((r.win_all, r.ra, y, r.fa, fa_copies, shards), (r.wout_all, r.rb, x, r.fb, fb_copies, r.gwo))
    for own, first, place, second, copies, gw in parts:
        for j in range(2):
            copies[j].wait_recv()

            def last(i, carry, own=own, first=first, place=place, second=second, gw=gw, j=j):
                e = j * per + i

                def total(rows):
                    return (
                        own[e, y, x, rows, :].astype(F32)
                        + first[e, place, rows, :].astype(F32)
                        + second[e, rows, :].astype(F32)
                    )

                own[e, y, x, other, :] = total(other).astype(BF)
                own[e, y, x, mine, :] = total(mine).astype(BF)
                return carry

            lax.fori_loop(0, per, last, 0)
            piece = pl.ds(j * per, per)
            fin_copies.append(go.to(own.at[piece, y, x, other], gw.at[c, piece], here.sib))
            kept.append(go.here(own.at[piece, y, x, mine], gw.at[c, piece]))
    for copy in fin_copies[:2]:
        copy.wait_recv()
    for copy in kept[:2]:
        copy.wait()
    r.gwi[...] = jnp.swapaxes(shards[...].reshape(s.experts, s.shard, s.ff), 0, 1)
    dn1 = dn1_sum.total(r.comb[3])
    dx_ln, _ = norm_back(r.x[...].astype(F32), gain_one, dn1)
    r.tmp[...] = r.comb[0] + dx_ln
    for i, at in enumerate(rows_at):
        r.gx[i] = r.tmp[at, :]
    total = r.gz_send[t].astype(F32)
    for k, copy in enumerate(gz_copies):
        copy.wait_recv()
        total = total + r.gz_recv[k].astype(F32)
    r.go[...] = total
    total = r.sz_send[...]
    for k, copy in enumerate(sm_copies):
        copy.wait_recv()
        total = total + r.sz_recv[k]
    r.gr[...] = total[: s.experts, : s.shard]
    r.gg[...] = total[s.experts : s.experts + 2, : s.shard]

    for copy in fin_copies[2:]:
        copy.wait_recv()
    for copy in kept[2:]:
        copy.wait()
    go.finish()


VSPEC = pl.BlockSpec(memory_space=pltpu.VMEM)
ASPEC = pl.BlockSpec(memory_space=pl.ANY)


def shape(dims, kind):
    return jax.ShapeDtypeStruct(dims, kind)


def linked_body(
    block_input,
    gains,
    w_qkv,
    w_o,
    w_router,
    w_in,
    w_out,
    pictures_alive_per_shard,
    expert_ids,
    slot_index,
    cotangent,
):
    images, quarter, width = block_input.shape
    n_dp, n_t = lax.axis_size("dp"), lax.axis_size("tensor")
    shard, experts, ff = w_in.shape
    heads = w_qkv.shape[2]
    length = quarter * n_t
    used = images * quarter
    rows = up(used, 16)
    s = Sizes(n_dp, n_t, images, quarter, rows, up(length, 16), width, shard, heads, experts, ff, up(rows, 128))
    wout_t = w_out.transpose(1, 2, 0).reshape(2, s.half, shard, ff)
    two_y, two_x = n_dp // 4, 2
    gsm_rows = up(experts + 2, 8)
    tokens = n_t * rows
    inputs = dict(
        x_in=block_input,
        dz_in=cotangent,
        wq=w_qkv.transpose(1, 0, 2),
        wo=w_o.T,
        wr=w_router.T,
        gains=gains.T,
        ids=expert_ids.transpose(0, 2, 1),
        slots=slot_index.transpose(0, 2, 1),
        alive=pictures_alive_per_shard,
        win=w_in,
        wout=wout_t,
    )
    in_specs = {"win": ASPEC, "wout": ASPEC, "alive": pl.BlockSpec(memory_space=pltpu.SMEM)}
    outputs = dict(
        out=shape((images, quarter, width), BF),
        gx=shape((images, quarter, width), F32),
        gq=shape((3, shard, heads), F32),
        go=shape((shard, heads), F32),
        gr=shape((experts, shard), F32),
        gg=shape((2, shard), F32),
        gwi=shape((shard, experts, ff), BF),
        gwo=shape((2, s.half, shard, ff), BF),
    )
    wide = (two_y, two_x, 2 * shard, ff)
    per = s.half // 2
    scratch = dict(
        win_all=((s.half, *wide), BF),
        wout_all=((s.half, *wide), BF),
        n2_all=((2, n_t, rows, width), BF),
        prob_all=((2, n_t, experts, s.lanes), BF),
        tgt_all=((2, 8, tokens), jnp.int32),
        tcol=((n_t, rows, 2), jnp.int32),
        y=((rows, width), F32),
        prob=((experts, s.lanes), F32),
        qkv=((images, s.irows, 3 * heads), BF),
        p=((images, heads // HEAD_DIM * s.irows, s.irows), BF),
        n1=((n_t, rows, width), BF),
        o=((n_t, rows, heads), BF),
        do=((n_t, rows, heads), BF),
        x=((rows, width), BF),
        dz=((rows, width), BF),
        tmp=((rows, width), F32),
        live=((rows, 1), F32),
        pack=((two_y, two_x, 2, 3 * shard + up(experts + 2, 16), heads), BF),
        wo_all=((two_y, two_x, 2, n_t, shard, heads), BF),
        wo_z=((n_t, shard, heads), BF),
        small=((up(experts + 2, 16), width), F32),
        img=((images, s.irows, 3 * heads), F32),
        oimg=((images, s.irows, heads), F32),
        o_send=((n_t, rows, heads), BF),
        dqkv=((n_t, rows, 3 * heads), BF),
        pr=((2, s.half, tokens), F32),
        dpr=((2, s.half, tokens), F32),
        dprs=((2, n_t, s.half, s.lanes), F32),
        dprf=((n_t, 2, s.half, s.lanes), F32),
        dprb=((n_t, experts, s.lanes), BF),
        dprz=((n_t - 1, experts, s.lanes), BF),
        hot=((2, CAP, tokens // 2), BF),
        xin=((2, s.half, CAP, width), BF),
        slot=((2, s.half, tokens), F32),
        sloth=((2, 2, s.half, tokens // 2), F32),
        zin=((2, s.half, CAP, width), BF),
        ge=((2, s.slots, width), BF),
        dxv=((s.half, CAP, width), BF),
        gev=((s.slots, width), BF),
        comb=((n_t, rows, width), F32),
        rs_send=((n_t - 1, rows, width), BF),
        rs_recv=((n_t - 1, rows, width), BF),
        m_send=((n_t - 1, rows, width), BF),
        m_recv=((n_t - 1, rows, width), BF),
        grads=((two_y, two_x, 2, shard, 7 * heads), BF),
        gs_recv=((two_y, two_x, shard, 7 * heads), BF),
        gx_recv=((two_y, shard, 7 * heads), BF),
        gy_recv=((shard, 7 * heads), BF),
        gz_send=((n_t, shard, heads), BF),
        gz_recv=((n_t - 1, shard, heads), BF),
        sm_send=((4, gsm_rows, width), F32),
        sm_recv=((3, gsm_rows, width), F32),
        sz_send=((gsm_rows, up(shard, 128)), F32),
        sz_recv=((n_t - 1, gsm_rows, up(shard, 128)), F32),
        ra=((s.half, two_y, 2 * shard, ff), BF),
        rb=((s.half, two_x, 2 * shard, ff), BF),
        fa=((s.half, 2 * shard, ff), BF),
        fb=((s.half, 2 * shard, ff), BF),
    )
    links = 160
    names = [*inputs, *outputs, *scratch, "send", "recv", "local"]
    out, gx, gq, grad_o, gr, gg, gwi, gwo = pl.pallas_call(
        lambda *refs: block_kernel(s, names, *refs),
        out_shape=tuple(outputs.values()),
        in_specs=[in_specs.get(name, VSPEC) for name in inputs],
        out_specs=[ASPEC if name == "gwo" else VSPEC for name in outputs],
        scratch_shapes=[pltpu.VMEM(dims, kind) for dims, kind in scratch.values()]
        + [pltpu.SemaphoreType.DMA((links,)), pltpu.SemaphoreType.DMA((links,)), pltpu.SemaphoreType.DMA((10,))],
        compiler_params=pltpu.CompilerParams(collective_id=1, has_side_effects=True, vmem_limit_bytes=VMEM_BYTES),
        name="block",
    )(*inputs.values())

    return (
        out,
        gx,
        gg.T,
        gq.transpose(1, 0, 2),
        grad_o.T,
        gr.T,
        gwi.astype(F32),
        gwo.reshape(experts, shard, ff).transpose(2, 0, 1).astype(F32),
    )


def solution(mesh):
    placed = (
        P("dp", "tensor", None),
        P("dp", None),
        P("dp", None, "tensor"),
        P("tensor", "dp"),
        P("dp", None),
        P("dp", None, "tensor"),
        P("tensor", None, "dp"),
        P("dp"),
        P("dp", None, None),
        P("dp", None, None),
        P("dp", "tensor", None),
    )
    linked = mesh.shape["dp"] == 8 and mesh.shape["tensor"] == 4
    return jax.shard_map(
        linked_body if linked else body,
        mesh=mesh,
        in_specs=placed,
        out_specs=(
            P("dp", "tensor", None),
            P("dp", "tensor", None),
            P("dp", None),
            P("dp", None, "tensor"),
            P("tensor", "dp"),
            P("dp", None),
            P("dp", None, "tensor"),
            P("tensor", None, "dp"),
        ),
        check_vma=False,
    )
```
